32 devices in a mesh: seq: 8 (over z, y), head: 4 (over x, core).
Axes of the slice: x: 2, y: 2, z: 4, core: 2. Of those that a mesh axis runs over, the one named last changes fastest.
Arguments:
- inputs: bfloat16 [8192, 1024], P('seq', 'head'), may hold values from -6 to 6
- cotangent: bfloat16 [8192, 1024], P('seq', 'head'), may hold values from -6 to 6
- norm_gain: bfloat16 [1024], P('head'), may hold values from 0.5 to 1.5
- qkv_weight: bfloat16 [3, 1024, 1024], P(None, None, 'head'), may hold values from -0.25 to 0.25
- conv_kernel: float32 [4, 3, 1024], P(None, None, 'head'), may hold values from -3 to 3
- persistent: bfloat16 [2, 16, 1024], P(None, None, 'head'), may hold values from -8 to 8
- out_weight: bfloat16 [1024, 1024], P('head'), may hold values from -0.1875 to 0.1875
- ffn_gain: bfloat16 [1024], P('head'), may hold values from 0.5 to 1.5
- gate_up: bfloat16 [2, 1024, 2816], P(None, None, 'head'), may hold values from -0.1875 to 0.1875
- down_weight: bfloat16 [2816, 1024], P('head'), may hold values from -0.109375 to 0.109375
- memory_decay: float32 [8192, 8], P('seq', 'head'), may hold values from 0.5 to 1
- momentum_decay: float32 [8192, 8], P('seq', 'head'), may hold values from 0.5 to 1
- doc_start: int32 [8192], P('seq'), may hold values from 0 to 8191, as said below
Outputs:
- output: bfloat16 [8192, 1024], P('seq', 'head')
- input_grad: float32 [8192, 1024], P('seq', 'head')
- grad_norm_gain: float32 [1024], P('head')
- grad_qkv: float32 [3, 1024, 1024], P(None, 'seq', 'head')
- grad_conv: float32 [4, 3, 1024], P(None, None, 'head')
- grad_persistent: float32 [2, 16, 1024], P(None, None, 'head')
- grad_out: float32 [1024, 1024], P('head', 'seq')
- grad_ffn_gain: float32 [1024], P('head')
- grad_gate_up: float32 [2, 1024, 2816], P(None, 'seq', 'head')
- grad_down: float32 [2816, 1024], P('head', 'seq')
The draws below stay inside these ranges and needn't reach their ends.
Inputs may be any that keep to these rules, and one draw needn't show every extreme that they name: doc_start[t] <= t, and doc_start[t] is t or doc_start[t - 1].
All inputs are finite; a program needn't handle non-finite values.
Results may differ from the reference program's by a relative error of at most 0.02.
Values may be sent and summed in bfloat16 or wider, within the bound.
No kernel may reach another device: no remote copies, remote signals or barrier semaphores. Data moves between devices by JAX's collectives and lax.ppermute only.
A program may use at most 192 MiB of HBM per device.

```python
import math
import jax
import jax.numpy as jnp
from jax import lax

D = 1024
HEADS = 8
DH = 128
FF = 2816
KW = 4
PERSIST = 16
SEG = 1024
MBLK = 256
TOK_DEV = 1024
TOKEN_COUNT = 8192
HD = 1024


def decay_law(key, slow_share, slow_low, slow_high):
    random_subkeys = jax.random.split(key, 7)
    slow_heads = jax.random.uniform(random_subkeys[0], (HEADS,)) < slow_share
    slow_rate = jnp.exp(jax.random.uniform(random_subkeys[1], (HEADS,), minval=math.log(slow_low), maxval=math.log(slow_high))) / TOK_DEV
    fast_rate = jnp.exp(jax.random.uniform(random_subkeys[2], (HEADS,), minval=math.log(1.0 / 50.0), maxval=math.log(1.0 / 30.0)))
    baseline_rate = jnp.where(slow_heads, slow_rate, fast_rate)
    device_count = TOKEN_COUNT // TOK_DEV
    device_multiplier = jnp.exp(jax.random.uniform(random_subkeys[3], (device_count, 1, HEADS), minval=-0.7, maxval=0.7))
    device_multiplier = jnp.broadcast_to(device_multiplier, (device_count, TOK_DEV, HEADS)).reshape(TOKEN_COUNT, HEADS)
    coarse_rows = jax.random.uniform(random_subkeys[4], (TOKEN_COUNT, HEADS), minval=0.5, maxval=1.5)
    spike_rows = jax.random.uniform(random_subkeys[5], (TOKEN_COUNT, 1)) < 3.0 / TOKEN_COUNT
    intensity = jax.random.uniform(random_subkeys[6], (TOKEN_COUNT, HEADS), minval=0.5, maxval=0.8)
    decay_factor_rows = jnp.where(spike_rows, intensity, jnp.exp(-baseline_rate * device_multiplier * coarse_rows))
    return decay_factor_rows.astype(jnp.float32)


def draw_memory_decay(key, part):
    key = jax.random.fold_in(key, 21)
    return decay_law(key, 0.5, 0.01, 0.05)


def draw_momentum_decay(key, part):
    key = jax.random.fold_in(key, 22)
    return decay_law(key, 0.5, 0.4, 1.2)


def draw_doc_start(key, part):
    key = jax.random.fold_in(key, 23)
    random_subkeys = jax.random.split(key, 4)
    first_end = jax.random.randint(random_subkeys[0], (), 1, TOK_DEV)
    last_start = jax.random.randint(random_subkeys[1], (), TOKEN_COUNT - TOK_DEV + 1, TOKEN_COUNT)
    head_cuts = jax.random.randint(random_subkeys[2], (4,), 0, first_end)
    tail_cuts = jax.random.randint(random_subkeys[3], (4,), last_start, TOKEN_COUNT)
    bounds = jnp.concatenate([jnp.zeros((1,), jnp.int32), first_end[None], last_start[None], head_cuts, tail_cuts]).astype(jnp.int32)
    places = jnp.arange(TOKEN_COUNT, dtype=jnp.int32)
    starts = jnp.max(jnp.where(bounds[None, :] <= places[:, None], bounds[None, :], 0), axis=1)
    return starts.astype(jnp.int32)


def spiked(entries, key, source, target, shards_of, factor):
    owner, partner = [(jnp.arange(entries.shape[axis_at]) // (entries.shape[axis_at] // shards_of)).reshape([-1 if axis == axis_at else 1 for axis in range(entries.ndim)]) for axis_at in (source, target)]
    chosen = jax.random.permutation(key, shards_of)[partner]
    strong = (owner == chosen) | (owner == (partner + shards_of // 2) % shards_of)
    return jnp.where(strong, factor * entries, entries)


def block_levels(key, shape, cuts, low, high):
    def one(dim, parts):
        heights = jax.random.uniform(jax.random.fold_in(jax.random.fold_in(key, 6), dim), (parts,), jnp.float32, low / len(cuts), high / len(cuts))
        return jnp.repeat(jnp.exp(heights), shape[dim] // parts).reshape((-1,) + (1,) * (len(shape) - dim - 1))

    loudness = one(*cuts[0])
    for cut in cuts[1:]:
        loudness = loudness * one(*cut)
    return loudness


def bell_draw(rng, dims, width, limit, cuts=(), held_as=jnp.bfloat16):
    factor_of = block_levels(rng, dims, cuts, -0.22, 0.18) if cuts else 1.0
    array = jax.random.normal(rng, dims, jnp.float32) * width * factor_of
    return jnp.minimum(jnp.maximum(array, -limit), limit).astype(held_as)


def noise_with(key, shape, width, limit, shards, heavy, kind=jnp.bfloat16):
    result = width * jax.random.normal(key, shape, jnp.float32)
    if shards:
        result = result * block_levels(key, shape, shards, -0.22, 0.18)
    return jnp.clip(spiked(result, jax.random.fold_in(key, 3), *heavy), -limit, limit).astype(kind)


def setup_inputs(seed: int = 0) -> dict:
    keys = jax.random.split(jax.random.key(seed), 14)
    return {
        "inputs": noise_with(keys[0], (TOKEN_COUNT, D), 1.0, 6.0, ((0, 8), (1, 4)), (0, 1, 8, 2.0)),
        "cotangent": noise_with(keys[1], (TOKEN_COUNT, D), 1.0, 6.0, ((0, 8), (1, 4)), (0, 1, 8, 2.0)),
        "norm_gain": jnp.clip(1.0 + 0.1 * jax.random.normal(keys[2], (D,), jnp.float32), 0.5, 1.5).astype(jnp.bfloat16),
        "qkv_weight": bell_draw(keys[3], (3, D, HD), (D // 2) ** -0.5, 0.25, ((2, 4),)),
        "conv_kernel": bell_draw(keys[4], (KW, 3, HD), KW ** -0.5, 3.0, ((2, 4),), jnp.float32),
        "persistent": bell_draw(keys[5], (2, PERSIST, HD), 1.41, 8.0, ((2, 4),)),
        "out_weight": bell_draw(keys[6], (HD, D), HD ** -0.5, 0.1875, ((0, 4),)),
        "ffn_gain": jnp.clip(1.0 + 0.1 * jax.random.normal(keys[7], (D,), jnp.float32), 0.5, 1.5).astype(jnp.bfloat16),
        "gate_up": bell_draw(keys[8], (2, D, FF), D ** -0.5, 0.1875, ((2, 4),)),
        "down_weight": bell_draw(keys[9], (FF, D), FF ** -0.5, 0.109375, ((0, 4),)),
        "memory_decay": draw_memory_decay(jax.random.fold_in(keys[13], 71), 0),
        "momentum_decay": draw_momentum_decay(jax.random.fold_in(keys[13], 71), 0),
        "doc_start": draw_doc_start(jax.random.fold_in(keys[13], 71), 0),
    }


PRECISE = lax.Precision.HIGHEST
EPSILON = 1e-06
MEMORY_FLOOR = 64.0
MASKED = -1e+30

@jax.custom_vjp
def low(v):
    return lax.optimization_barrier(v.astype(jnp.bfloat16)).astype(jnp.float32)

@jax.custom_vjp
def low_back(v):
    return v

def low_keep(v):
    return (low(v), None)

def low_pass(kept, grad):
    return (grad,)

def back_keep(v):
    return (v, None)

def back_low(kept, grad):
    return (low(grad),)
low.defvjp(low_keep, low_pass)
low_back.defvjp(back_keep, back_low)

def memory_block(carry_mem, carry_mom, query_block, key_block, value_block, log_keep, log_carry, starts, places):
    keep_sum = jnp.cumsum(log_keep)
    carry_sum = jnp.cumsum(log_carry)
    linked = (starts[:, None] <= places[None, :]) & (places[None, :] <= places[:, None])
    keep_mat = jnp.where(linked, jnp.exp(jnp.minimum(keep_sum[:, None] - keep_sum[None, :], 0.0)), 0.0)
    carry_mat = jnp.where(linked, jnp.exp(jnp.minimum(carry_sum[:, None] - carry_sum[None, :], 0.0)), 0.0)
    fresh_rows = starts < places[0]
    keep_weight = jnp.where(fresh_rows, jnp.exp(keep_sum), 0.0)
    carried = jnp.where(fresh_rows, jnp.exp(carry_sum), 0.0)
    kernel = jnp.dot(keep_mat, carry_mat, precision=PRECISE)
    cross_weight = jnp.dot(keep_mat, carried, precision=PRECISE)
    affinity = jnp.dot(query_block, key_block.T, precision=PRECISE)
    reading = jnp.dot(kernel * affinity, value_block, precision=PRECISE)
    reading = reading + keep_weight[:, None] * jnp.dot(query_block, carry_mem.T, precision=PRECISE)
    reading = reading + cross_weight[:, None] * jnp.dot(query_block, carry_mom.T, precision=PRECISE)
    mem_end = keep_weight[-1] * carry_mem + cross_weight[-1] * carry_mom + jnp.dot((value_block * kernel[-1][:, None]).T, key_block, precision=PRECISE)
    mom_end = carried[-1] * carry_mom + jnp.dot((value_block * carry_mat[-1][:, None]).T, key_block, precision=PRECISE)
    return (reading, mem_end, mom_end, keep_weight, cross_weight, carried)

def memory_stream(queries, key_rows, value_rows, log_keep, log_carry, starts):
    block_count = TOKEN_COUNT // MBLK

    def blocks(tensor):
        return tensor.reshape(block_count, MBLK, HEADS, DH).transpose(0, 2, 1, 3)

    def rate_blocks(tensor):
        return tensor.reshape(block_count, MBLK, HEADS).transpose(0, 2, 1)
    places = jnp.arange(TOKEN_COUNT, dtype=jnp.int32).reshape(block_count, MBLK)

    def advance(carry, pieces):
        reading, mem_end, mom_end, _, _, _ = jax.vmap(memory_block, in_axes=(0, 0, 0, 0, 0, 0, 0, None, None))(carry[0], carry[1], *pieces)
        return ((mem_end, mom_end), reading)
    zero_state = jnp.zeros((HEADS, DH, DH), queries.dtype)
    scanned = (blocks(queries), blocks(key_rows), blocks(value_rows), rate_blocks(log_keep), rate_blocks(log_carry), starts.reshape(block_count, MBLK), places)
    _, readings = lax.scan(jax.checkpoint(advance), (zero_state, zero_state), scanned)
    return readings.transpose(0, 2, 1, 3).reshape(TOKEN_COUNT, HEADS, DH)

def segment_attention(queries, key_rows, value_rows, starts, places, fixed_keys, fixed_values):
    all_keys = jnp.concatenate([fixed_keys, key_rows], 0)
    all_values = jnp.concatenate([fixed_values, value_rows], 0)
    raw_scores = low_back(jnp.einsum('thd,shd->hts', queries, all_keys, precision=PRECISE))
    scores = raw_scores * DH ** (-0.5)
    token_ok = (places[None, :] <= places[:, None]) & (places[None, :] >= starts[:, None])
    visible = jnp.concatenate([jnp.ones((queries.shape[0], fixed_keys.shape[0]), jnp.bool_), token_ok], 1)
    scores = jnp.where(visible[None], scores, MASKED)
    weights = jax.nn.softmax(scores, axis=-1)
    return low_back(jnp.einsum('hts,shd->thd', low(weights), all_values, precision=PRECISE))

def forward(inputs, norm_gain, qkv_weight, conv_kernel, persistent, out_weight, ffn_gain, gate_up, down_weight, log_keep, log_carry, starts):
    scale_one = lax.rsqrt(lax.optimization_barrier(jnp.mean(inputs * inputs, -1, keepdims=True)) + EPSILON)
    hidden_one = low(inputs * scale_one * norm_gain)
    projected = low_back(jnp.einsum('td,kdn->tkn', hidden_one, qkv_weight, precision=PRECISE))
    places = jnp.arange(TOKEN_COUNT, dtype=jnp.int32)
    mixed_rows = jnp.zeros_like(projected)
    for shift_tap in range(KW):
        shifted = jnp.concatenate([jnp.zeros((shift_tap,) + projected.shape[1:], projected.dtype), projected[:TOKEN_COUNT - shift_tap]], 0)
        inside = (places - shift_tap >= starts).astype(projected.dtype)
        mixed_rows = mixed_rows + conv_kernel[shift_tap][None] * shifted * inside[:, None, None]
    rounded = low(mixed_rows)
    queries = rounded[:, 0].reshape(TOKEN_COUNT, HEADS, DH)
    key_rows = rounded[:, 1].reshape(TOKEN_COUNT, HEADS, DH)
    value_rows = rounded[:, 2].reshape(TOKEN_COUNT, HEADS, DH)
    fixed_keys = persistent[0].reshape(PERSIST, HEADS, DH)
    fixed_values = persistent[1].reshape(PERSIST, HEADS, DH)
    seg_count = TOKEN_COUNT // SEG

    def one_segment(pieces):
        return segment_attention(pieces[0], pieces[1], pieces[2], pieces[3], pieces[4], fixed_keys, fixed_values)
    attended = lax.map(jax.checkpoint(one_segment), (queries.reshape(seg_count, SEG, HEADS, DH), key_rows.reshape(seg_count, SEG, HEADS, DH), value_rows.reshape(seg_count, SEG, HEADS, DH), starts.reshape(seg_count, SEG), places.reshape(seg_count, SEG)))
    attended = attended.reshape(TOKEN_COUNT, HEADS, DH)
    memory_out = memory_stream(queries, key_rows, value_rows, log_keep, log_carry, starts)
    normed_mem = memory_out * lax.rsqrt(lax.optimization_barrier(jnp.mean(memory_out * memory_out, -1, keepdims=True)) + MEMORY_FLOOR)
    merged = low((attended + normed_mem).reshape(TOKEN_COUNT, HEADS * DH))
    middle = inputs + low_back(jnp.dot(merged, out_weight, precision=PRECISE))
    scale_two = lax.rsqrt(lax.optimization_barrier(jnp.mean(middle * middle, -1, keepdims=True)) + EPSILON)
    hidden_two = low(middle * scale_two * ffn_gain)
    gate_vals = low_back(jnp.dot(hidden_two, gate_up[0], precision=PRECISE))
    up_vals = low_back(jnp.dot(hidden_two, gate_up[1], precision=PRECISE))
    activated = low(jax.nn.silu(gate_vals) * up_vals)
    return middle + low_back(jnp.dot(activated, down_weight, precision=PRECISE))

def reference(inputs, cotangent, norm_gain, qkv_weight, conv_kernel, persistent, out_weight, ffn_gain, gate_up, down_weight, memory_decay, momentum_decay, doc_start):
    log_keep = jnp.log(memory_decay.astype(jnp.float32))
    log_carry = jnp.log(momentum_decay.astype(jnp.float32))

    def closed(*weights):
        return forward(*weights, log_keep, log_carry, doc_start)
    primal = (inputs.astype(jnp.float32), norm_gain.astype(jnp.float32), qkv_weight.astype(jnp.float32), conv_kernel.astype(jnp.float32), persistent.astype(jnp.float32), out_weight.astype(jnp.float32), ffn_gain.astype(jnp.float32), gate_up.astype(jnp.float32), down_weight.astype(jnp.float32))
    result_rows, pull_grads = jax.vjp(closed, *primal)
    gradients = pull_grads(cotangent.astype(jnp.float32))
    return (result_rows.astype(jnp.bfloat16), gradients[0], gradients[1], gradients[2], gradients[3], gradients[4], gradients[5], gradients[6], gradients[7], gradients[8])
```

```python
import functools

import jax
import jax.numpy as jnp
from jax import lax
from jax.experimental import pallas as pl
from jax.experimental.pallas import tpu as pltpu
from jax.sharding import PartitionSpec as P

DH = 128
KW = 4
SEG = 1024
MBLK = 256
EPSILON = 1e-06
MEMORY_FLOOR = 64.0
MASKED = -1e30
F32 = jnp.float32
BF16 = jnp.bfloat16
NN = (((1,), (0,)), ((), ()))
NT = (((1,), (1,)), ((), ()))
TN = (((0,), (0,)), ((), ()))
REL = 4


def mm(a, b, dims=NN):
    return lax.dot_general(a, b, dims, preferred_element_type=F32)


def exact(a, b, dims=NN):
    return lax.dot_general(
        a, b, dims, precision=lax.Precision.HIGHEST, preferred_element_type=F32
    )


def call(kernel, grid, in_specs, out_specs, out_shape, scratch=(), flops=0, moved=0, prefetch=0):
    spec = pltpu.PrefetchScalarGridSpec(
        num_scalar_prefetch=prefetch,
        grid=grid,
        in_specs=in_specs,
        out_specs=out_specs,
        scratch_shapes=list(scratch),
    )
    return pl.pallas_call(
        kernel,
        grid_spec=spec,
        out_shape=out_shape,
        compiler_params=pltpu.CompilerParams(vmem_limit_bytes=56 * 2**20),
        cost_estimate=pl.CostEstimate(
            flops=int(flops), bytes_accessed=int(moved), transcendentals=0
        ),
    )


def whole(shape):
    return pl.BlockSpec(shape, lambda *_: (0,) * len(shape))


def sds(shape, dtype):
    return jax.ShapeDtypeStruct(shape, dtype)


def iota(shape, dim):
    return lax.broadcasted_iota(jnp.int32, shape, dim)


def swap(x, axis, bit):
    count = lax.axis_size(axis)
    return lax.ppermute(x, axis, [(i, i ^ bit) for i in range(count)])


def shifted(x, axis, by):
    count = lax.axis_size(axis)
    return lax.ppermute(x, axis, [(i, i + by) for i in range(count) if 0 <= i + by < count])


def gather_rel(x):
    far = swap(x, "head", 2)
    near = swap(x, "head", 1)
    return [x, near, far, swap(far, "head", 1)]


def sum_over(x, axis):
    bit = 1
    while bit < lax.axis_size(axis):
        x = x + swap(x, axis, bit)
        bit *= 2
    return x


def front_kernel(rank_ref, *refs, heads):
    blocks, smalls = refs[:REL], refs[REL : 2 * REL]
    (
        w_ref,
        conv_ref,
        starts_ref,
        decay_ref,
        x_out,
        hid_out,
        scale_out,
        proj_out,
        qkv_out,
        kmat_out,
        aux_out,
        part_out,
        halo_out,
        gain_out,
        state_out,
        load_out,
        small_sc,
        proj_sc,
        state_sc,
    ) = refs[2 * REL :]
    b = pl.program_id(0)
    rank = rank_ref[0]
    rows, width = blocks[0].shape
    local = heads * DH
    spans = [pl.ds(pl.multiple_of((rank ^ k) * width, width), width) for k in range(REL)]
    for k in range(REL):
        x_out[:, spans[k]] = blocks[k][...]
    scal = 2 * heads * DH

    @pl.when(b == 0)
    def _():
        for k in range(REL):
            small_sc[:, spans[k]] = smalls[k][...]
        small = small_sc[...].astype(F32)
        gain_out[...] = small
        scale = lax.rsqrt(jnp.mean(small * small, -1, keepdims=True) + EPSILON)
        hidden = (small * scale * small[8:9]).astype(BF16)
        for c in range(3):
            proj_sc[0:8, c * local : (c + 1) * local] = mm(hidden, w_ref[c])[0:8]
        halo_out[...] = proj_sc[0:8]
        state_sc[0:scal] = jnp.zeros((scal, DH), F32)
        row = iota((8, DH), 0)
        state_sc[scal : scal + 8] = jnp.where(
            (row < heads) | ((row >= 2 * heads) & (row < 3 * heads)), 1.0, 0.0
        ).astype(F32)

    gain = gain_out[8:9]
    x = x_out[...].astype(F32)
    scale = lax.rsqrt(jnp.mean(x * x, -1, keepdims=True) + EPSILON)
    hidden = (x * scale * gain).astype(BF16)
    hid_out[...] = hidden
    scale_out[...] = scale
    for c in range(3):
        proj_sc[8 : 8 + rows, c * local : (c + 1) * local] = mm(hidden, w_ref[c])
    base = b * rows
    place = base + iota((rows, 1), 0)
    starts = starts_ref[...]
    mixed = jnp.zeros((rows, 3 * local), F32)
    for j in range(KW):
        inside = (place - j >= starts).astype(F32)
        mixed = mixed + conv_ref[j : j + 1] * proj_sc[8 - j : 8 - j + rows] * inside
    rounded = mixed.astype(BF16)
    qkv_out[...] = rounded
    proj_out[...] = proj_sc[8 : 8 + rows].astype(BF16)
    proj_sc[0:8] = proj_sc[rows : rows + 8]

    logs = jnp.log(decay_ref[...])
    below = iota((rows, rows), 0)
    right = iota((rows, rows), 1)
    rows_sum = exact(logs, (below <= right).astype(F32))
    cols_sum = exact((right <= below).astype(F32), logs, NT)
    linked = (right <= below) & (base + right >= starts)
    fresh = starts < base
    last_start = starts[rows - 1 : rows]
    reaches_end = place >= last_start
    last_row = (iota((rows, DH), 0) == rows - 1).astype(BF16)
    lane = iota((rows, DH), 1)
    aux = jnp.zeros((rows, DH), F32)
    for h in range(heads):
        keep_col, keep_row = cols_sum[:, h : h + 1], rows_sum[h : h + 1]
        carry_col = cols_sum[:, heads + h : heads + h + 1]
        carry_row = rows_sum[heads + h : heads + h + 1]
        keep_mat = jnp.where(linked, jnp.exp(jnp.minimum(keep_col - keep_row, 0.0)), 0.0)
        carry_mat = jnp.where(linked, jnp.exp(jnp.minimum(carry_col - carry_row, 0.0)), 0.0)
        keep_low = keep_mat.astype(BF16)
        kernel = mm(keep_low, carry_mat.astype(BF16)).astype(BF16)
        kmat_out[h, 0] = kernel
        keep_weight = jnp.where(fresh, jnp.exp(keep_col), 0.0)
        carried = jnp.where(fresh, jnp.exp(carry_col), 0.0)
        cross = mm(keep_low, jnp.broadcast_to(carried, (rows, DH)).astype(BF16))
        end_kernel = mm(kernel, last_row, TN)
        end_carry = jnp.where(
            reaches_end, jnp.exp(jnp.minimum(carry_col[rows - 1 : rows] - carry_col, 0.0)), 0.0
        )
        for slot, column in enumerate((keep_weight, cross, carried, end_kernel, end_carry)):
            aux = jnp.where(lane == slot * heads + h, column, aux)
        keys = rounded[:, local + h * DH : local + (h + 1) * DH]
        values = rounded[:, 2 * local + h * DH : 2 * local + (h + 1) * DH].astype(F32)
        mem_part = mm((values * end_kernel).astype(BF16), keys, TN)
        mom_part = mm((values * end_carry).astype(BF16), keys, TN)
        lo, mid = h * DH, (heads + h) * DH
        part_out[0, lo : lo + DH] = mem_part
        part_out[0, mid : mid + DH] = mom_part
        keep_end = jnp.broadcast_to(keep_weight[rows - 1 : rows], (1, DH))
        cross_end = cross[rows - 1 : rows]
        carry_end = jnp.broadcast_to(carried[rows - 1 : rows], (1, DH))
        memory, momentum = state_sc[lo : lo + DH], state_sc[mid : mid + DH]
        state_sc[lo : lo + DH] = keep_end * memory + cross_end * momentum + mem_part
        state_sc[mid : mid + DH] = carry_end * momentum + mom_part
        keep_at, cross_at, carry_at = scal + h, scal + heads + h, scal + 2 * heads + h
        keep_dev = state_sc[keep_at : keep_at + 1]
        cross_dev = state_sc[cross_at : cross_at + 1]
        carry_dev = state_sc[carry_at : carry_at + 1]
        state_sc[keep_at : keep_at + 1] = keep_end * keep_dev
        state_sc[cross_at : cross_at + 1] = keep_end * cross_dev + cross_end * carry_dev
        state_sc[carry_at : carry_at + 1] = carry_end * carry_dev
    aux_out[...] = aux

    @pl.when(b == pl.num_programs(0) - 1)
    def _():
        state_out[...] = state_sc[...]
        pack_load(load_out, state_sc[...], scal)


def pack_load(load_out, state, scal):
    load_out[0:scal] = state[0:scal].astype(BF16)
    tail = state[scal : scal + 8]
    high = tail.astype(BF16).astype(F32)
    load_out[scal : scal + 16] = jnp.concatenate([high, tail - high], 0).astype(BF16)


def unpack(ref, scal):
    if ref.dtype == F32:
        return ref[0:scal], ref[scal : scal + 8]
    tail = ref[scal : scal + 16].astype(F32)
    return ref[0:scal].astype(F32), tail[0:8] + tail[8:16]


def front(rank, blocks, smalls, weight, conv, starts, decays, heads):
    total, width = blocks[0].shape
    model = width * REL
    local = heads * DH
    count = total // MBLK
    scal = 2 * heads * DH
    at = lambda b, *_: (b, 0)
    return call(
        functools.partial(front_kernel, heads=heads),
        (count,),
        [pl.BlockSpec((MBLK, width), at)] * REL
        + [whole(smalls[0].shape)] * REL
        + [
            whole(weight.shape),
            whole(conv.shape),
            pl.BlockSpec((MBLK, 1), at),
            pl.BlockSpec((8, MBLK), lambda b, *_: (0, b)),
        ],
        [
            pl.BlockSpec((MBLK, model), at),
            pl.BlockSpec((MBLK, model), at),
            pl.BlockSpec((MBLK, 1), at),
            pl.BlockSpec((MBLK, 3 * local), at),
            pl.BlockSpec((MBLK, 3 * local), at),
            pl.BlockSpec((heads, 1, MBLK, MBLK), lambda b, *_: (0, b, 0, 0)),
            pl.BlockSpec((MBLK, DH), at),
            pl.BlockSpec((1, scal, DH), lambda b, *_: (b, 0, 0)),
            whole((8, 3 * local)),
            whole((16, model)),
            whole((scal + 8, DH)),
            whole((scal + 16, DH)),
        ],
        [
            sds((total, model), BF16),
            sds((total, model), BF16),
            sds((total, 1), F32),
            sds((total, 3 * local), BF16),
            sds((total, 3 * local), BF16),
            sds((heads, count, MBLK, MBLK), BF16),
            sds((total, DH), F32),
            sds((count, scal, DH), F32),
            sds((8, 3 * local), F32),
            sds((16, model), F32),
            sds((scal + 8, DH), F32),
            sds((scal + 16, DH), BF16),
        ],
        [
            pltpu.VMEM((16, model), BF16),
            pltpu.VMEM((MBLK + 8, 3 * local), F32),
            pltpu.VMEM((scal + 8, DH), F32),
        ],
        flops=2.2e9,
        moved=12e6,
        prefetch=1,
    )(rank, *blocks, *smalls, weight, conv, starts, decays)


def join_kernel(first_ref, second_ref, state_out, load_out, *, heads, backward):
    scal = 2 * heads * DH
    first, first_tail = unpack(first_ref, scal)
    second, second_tail = unpack(second_ref, scal)
    tail = []
    for h in range(heads):
        lo, mid = h * DH, (heads + h) * DH
        keep_one, keep_two = first_tail[h : h + 1], second_tail[h : h + 1]
        cross_one, cross_two = (
            first_tail[heads + h : heads + h + 1],
            second_tail[heads + h : heads + h + 1],
        )
        carry_one, carry_two = (
            first_tail[2 * heads + h : 2 * heads + h + 1],
            second_tail[2 * heads + h : 2 * heads + h + 1],
        )
        mem_one, mom_one = first[lo : lo + DH], first[mid : mid + DH]
        mem_two, mom_two = second[lo : lo + DH], second[mid : mid + DH]
        if backward:
            state_out[lo : lo + DH] = mem_two + keep_two * mem_one
            state_out[mid : mid + DH] = mom_two + cross_two * mem_one + carry_two * mom_one
            cross = cross_two * keep_one + carry_two * cross_one
        else:
            state_out[lo : lo + DH] = keep_two * mem_one + cross_two * mom_one + mem_two
            state_out[mid : mid + DH] = carry_two * mom_one + mom_two
            cross = keep_two * cross_one + cross_two * carry_one
        state_out[scal + h : scal + h + 1] = keep_two * keep_one
        state_out[scal + heads + h : scal + heads + h + 1] = cross
        state_out[scal + 2 * heads + h : scal + 2 * heads + h + 1] = carry_two * carry_one
    for spare in range(3 * heads, 8):
        state_out[scal + spare : scal + spare + 1] = jnp.zeros((1, DH), F32)
    pack_load(load_out, state_out[...], scal)


def join(first, second, heads, backward):
    scal = 2 * heads * DH
    return call(
        functools.partial(join_kernel, heads=heads, backward=backward),
        (1,),
        [whole(first.shape), whole(second.shape)],
        [whole((scal + 8, DH)), whole((scal + 16, DH))],
        [sds((scal + 8, DH), F32), sds((scal + 16, DH), BF16)],
        flops=1e6,
        moved=1e6,
    )(first, second)


def entering(load, heads, backward):
    count = lax.axis_size("seq")
    sign = -1 if backward else 1
    one = shifted(load, "seq", sign)
    two = shifted(load, "seq", 2 * sign)
    covered = 2
    state, load = join(two, one, heads, backward)
    while covered < count - 1:
        state, load = join(shifted(load, "seq", covered * sign), state, heads, backward)
        covered *= 2
    return state


def attend_kernel(q_ref, k_ref, v_ref, fix_ref, starts_ref, kmat_ref, *outs):
    att_out, ratio_out, intra_out, prob_out, fixp_out = outs
    total = q_ref.shape[0]
    fixed_keys, fixed_values = fix_ref[0], fix_ref[1]
    factor = DH ** (-0.5)
    for i in range(total // MBLK):
        span = slice(i * MBLK, (i + 1) * MBLK)
        seen = (i + 1) * MBLK
        query = q_ref[span]
        raw = mm(query, k_ref[0:seen], NT)
        fixed = mm(query, fixed_keys, NT)
        key_at = iota((MBLK, seen), 1)
        ok = (key_at >= starts_ref[span]) & (key_at <= i * MBLK + iota((MBLK, seen), 0))
        raw = jnp.where(ok, raw, MASKED)
        top = jnp.maximum(jnp.max(raw, -1, keepdims=True), jnp.max(fixed, -1, keepdims=True))
        weights = jnp.exp((raw - top) * factor)
        fix_weights = jnp.exp((fixed - top) * factor)
        scale = 1.0 / (
            jnp.sum(weights, -1, keepdims=True) + jnp.sum(fix_weights, -1, keepdims=True)
        )
        low = (weights * scale).astype(BF16)
        fix_low = (fix_weights * scale).astype(BF16)
        prob_out[span, 0:seen] = low
        fixp_out[span] = fix_low
        attended = mm(low, v_ref[0:seen]) + mm(fix_low, fixed_values)
        held = jnp.sum(low.astype(F32), -1, keepdims=True) + jnp.sum(
            fix_low.astype(F32), -1, keepdims=True
        )
        att_out[span] = attended
        ratio_out[span] = attended / held
        near = mm(query, k_ref[span], NT)
        kernel = kmat_ref[0, i].astype(F32)
        intra_out[span] = mm((kernel * near).astype(BF16), v_ref[span])


def attend(qkv, fixed, starts, kmat, head, heads):
    total = qkv.shape[0]
    count = total // MBLK
    fixed_count = fixed.shape[1]
    lanes = lambda c: pl.BlockSpec((total, DH), lambda *_: (0, c * heads + head))
    return call(
        attend_kernel,
        (1,),
        [
            lanes(0),
            lanes(1),
            lanes(2),
            pl.BlockSpec((2, fixed_count, DH), lambda *_: (0, 0, head)),
            whole((total, 1)),
            pl.BlockSpec((1, count, MBLK, MBLK), lambda *_: (head, 0, 0, 0)),
        ],
        [whole((total, DH))] * 3 + [whole((total, total)), whole((total, fixed_count))],
        [sds((total, DH), F32)] * 3
        + [sds((total, total), BF16), sds((total, fixed_count), BF16)],
        flops=1.5e9,
        moved=8e6,
    )(qkv, qkv, qkv, fixed, starts, kmat)


def attend_back_kernel(
    q_ref, k_ref, v_ref, fix_ref, prob_ref, fixp_ref, ratio_ref, grad_ref, gmem_ref, kmat_ref, *outs
):
    dq_out, dk_out, dv_out, dfix_out, dqm_out, dkm_out, dvm_out = outs
    total = q_ref.shape[0]
    fixed_keys, fixed_values = fix_ref[0], fix_ref[1]
    factor = DH ** (-0.5)
    dfix_k = jnp.zeros(fixed_keys.shape, F32)
    dfix_v = jnp.zeros(fixed_keys.shape, F32)
    for i in reversed(range(total // MBLK)):
        span = slice(i * MBLK, (i + 1) * MBLK)
        seen = (i + 1) * MBLK
        query, grad = q_ref[span], grad_ref[span]
        delta = jnp.sum(grad.astype(F32) * ratio_ref[span], -1, keepdims=True)
        low, fix_low = prob_ref[span, 0:seen], fixp_ref[span]
        back = mm(grad, v_ref[0:seen], NT)
        fix_back = mm(grad, fixed_values, NT)
        grad_raw = (low.astype(F32) * (back - delta) * factor).astype(BF16)
        fix_raw = (fix_low.astype(F32) * (fix_back - delta) * factor).astype(BF16)
        dq_out[span] = mm(grad_raw, k_ref[0:seen]) + mm(fix_raw, fixed_keys)
        dk, dv = mm(grad_raw, query, TN), mm(low, grad, TN)
        if seen == total:
            dk_out[...] = dk
            dv_out[...] = dv
        else:
            dk_out[0:seen] += dk
            dv_out[0:seen] += dv
        dfix_k += mm(fix_raw, query, TN)
        dfix_v += mm(fix_low, grad, TN)
        keys, values, gmem = k_ref[span], v_ref[span], gmem_ref[span]
        kernel = kmat_ref[0, i].astype(F32)
        near = (kernel * mm(query, keys, NT)).astype(BF16)
        cross = (kernel * mm(gmem, values, NT)).astype(BF16)
        dqm_out[span] = mm(cross, keys)
        dkm_out[span] = mm(cross, query, TN)
        dvm_out[span] = mm(near, gmem, TN)
    dfix_out[0] = dfix_k
    dfix_out[1] = dfix_v


def attend_back(qkv, fixed, prob, fixp, ratio, grads, gmem, kmat, head, heads):
    total = qkv.shape[0]
    count = total // MBLK
    fixed_count = fixed.shape[1]
    lanes = lambda c: pl.BlockSpec((total, DH), lambda *_: (0, c * heads + head))
    return call(
        attend_back_kernel,
        (1,),
        [
            lanes(0),
            lanes(1),
            lanes(2),
            pl.BlockSpec((2, fixed_count, DH), lambda *_: (0, 0, head)),
            whole((total, total)),
            whole((total, fixed_count)),
            whole((total, DH)),
            lanes(0),
            lanes(0),
            pl.BlockSpec((1, count, MBLK, MBLK), lambda *_: (head, 0, 0, 0)),
        ],
        [whole((total, DH))] * 3 + [whole((2, fixed_count, DH))] + [whole((total, DH))] * 3,
        [sds((total, DH), F32)] * 3
        + [sds((2, fixed_count, DH), F32)]
        + [sds((total, DH), F32)] * 3,
        flops=3e9,
        moved=10e6,
    )(qkv, qkv, qkv, fixed, prob, fixp, ratio, grads, gmem, kmat)


def merge_kernel(q_ref, *refs, heads):
    atts, intras = refs[:heads], refs[heads : 2 * heads]
    aux_ref, part_ref, state_ref, merged_out, normed_out, scale_out, state_low, state_sc = refs[
        2 * heads :
    ]
    rows = q_ref.shape[0]
    lane = iota((rows, DH), 1)
    scales = jnp.zeros((rows, DH), F32)

    @pl.when(pl.program_id(0) == 0)
    def _():
        state_sc[...] = state_ref[0 : state_sc.shape[0]]

    for h in range(heads):
        lo, mid = h * DH, (heads + h) * DH
        memory, momentum = state_sc[lo : lo + DH], state_sc[mid : mid + DH]
        memory_low, momentum_low = memory.astype(BF16), momentum.astype(BF16)
        state_low[0, lo : lo + DH] = memory_low
        state_low[0, mid : mid + DH] = momentum_low
        query = q_ref[:, lo : lo + DH]
        keep = aux_ref[:, h : h + 1]
        cross = aux_ref[:, heads + h : heads + h + 1]
        carry = aux_ref[:, 2 * heads + h : 2 * heads + h + 1]
        out = (
            intras[h][...]
            + keep * mm(query, memory_low, NT)
            + cross * mm(query, momentum_low, NT)
        )
        scale = lax.rsqrt(jnp.mean(out * out, -1, keepdims=True) + MEMORY_FLOOR)
        normed = out * scale
        normed_out[:, lo : lo + DH] = normed
        scales = jnp.where(lane == h, scale, scales)
        merged_out[:, lo : lo + DH] = (atts[h][...] + normed).astype(BF16)
        end = slice(rows - 1, rows)
        state_sc[lo : lo + DH] = (
            keep[end] * memory + cross[end] * momentum + part_ref[0, lo : lo + DH]
        )
        state_sc[mid : mid + DH] = carry[end] * momentum + part_ref[0, mid : mid + DH]
    scale_out[...] = scales


def merge(qkv, atts, intras, aux, parts, state, heads):
    total = qkv.shape[0]
    count = total // MBLK
    local = heads * DH
    scal = 2 * local
    at = lambda b, *_: (b, 0)
    by_block = pl.BlockSpec((1, scal, DH), lambda b, *_: (b, 0, 0))
    return call(
        functools.partial(merge_kernel, heads=heads),
        (count,),
        [pl.BlockSpec((MBLK, local), at)]
        + [pl.BlockSpec((MBLK, DH), at)] * (2 * heads + 1)
        + [by_block, whole(state.shape)],
        [
            pl.BlockSpec((MBLK, local), at),
            pl.BlockSpec((MBLK, local), at),
            pl.BlockSpec((MBLK, DH), at),
            by_block,
        ],
        [
            sds((total, local), BF16),
            sds((total, local), F32),
            sds((total, DH), F32),
            sds((count, scal, DH), BF16),
        ],
        [pltpu.VMEM((scal, DH), F32)],
        flops=3e8,
        moved=6e6,
    )(qkv, *atts, *intras, aux, parts, state)


def middle_kernel(rank_ref, *refs):
    merged, weights = refs[:REL], refs[REL : 2 * REL]
    x_ref, gain_ref, hid_out, normed_out, scale_out, share_out, mid_sc = refs[2 * REL :]
    width = share_out.shape[1]
    middle = x_ref[...].astype(F32)
    for k in range(REL):
        middle = middle + mm(merged[k][...], weights[k][...])
    mid_sc[...] = middle
    scale = lax.rsqrt(jnp.mean(middle * middle, -1, keepdims=True) + EPSILON)
    normed = middle * scale
    normed_out[...] = normed.astype(BF16)
    hid_out[...] = (normed * gain_ref[9:10]).astype(BF16)
    scale_out[...] = scale
    share_out[...] = mid_sc[:, pl.ds(pl.multiple_of(rank_ref[0] * width, width), width)]


def middle(rank, merged, weights, x, gains):
    total, model = x.shape
    local = merged[0].shape[1]
    width = model // REL
    at = lambda b, *_: (b, 0)
    return call(
        middle_kernel,
        (total // MBLK,),
        [pl.BlockSpec((MBLK, local), at)] * REL
        + [whole(weights[0].shape)] * REL
        + [pl.BlockSpec((MBLK, model), at), whole(gains.shape)],
        [
            pl.BlockSpec((MBLK, model), at),
            pl.BlockSpec((MBLK, model), at),
            pl.BlockSpec((MBLK, 1), at),
            pl.BlockSpec((MBLK, width), at),
        ],
        [
            sds((total, model), BF16),
            sds((total, model), BF16),
            sds((total, 1), F32),
            sds((total, width), F32),
        ],
        [pltpu.VMEM((MBLK, model), F32)],
        flops=2.2e9,
        moved=10e6,
        prefetch=1,
    )(rank, *merged, *weights, x, gains)


def ffn_kernel(rank_ref, hid_ref, *refs):
    cots = refs[:REL]
    (
        gate_ref,
        down_ref,
        act_out,
        gg_out,
        gu_out,
        cot_out,
        send_out,
        far_out,
        keep_out,
        fsend_out,
        ffar_out,
        fkeep_out,
    ) = refs[REL:]
    step = pl.program_id(0)
    rank = rank_ref[0]
    width = cots[0].shape[1]
    spans = [pl.ds(pl.multiple_of((rank ^ k) * width, width), width) for k in range(REL)]
    for k in range(REL):
        cot_out[:, spans[k]] = cots[k][...]
    hidden = hid_ref[...]
    gate = mm(hidden, gate_ref[0])
    up = mm(hidden, gate_ref[1])
    grad_act = mm(cot_out[...], down_ref[...], NT)
    sig = jax.nn.sigmoid(gate)
    silu = gate * sig
    act = (silu * up).astype(BF16)
    act_out[...] = act
    grad_gate = (grad_act * up * (sig * (1.0 + gate * (1.0 - sig)))).astype(BF16)
    grad_up = (grad_act * silu).astype(BF16)
    gg_out[...] = grad_gate
    gu_out[...] = grad_up
    back = (mm(grad_gate, gate_ref[0], NT) + mm(grad_up, gate_ref[1], NT)).astype(BF16)

    @pl.when(step < 2)
    def _():
        send_out[0] = back

    @pl.when(step == 2)
    def _():
        far_out[0] = back

    @pl.when(step == 3)
    def _():
        keep_out[0] = back

    fkeep_out[...] = mm(act, down_ref[:, spans[0]]).astype(BF16)
    fsend_out[0] = mm(act, down_ref[:, spans[1]]).astype(BF16)
    ffar_out[...] = mm(act, down_ref[:, spans[2]]).astype(BF16)
    fsend_out[1] = mm(act, down_ref[:, spans[3]]).astype(BF16)


def ffn(rank, hidden, cots, gate_up, down):
    total, model = hidden.shape
    units = down.shape[0]
    width = model // REL
    rows = total // REL

    def tok(s, rank_ref):
        g = (s + 1) & 3
        return (rank_ref[0] ^ (g ^ (g >> 1)), 0)

    tok3 = lambda s, r: (0,) + tok(s, r)
    return call(
        ffn_kernel,
        (REL,),
        [pl.BlockSpec((rows, model), tok)]
        + [pl.BlockSpec((rows, width), tok)] * REL
        + [whole(gate_up.shape), whole(down.shape)],
        [pl.BlockSpec((rows, units), tok)] * 3
        + [
            pl.BlockSpec((rows, model), tok),
            pl.BlockSpec((1, rows, model), lambda s, r: (jnp.minimum(s, 1), 0, 0)),
            whole((1, rows, model)),
            whole((1, rows, model)),
            pl.BlockSpec((2, rows, width), tok3),
            pl.BlockSpec((rows, width), tok),
            pl.BlockSpec((rows, width), tok),
        ],
        [sds((total, units), BF16)] * 3
        + [
            sds((total, model), BF16),
            sds((2, rows, model), BF16),
            sds((1, rows, model), BF16),
            sds((1, rows, model), BF16),
            sds((2, total, width), BF16),
            sds((total, width), BF16),
            sds((total, width), BF16),
        ],
        flops=9e9,
        moved=16e6,
        prefetch=1,
    )(rank, hidden, *cots, gate_up, down)


def bend_kernel(rank_ref, keep_ref, near_ref, far_ref, cot_ref, normed_ref, scale_ref, gain_ref, *outs):
    low_out, dgain_out = outs
    grad = (
        keep_ref[0].astype(F32) + near_ref[0].astype(F32) + far_ref[0].astype(F32)
    )
    normed = normed_ref[...].astype(F32)
    dgain_out[...] = jnp.broadcast_to(jnp.sum(grad * normed, 0, keepdims=True), dgain_out.shape)
    g = grad * gain_ref[9:10]
    mean = jnp.mean(g * normed, -1, keepdims=True)
    low_out[...] = (cot_ref[...].astype(F32) + scale_ref[...] * (g - normed * mean)).astype(BF16)


def bend(rank, keep, near, far, cot, normed, scale, gains):
    total, model = cot.shape
    rows = total // REL
    own = lambda s, r: (r[0], 0)
    one = pl.BlockSpec((1, rows, model), lambda *_: (0, 0, 0))
    return call(
        bend_kernel,
        (1,),
        [
            one,
            one,
            one,
            pl.BlockSpec((rows, model), own),
            pl.BlockSpec((rows, model), own),
            pl.BlockSpec((rows, 1), own),
            whole(gains.shape),
        ],
        [whole((rows, model)), whole((8, model))],
        [sds((rows, model), BF16), sds((8, model), F32)],
        flops=5e6,
        moved=4e6,
        prefetch=1,
    )(rank, keep, near, far, cot, normed, scale, gains)


def turn_kernel(rank_ref, *refs, heads):
    lows = refs[:REL]
    (
        w_ref,
        q_ref,
        normed_ref,
        scale_ref,
        aux_ref,
        merged_ref,
        dev_ref,
        ga_out,
        gm_out,
        part_out,
        gout_out,
        share_out,
        load_out,
        low_sc,
        acc_sc,
        state_sc,
    ) = refs[REL:]
    step = pl.program_id(0)
    last = pl.num_programs(0) - 1
    block = last - step
    rank = rank_ref[0]
    rows = q_ref.shape[0]
    scal = 2 * heads * DH
    for k in range(REL):

        @pl.when((rank ^ k) == block)
        def _():
            low_sc[...] = lows[k][...]

    @pl.when(step == 0)
    def _():
        state_sc[...] = jnp.zeros_like(state_sc)
        acc_sc[...] = jnp.zeros_like(acc_sc)

    low = low_sc[...]
    width = share_out.shape[1]
    share_out[...] = low_sc[:, pl.ds(pl.multiple_of(rank * width, width), width)]
    grad_merged = mm(low, w_ref[...], NT)
    ga_out[...] = grad_merged.astype(BF16)
    acc_sc[...] += mm(merged_ref[...], low, TN)
    end = slice(rows - 1, rows)
    for h in range(heads):
        lo, mid = h * DH, (heads + h) * DH
        g = grad_merged[:, lo : lo + DH]
        normed = normed_ref[:, lo : lo + DH]
        scale = scale_ref[:, h : h + 1]
        grad = scale * (g - normed * jnp.mean(g * normed, -1, keepdims=True))
        gm_out[:, lo : lo + DH] = grad.astype(BF16)
        query = q_ref[:, lo : lo + DH]
        keep = aux_ref[:, h : h + 1]
        cross = aux_ref[:, heads + h : heads + h + 1]
        carry = aux_ref[:, 2 * heads + h : 2 * heads + h + 1]
        mem_part = mm((keep * grad).astype(BF16), query, TN)
        mom_part = mm((cross * grad).astype(BF16), query, TN)
        part_out[0, lo : lo + DH] = mem_part
        part_out[0, mid : mid + DH] = mom_part
        memory, momentum = state_sc[lo : lo + DH], state_sc[mid : mid + DH]
        state_sc[lo : lo + DH] = keep[end] * memory + mem_part
        state_sc[mid : mid + DH] = cross[end] * memory + carry[end] * momentum + mom_part

    @pl.when(step == last)
    def _():
        gout_out[...] = acc_sc[...].astype(BF16)
        state_sc[scal : scal + 8] = dev_ref[scal : scal + 8]
        pack_load(load_out, state_sc[...], scal)


def turn(rank, lows, weight, qkv, normed, scales, aux, merged, dev, heads):
    total = qkv.shape[0]
    count = total // MBLK
    local, model = weight.shape
    width = model // REL
    scal = 2 * local
    at = lambda b, *_: (count - 1 - b, 0)
    return call(
        functools.partial(turn_kernel, heads=heads),
        (count,),
        [whole(lows[0].shape)] * REL
        + [
            whole(weight.shape),
            pl.BlockSpec((MBLK, local), at),
            pl.BlockSpec((MBLK, local), at),
            pl.BlockSpec((MBLK, DH), at),
            pl.BlockSpec((MBLK, DH), at),
            pl.BlockSpec((MBLK, local), at),
            whole(dev.shape),
        ],
        [
            pl.BlockSpec((MBLK, local), at),
            pl.BlockSpec((MBLK, local), at),
            pl.BlockSpec((1, scal, DH), lambda b, *_: (count - 1 - b, 0, 0)),
            whole((local, model)),
            pl.BlockSpec((MBLK, width), at),
            whole((scal + 16, DH)),
        ],
        [
            sds((total, local), BF16),
            sds((total, local), BF16),
            sds((count, scal, DH), F32),
            sds((local, model), BF16),
            sds((total, width), BF16),
            sds((scal + 16, DH), BF16),
        ],
        [
            pltpu.VMEM((MBLK, model), BF16),
            pltpu.VMEM((local, model), F32),
            pltpu.VMEM((scal + 8, DH), F32),
        ],
        flops=1.5e9,
        moved=8e6,
        prefetch=1,
    )(rank, *lows, weight, qkv, normed, scales, aux, merged, dev)


def settle_kernel(qkv_ref, *refs, heads):
    atts = refs[: 3 * heads]
    mems = refs[3 * heads : 6 * heads]
    (
        gm_ref,
        aux_ref,
        low_ref,
        part_ref,
        state_ref,
        proj_ref,
        halo_ref,
        conv_ref,
        starts_ref,
        gp_out,
        tail_out,
        head_out,
        gconv_out,
        state_sc,
        mix_sc,
        ext_sc,
        proj_sc,
    ) = refs[6 * heads :]
    step = pl.program_id(0)
    last = pl.num_programs(0) - 1
    block = last - step
    rows = qkv_ref.shape[0]
    local = heads * DH
    base = block * rows

    @pl.when(step == 0)
    def _():
        state_sc[...] = state_ref[0 : state_sc.shape[0]]
        ext_sc[0:8] = jnp.zeros((8, 3 * local), F32)
        gconv_out[...] = jnp.zeros_like(gconv_out)

    end = slice(rows - 1, rows)
    for h in range(heads):
        lo, mid = h * DH, (heads + h) * DH
        memory, momentum = state_sc[lo : lo + DH], state_sc[mid : mid + DH]
        memory_low, momentum_low = memory.astype(BF16), momentum.astype(BF16)
        keep = aux_ref[:, h : h + 1]
        cross = aux_ref[:, heads + h : heads + h + 1]
        carry = aux_ref[:, 2 * heads + h : 2 * heads + h + 1]
        end_kernel = aux_ref[:, 3 * heads + h : 3 * heads + h + 1]
        end_carry = aux_ref[:, 4 * heads + h : 4 * heads + h + 1]
        keys = qkv_ref[:, local + lo : local + lo + DH]
        values = qkv_ref[:, 2 * local + lo : 2 * local + lo + DH]
        gmem = gm_ref[:, lo : lo + DH]
        dq = keep * mm(gmem, low_ref[0, lo : lo + DH]) + cross * mm(
            gmem, low_ref[0, mid : mid + DH]
        )
        dk = end_kernel * mm(values, memory_low) + end_carry * mm(values, momentum_low)
        dv = end_kernel * mm(keys, memory_low, NT) + end_carry * mm(keys, momentum_low, NT)
        for c, extra in enumerate((dq, dk, dv)):
            mix_sc[:, c * local + lo : c * local + lo + DH] = (
                atts[c * heads + h][...] + mems[c * heads + h][...] + extra
            )
        state_sc[lo : lo + DH] = keep[end] * memory + part_ref[0, lo : lo + DH]
        state_sc[mid : mid + DH] = (
            cross[end] * memory + carry[end] * momentum + part_ref[0, mid : mid + DH]
        )
    before = proj_ref[pl.ds(pl.multiple_of(jnp.maximum(base - 16, 0), 16), 16)].astype(F32)[8:16]
    proj_sc[0:8] = jnp.where(block == 0, halo_ref[...], before)
    proj_sc[8 : 8 + rows] = proj_ref[pl.ds(pl.multiple_of(base, rows), rows)].astype(F32)
    ext_sc[rows : rows + 8] = ext_sc[0:8]
    ext_sc[0:rows] = jnp.zeros((rows, 3 * local), F32)
    place = base + iota((rows, 1), 0)
    starts = starts_ref[...]
    for j in range(KW):
        tap = mix_sc[...] * (place - j >= starts).astype(F32)
        ext_sc[8 - j : 8 - j + rows] += conv_ref[j : j + 1] * tap
        gconv_out[j : j + 1] += jnp.sum(tap * proj_sc[8 - j : 8 - j + rows], 0, keepdims=True)
    gp_out[...] = ext_sc[8 : 8 + rows].astype(BF16)

    @pl.when(step == 0)
    def _():
        tail_out[...] = ext_sc[rows - 8 : rows + 8]

    @pl.when(step == last)
    def _():
        head_out[...] = ext_sc[0:8]


def settle(qkv, att_grads, mem_grads, gm, aux, lows, parts, state, proj, halo, conv, starts, heads):
    total = qkv.shape[0]
    count = total // MBLK
    local = heads * DH
    scal = 2 * local
    at = lambda b, *_: (count - 1 - b, 0)
    by_block = pl.BlockSpec((1, scal, DH), lambda b, *_: (count - 1 - b, 0, 0))
    return call(
        functools.partial(settle_kernel, heads=heads),
        (count,),
        [pl.BlockSpec((MBLK, 3 * local), at)]
        + [pl.BlockSpec((MBLK, DH), at)] * (6 * heads)
        + [
            pl.BlockSpec((MBLK, local), at),
            pl.BlockSpec((MBLK, DH), at),
            by_block,
            by_block,
            whole(state.shape),
            whole(proj.shape),
            whole(halo.shape),
            whole(conv.shape),
            pl.BlockSpec((MBLK, 1), at),
        ],
        [
            pl.BlockSpec((MBLK, 3 * local), at),
            whole((16, 3 * local)),
            whole((8, 3 * local)),
            whole((8, 3 * local)),
        ],
        [
            sds((total, 3 * local), BF16),
            sds((16, 3 * local), F32),
            sds((8, 3 * local), F32),
            sds((8, 3 * local), F32),
        ],
        [
            pltpu.VMEM((scal, DH), F32),
            pltpu.VMEM((MBLK, 3 * local), F32),
            pltpu.VMEM((MBLK + 8, 3 * local), F32),
            pltpu.VMEM((MBLK + 8, 3 * local), F32),
        ],
        flops=6e8,
        moved=14e6,
    )(qkv, *att_grads, *mem_grads, gm, aux, lows, parts, state, proj, halo, conv, starts)


def back_kernel(rank_ref, gp_ref, w_ref, x_ref, scale_ref, gain_ref, *outs):
    send_out, far_out, keep_out, dgain_out, grad_sc = outs
    rank = rank_ref[0]
    width = keep_out.shape[1]
    local = w_ref.shape[2]

    @pl.when(pl.program_id(0) == 0)
    def _():
        dgain_out[...] = jnp.zeros_like(dgain_out)

    grad = mm(gp_ref[:, 0:local], w_ref[0], NT)
    for c in range(1, 3):
        grad = grad + mm(gp_ref[:, c * local : (c + 1) * local], w_ref[c], NT)
    scale = scale_ref[...]
    normed = x_ref[...].astype(F32) * scale
    dgain_out[...] += jnp.broadcast_to(jnp.sum(grad * normed, 0, keepdims=True), dgain_out.shape)
    g = grad * gain_ref[8:9]
    grad_sc[...] = (scale * (g - normed * jnp.mean(g * normed, -1, keepdims=True))).astype(BF16)
    spans = [pl.ds(pl.multiple_of((rank ^ k) * width, width), width) for k in range(REL)]
    keep_out[...] = grad_sc[:, spans[0]]
    send_out[0] = grad_sc[:, spans[1]]
    far_out[...] = grad_sc[:, spans[2]]
    send_out[1] = grad_sc[:, spans[3]]


def back(rank, gp, weight, x, scale, gains):
    total, model = x.shape
    width = model // REL
    at = lambda b, *_: (b, 0)
    return call(
        back_kernel,
        (total // MBLK,),
        [
            pl.BlockSpec((MBLK, gp.shape[1]), at),
            whole(weight.shape),
            pl.BlockSpec((MBLK, model), at),
            pl.BlockSpec((MBLK, 1), at),
            whole(gains.shape),
        ],
        [
            pl.BlockSpec((2, MBLK, width), lambda b, *_: (0, b, 0)),
            pl.BlockSpec((MBLK, width), at),
            pl.BlockSpec((MBLK, width), at),
            whole((8, model)),
        ],
        [
            sds((2, total, width), BF16),
            sds((total, width), BF16),
            sds((total, width), BF16),
            sds((8, model), F32),
        ],
        [pltpu.VMEM((MBLK, model), BF16)],
        flops=1.7e9,
        moved=8e6,
        prefetch=1,
    )(rank, gp, weight, x, scale, gains)


def scatter_rel(send, far, keep):
    got = swap(send, "head", 1)
    got_far = swap(far + got[1], "head", 2)
    return keep.astype(F32) + got[0].astype(F32) + got_far.astype(F32)


def per_device(
    inputs,
    cotangent,
    norm_gain,
    qkv_weight,
    conv_kernel,
    persistent,
    out_weight,
    ffn_gain,
    gate_up,
    down_weight,
    memory_decay,
    momentum_decay,
    doc_start,
):
    total, width = inputs.shape
    local = qkv_weight.shape[2]
    heads = local // DH
    model = width * REL
    rank = lax.axis_index("head").astype(jnp.int32).reshape(1)
    starts = (doc_start - lax.axis_index("seq") * total).reshape(total, 1)
    decays = jnp.concatenate(
        [memory_decay.T, momentum_decay.T, jnp.ones((8 - 2 * heads, total), F32)], 0
    )
    conv = conv_kernel.reshape(KW, 3 * local)

    halo_rows = shifted(inputs[total - 8 :], "seq", 1)
    small = jnp.concatenate(
        [halo_rows, norm_gain[None], ffn_gain[None], jnp.zeros((6, width), BF16)], 0
    )
    blocks = gather_rel(inputs)
    smalls = gather_rel(small)
    cots = gather_rel(cotangent)
    out_weights = gather_rel(out_weight)

    (
        x,
        hidden_one,
        scale_one,
        proj,
        qkv,
        kmat,
        aux,
        parts,
        halo,
        gains,
        dev_state,
        load,
    ) = front(rank, blocks, smalls, qkv_weight, conv, starts, decays, heads)

    atts, ratios, intras, probs, fixps = zip(
        *[attend(qkv, persistent, starts, kmat, h, heads) for h in range(heads)]
    )
    prefix = entering(load, heads, False)
    merged, normed_mem, mem_scales, state_lows = merge(
        qkv, atts, intras, aux, parts, prefix, heads
    )
    merged_rel = gather_rel(merged)
    hidden_two, normed_two, scale_two, middle_share = middle(
        rank, merged_rel, out_weights, x, gains
    )
    act, grad_gate, grad_up, cot, send, far, keep, fsend, ffar, fkeep = ffn(
        rank, hidden_two, cots, gate_up, down_weight
    )
    near = swap(send, "head", 1)
    far_sum = swap(far + near[1:2], "head", 2)
    low_own, dgain_two = bend(rank, keep, near, far_sum, cot, normed_two, scale_two, gains)
    lows = gather_rel(low_own)

    output = (middle_share + scatter_rel(fsend, ffar, fkeep)).astype(BF16)
    grad_down = lax.dot_general(act, cot, TN, preferred_element_type=F32).astype(BF16)
    grad_gate_full = lax.dot_general(
        hidden_two, grad_gate, TN, preferred_element_type=F32
    ).astype(BF16)
    grad_up_full = lax.dot_general(hidden_two, grad_up, TN, preferred_element_type=F32).astype(
        BF16
    )

    grad_att, grad_mem, mem_parts, grad_out, low_share, back_load = turn(
        rank, lows, out_weight, qkv, normed_mem, mem_scales, aux, merged, dev_state, heads
    )
    pieces = [
        attend_back(
            qkv, persistent, probs[h], fixps[h], ratios[h], grad_att, grad_mem, kmat, h, heads
        )
        for h in range(heads)
    ]
    suffix = entering(back_load, heads, True)
    att_grads = [pieces[h][c] for c in range(3) for h in range(heads)]
    mem_grads = [pieces[h][4 + c] for c in range(3) for h in range(heads)]
    gp, tail, head_rows, gconv = settle(
        qkv,
        att_grads,
        mem_grads,
        grad_mem,
        aux,
        state_lows,
        mem_parts,
        suffix,
        proj,
        halo,
        conv,
        starts,
        heads,
    )
    returned = shifted(head_rows, "seq", -1)
    fixed_tail = jnp.concatenate([tail[:8], tail[8:] + returned], 0).astype(BF16)
    gp = lax.dynamic_update_slice(gp, fixed_tail, (total - 16, 0))
    bsend, bfar, bkeep, dgain_one = back(rank, gp, qkv_weight, x, scale_one, gains)
    grad_qkv = jnp.stack(
        [
            lax.dot_general(
                hidden_one,
                gp[:, c * local : (c + 1) * local],
                TN,
                preferred_element_type=F32,
            ).astype(BF16)
            for c in range(3)
        ],
        0,
    )
    input_grad = scatter_rel(bsend, bfar, bkeep) + low_share.astype(F32)

    grad_fixed = jnp.concatenate([p[3] for p in pieces], -1)
    gain_sums = sum_over(jnp.stack([dgain_one[0], dgain_two[0]], 0), "head")
    gain_own = lax.dynamic_slice_in_dim(
        gain_sums, lax.axis_index("head") * width, width, 1
    )
    fixed_count = persistent.shape[1]
    little = jnp.concatenate(
        [
            gain_own,
            gconv[:KW].reshape(3 * KW, local),
            grad_fixed.reshape(2 * fixed_count, local),
        ],
        0,
    )
    little = sum_over(little, "seq")
    scatter = lambda g, dim: lax.psum_scatter(
        g, "seq", scatter_dimension=dim, tiled=True
    ).astype(F32)
    return (
        output,
        input_grad,
        little[0],
        scatter(grad_qkv, 1),
        little[2 : 2 + 3 * KW].reshape(KW, 3, local),
        little[2 + 3 * KW :].reshape(2, fixed_count, local),
        scatter(grad_out, 1),
        little[1],
        scatter(jnp.stack([grad_gate_full, grad_up_full], 0), 1),
        scatter(grad_down, 1),
    )


def solution(mesh):
    placed = (
        P("seq", "head"),
        P("seq", "head"),
        P("head"),
        P(None, None, "head"),
        P(None, None, "head"),
        P(None, None, "head"),
        P("head", None),
        P("head"),
        P(None, None, "head"),
        P("head", None),
        P("seq", "head"),
        P("seq", "head"),
        P("seq"),
    )
    return jax.shard_map(
        per_device,
        mesh=mesh,
        in_specs=placed,
        out_specs=(
            P("seq", "head"),
            P("seq", "head"),
            P("head"),
            P(None, "seq", "head"),
            P(None, None, "head"),
            P(None, None, "head"),
            P("head", "seq"),
            P("head"),
            P(None, "seq", "head"),
            P("head", "seq"),
        ),
        check_vma=False,
    )
```

```python
import functools

import jax
import jax.numpy as jnp
from jax import lax
from jax.experimental import pallas as pl
from jax.experimental.pallas import tpu as pltpu
from jax.sharding import PartitionSpec as P

DH = 128
KW = 4
SEG = 1024
MBLK = 256
EPSILON = 1e-06
MEMORY_FLOOR = 64.0
MASKED = -1e30
F32 = jnp.float32
BF16 = jnp.bfloat16
NN = (((1,), (0,)), ((), ()))
NT = (((1,), (1,)), ((), ()))
TN = (((0,), (0,)), ((), ()))
REL = 4


def mm(a, b, dims=NN):
    return lax.dot_general(a, b, dims, preferred_element_type=F32)


def exact(a, b, dims=NN):
    return lax.dot_general(
        a, b, dims, precision=lax.Precision.HIGHEST, preferred_element_type=F32
    )


def call(
    kernel, grid, in_specs, out_specs, out_shape, scratch=(), flops=0, moved=0, prefetch=0, after=()
):
    taken = prefetch + len(in_specs)
    waits = len(after)

    def body(*refs):
        kernel(*refs[:taken], *refs[taken + waits :])

    spec = pltpu.PrefetchScalarGridSpec(
        num_scalar_prefetch=prefetch,
        grid=grid,
        in_specs=list(in_specs) + [pl.BlockSpec(memory_space=pl.ANY)] * waits,
        out_specs=out_specs,
        scratch_shapes=list(scratch),
    )
    made = pl.pallas_call(
        body,
        grid_spec=spec,
        out_shape=out_shape,
        compiler_params=pltpu.CompilerParams(vmem_limit_bytes=24 * 2**20),
        cost_estimate=pl.CostEstimate(
            flops=int(flops), bytes_accessed=int(moved), transcendentals=0
        ),
    )
    return lambda *operands: made(*operands, *after)


def whole(shape):
    return pl.BlockSpec(shape, lambda *_: (0,) * len(shape))


def sds(shape, dtype):
    return jax.ShapeDtypeStruct(shape, dtype)


def iota(shape, dim):
    return lax.broadcasted_iota(jnp.int32, shape, dim)


def swap(x, axis, bit):
    count = lax.axis_size(axis)
    return lax.ppermute(x, axis, [(i, i ^ bit) for i in range(count)])


def shifted(x, axis, by):
    count = lax.axis_size(axis)
    return lax.ppermute(x, axis, [(i, i + by) for i in range(count) if 0 <= i + by < count])


def gather_rel(x):
    far = swap(x, "head", 2)
    near = swap(x, "head", 1)
    return [x, near, far, swap(far, "head", 1)]


def sum_over(x, axis):
    bit = 1
    while bit < lax.axis_size(axis):
        x = x + swap(x, axis, bit)
        bit *= 2
    return x


def front_kernel(rank_ref, *refs, heads):
    blocks, smalls = refs[:REL], refs[REL : 2 * REL]
    (
        w_ref,
        conv_ref,
        starts_ref,
        decay_ref,
        x_out,
        hid_out,
        scale_out,
        proj_out,
        qkv_out,
        kmat_out,
        aux_out,
        part_out,
        halo_out,
        gain_out,
        state_out,
        load_out,
        small_sc,
        proj_sc,
        state_sc,
    ) = refs[2 * REL :]
    b = pl.program_id(0)
    rank = rank_ref[0]
    rows, width = blocks[0].shape
    local = heads * DH
    spans = [pl.ds(pl.multiple_of((rank ^ k) * width, width), width) for k in range(REL)]
    for k in range(REL):
        x_out[:, spans[k]] = blocks[k][...]
    scal = 2 * heads * DH

    @pl.when(b == 0)
    def _():
        for k in range(REL):
            small_sc[:, spans[k]] = smalls[k][...]
        small = small_sc[...].astype(F32)
        gain_out[...] = small
        scale = lax.rsqrt(jnp.mean(small * small, -1, keepdims=True) + EPSILON)
        hidden = (small * scale * small[8:9]).astype(BF16)
        for c in range(3):
            proj_sc[0:8, c * local : (c + 1) * local] = mm(hidden, w_ref[c])[0:8]
        halo_out[...] = proj_sc[0:8]
        state_sc[0:scal] = jnp.zeros((scal, DH), F32)
        row = iota((8, DH), 0)
        state_sc[scal : scal + 8] = jnp.where(
            (row < heads) | ((row >= 2 * heads) & (row < 3 * heads)), 1.0, 0.0
        ).astype(F32)

    gain = gain_out[8:9]
    x = x_out[...].astype(F32)
    scale = lax.rsqrt(jnp.mean(x * x, -1, keepdims=True) + EPSILON)
    hidden = (x * scale * gain).astype(BF16)
    hid_out[...] = hidden
    scale_out[...] = scale
    for c in range(3):
        proj_sc[8 : 8 + rows, c * local : (c + 1) * local] = mm(hidden, w_ref[c])
    base = b * rows
    place = base + iota((rows, 1), 0)
    starts = starts_ref[...]
    mixed = jnp.zeros((rows, 3 * local), F32)
    for j in range(KW):
        inside = (place - j >= starts).astype(F32)
        mixed = mixed + conv_ref[j : j + 1] * proj_sc[8 - j : 8 - j + rows] * inside
    rounded = mixed.astype(BF16)
    qkv_out[...] = rounded
    proj_out[...] = proj_sc[8 : 8 + rows].astype(BF16)
    proj_sc[0:8] = proj_sc[rows : rows + 8]

    logs = jnp.log(decay_ref[...])
    below = iota((rows, rows), 0)
    right = iota((rows, rows), 1)
    rows_sum = exact(logs, (below <= right).astype(F32))
    cols_sum = exact((right <= below).astype(F32), logs, NT)
    linked = (right <= below) & (base + right >= starts)
    fresh = starts < base
    last_start = starts[rows - 1 : rows]
    reaches_end = place >= last_start
    last_row = (iota((rows, DH), 0) == rows - 1).astype(BF16)
    lane = iota((rows, DH), 1)
    aux = jnp.zeros((rows, DH), F32)
    for h in range(heads):
        keep_col, keep_row = cols_sum[:, h : h + 1], rows_sum[h : h + 1]
        carry_col = cols_sum[:, heads + h : heads + h + 1]
        carry_row = rows_sum[heads + h : heads + h + 1]
        keep_mat = jnp.where(linked, jnp.exp(jnp.minimum(keep_col - keep_row, 0.0)), 0.0)
        carry_mat = jnp.where(linked, jnp.exp(jnp.minimum(carry_col - carry_row, 0.0)), 0.0)
        keep_low = keep_mat.astype(BF16)
        kernel = mm(keep_low, carry_mat.astype(BF16)).astype(BF16)
        kmat_out[h, 0] = kernel
        keep_weight = jnp.where(fresh, jnp.exp(keep_col), 0.0)
        carried = jnp.where(fresh, jnp.exp(carry_col), 0.0)
        cross = mm(keep_low, jnp.broadcast_to(carried, (rows, DH)).astype(BF16))
        end_kernel = mm(kernel, last_row, TN)
        end_carry = jnp.where(
            reaches_end, jnp.exp(jnp.minimum(carry_col[rows - 1 : rows] - carry_col, 0.0)), 0.0
        )
        for slot, column in enumerate((keep_weight, cross, carried, end_kernel, end_carry)):
            aux = jnp.where(lane == slot * heads + h, column, aux)
        keys = rounded[:, local + h * DH : local + (h + 1) * DH]
        values = rounded[:, 2 * local + h * DH : 2 * local + (h + 1) * DH].astype(F32)
        mem_part = mm((values * end_kernel).astype(BF16), keys, TN)
        mom_part = mm((values * end_carry).astype(BF16), keys, TN)
        lo, mid = h * DH, (heads + h) * DH
        part_out[0, lo : lo + DH] = mem_part
        part_out[0, mid : mid + DH] = mom_part
        keep_end = jnp.broadcast_to(keep_weight[rows - 1 : rows], (1, DH))
        cross_end = cross[rows - 1 : rows]
        carry_end = jnp.broadcast_to(carried[rows - 1 : rows], (1, DH))
        memory, momentum = state_sc[lo : lo + DH], state_sc[mid : mid + DH]
        state_sc[lo : lo + DH] = keep_end * memory + cross_end * momentum + mem_part
        state_sc[mid : mid + DH] = carry_end * momentum + mom_part
        keep_at, cross_at, carry_at = scal + h, scal + heads + h, scal + 2 * heads + h
        keep_dev = state_sc[keep_at : keep_at + 1]
        cross_dev = state_sc[cross_at : cross_at + 1]
        carry_dev = state_sc[carry_at : carry_at + 1]
        state_sc[keep_at : keep_at + 1] = keep_end * keep_dev
        state_sc[cross_at : cross_at + 1] = keep_end * cross_dev + cross_end * carry_dev
        state_sc[carry_at : carry_at + 1] = carry_end * carry_dev
    aux_out[...] = aux

    @pl.when(b == pl.num_programs(0) - 1)
    def _():
        state_out[...] = state_sc[...]
        pack_load(load_out, state_sc[...], scal)


def pack_load(load_out, state, scal):
    load_out[0:scal] = state[0:scal].astype(BF16)
    tail = state[scal : scal + 8]
    high = tail.astype(BF16).astype(F32)
    load_out[scal : scal + 16] = jnp.concatenate([high, tail - high], 0).astype(BF16)


def unpack(ref, scal):
    if ref.dtype == F32:
        return ref[0:scal], ref[scal : scal + 8]
    tail = ref[scal : scal + 16].astype(F32)
    return ref[0:scal].astype(F32), tail[0:8] + tail[8:16]


def front(rank, blocks, smalls, weight, conv, starts, decays, heads):
    total, width = blocks[0].shape
    model = width * REL
    local = heads * DH
    count = total // MBLK
    scal = 2 * heads * DH
    at = lambda b, *_: (b, 0)
    return call(
        functools.partial(front_kernel, heads=heads),
        (count,),
        [pl.BlockSpec((MBLK, width), at)] * REL
        + [whole(smalls[0].shape)] * REL
        + [
            whole(weight.shape),
            whole(conv.shape),
            pl.BlockSpec((MBLK, 1), at),
            pl.BlockSpec((8, MBLK), lambda b, *_: (0, b)),
        ],
        [
            pl.BlockSpec((MBLK, model), at),
            pl.BlockSpec((MBLK, model), at),
            pl.BlockSpec((MBLK, 1), at),
            pl.BlockSpec((MBLK, 3 * local), at),
            pl.BlockSpec((MBLK, 3 * local), at),
            pl.BlockSpec((heads, 1, MBLK, MBLK), lambda b, *_: (0, b, 0, 0)),
            pl.BlockSpec((MBLK, DH), at),
            pl.BlockSpec((1, scal, DH), lambda b, *_: (b, 0, 0)),
            whole((8, 3 * local)),
            whole((16, model)),
            whole((scal + 8, DH)),
            whole((scal + 16, DH)),
        ],
        [
            sds((total, model), BF16),
            sds((total, model), BF16),
            sds((total, 1), F32),
            sds((total, 3 * local), BF16),
            sds((total, 3 * local), BF16),
            sds((heads, count, MBLK, MBLK), BF16),
            sds((total, DH), F32),
            sds((count, scal, DH), F32),
            sds((8, 3 * local), F32),
            sds((16, model), F32),
            sds((scal + 8, DH), F32),
            sds((scal + 16, DH), BF16),
        ],
        [
            pltpu.VMEM((16, model), BF16),
            pltpu.VMEM((MBLK + 8, 3 * local), F32),
            pltpu.VMEM((scal + 8, DH), F32),
        ],
        flops=2.2e9,
        moved=12e6,
        prefetch=1,
    )(rank, *blocks, *smalls, weight, conv, starts, decays)


def join_kernel(first_ref, second_ref, state_out, load_out, *, heads, backward):
    scal = 2 * heads * DH
    first, first_tail = unpack(first_ref, scal)
    second, second_tail = unpack(second_ref, scal)
    tail = []
    for h in range(heads):
        lo, mid = h * DH, (heads + h) * DH
        keep_one, keep_two = first_tail[h : h + 1], second_tail[h : h + 1]
        cross_one, cross_two = (
            first_tail[heads + h : heads + h + 1],
            second_tail[heads + h : heads + h + 1],
        )
        carry_one, carry_two = (
            first_tail[2 * heads + h : 2 * heads + h + 1],
            second_tail[2 * heads + h : 2 * heads + h + 1],
        )
        mem_one, mom_one = first[lo : lo + DH], first[mid : mid + DH]
        mem_two, mom_two = second[lo : lo + DH], second[mid : mid + DH]
        if backward:
            state_out[lo : lo + DH] = mem_two + keep_two * mem_one
            state_out[mid : mid + DH] = mom_two + cross_two * mem_one + carry_two * mom_one
            cross = cross_two * keep_one + carry_two * cross_one
        else:
            state_out[lo : lo + DH] = keep_two * mem_one + cross_two * mom_one + mem_two
            state_out[mid : mid + DH] = carry_two * mom_one + mom_two
            cross = keep_two * cross_one + cross_two * carry_one
        state_out[scal + h : scal + h + 1] = keep_two * keep_one
        state_out[scal + heads + h : scal + heads + h + 1] = cross
        state_out[scal + 2 * heads + h : scal + 2 * heads + h + 1] = carry_two * carry_one
    for spare in range(3 * heads, 8):
        state_out[scal + spare : scal + spare + 1] = jnp.zeros((1, DH), F32)
    pack_load(load_out, state_out[...], scal)


def join(first, second, heads, backward, after=()):
    scal = 2 * heads * DH
    return call(
        functools.partial(join_kernel, heads=heads, backward=backward),
        (1,),
        [whole(first.shape), whole(second.shape)],
        [whole((scal + 8, DH)), whole((scal + 16, DH))],
        [sds((scal + 8, DH), F32), sds((scal + 16, DH), BF16)],
        flops=1e6,
        moved=1e6,
        after=after,
    )(first, second)


def entering(load, heads, backward, beside):
    count = lax.axis_size("seq")
    sign = -1 if backward else 1
    one = shifted(load, "seq", sign)
    two = shifted(load, "seq", 2 * sign)
    covered = 2
    lap = 0
    state, load = join(two, one, heads, backward, beside[0])
    while covered < count - 1:
        lap += 1
        after = beside[lap] if lap < len(beside) else ()
        state, load = join(shifted(load, "seq", covered * sign), state, heads, backward, after)
        covered *= 2
    return state


def attend_kernel(q_ref, k_ref, v_ref, fix_ref, starts_ref, kmat_ref, *outs):
    att_out, ratio_out, intra_out, prob_out, fixp_out = outs
    total = q_ref.shape[0]
    fixed_keys, fixed_values = fix_ref[0], fix_ref[1]
    factor = DH ** (-0.5)
    for i in range(total // MBLK):
        span = slice(i * MBLK, (i + 1) * MBLK)
        seen = (i + 1) * MBLK
        query = q_ref[span]
        raw = mm(query, k_ref[0:seen], NT)
        fixed = mm(query, fixed_keys, NT)
        key_at = iota((MBLK, seen), 1)
        ok = (key_at >= starts_ref[span]) & (key_at <= i * MBLK + iota((MBLK, seen), 0))
        raw = jnp.where(ok, raw, MASKED)
        top = jnp.maximum(jnp.max(raw, -1, keepdims=True), jnp.max(fixed, -1, keepdims=True))
        weights = jnp.exp((raw - top) * factor)
        fix_weights = jnp.exp((fixed - top) * factor)
        scale = 1.0 / (
            jnp.sum(weights, -1, keepdims=True) + jnp.sum(fix_weights, -1, keepdims=True)
        )
        low = (weights * scale).astype(BF16)
        fix_low = (fix_weights * scale).astype(BF16)
        prob_out[span, 0:seen] = low
        fixp_out[span] = fix_low
        attended = mm(low, v_ref[0:seen]) + mm(fix_low, fixed_values)
        held = jnp.sum(low.astype(F32), -1, keepdims=True) + jnp.sum(
            fix_low.astype(F32), -1, keepdims=True
        )
        att_out[span] = attended
        ratio_out[span] = attended / held
        near = mm(query, k_ref[span], NT)
        kernel = kmat_ref[0, i].astype(F32)
        intra_out[span] = mm((kernel * near).astype(BF16), v_ref[span])


def attend(qkv, fixed, starts, kmat, head, heads):
    total = qkv.shape[0]
    count = total // MBLK
    fixed_count = fixed.shape[1]
    lanes = lambda c: pl.BlockSpec((total, DH), lambda *_: (0, c * heads + head))
    return call(
        attend_kernel,
        (1,),
        [
            lanes(0),
            lanes(1),
            lanes(2),
            pl.BlockSpec((2, fixed_count, DH), lambda *_: (0, 0, head)),
            whole((total, 1)),
            pl.BlockSpec((1, count, MBLK, MBLK), lambda *_: (head, 0, 0, 0)),
        ],
        [whole((total, DH))] * 3 + [whole((total, total)), whole((total, fixed_count))],
        [sds((total, DH), F32)] * 3
        + [sds((total, total), BF16), sds((total, fixed_count), BF16)],
        flops=1.5e9,
        moved=8e6,
    )(qkv, qkv, qkv, fixed, starts, kmat)


def attend_back_kernel(
    q_ref, k_ref, v_ref, fix_ref, prob_ref, fixp_ref, ratio_ref, grad_ref, gmem_ref, kmat_ref, *outs
):
    dq_out, dk_out, dv_out, dfix_out, dqm_out, dkm_out, dvm_out = outs
    total = q_ref.shape[0]
    fixed_keys, fixed_values = fix_ref[0], fix_ref[1]
    factor = DH ** (-0.5)
    dfix_k = jnp.zeros(fixed_keys.shape, F32)
    dfix_v = jnp.zeros(fixed_keys.shape, F32)
    for i in reversed(range(total // MBLK)):
        span = slice(i * MBLK, (i + 1) * MBLK)
        seen = (i + 1) * MBLK
        query, grad = q_ref[span], grad_ref[span]
        delta = jnp.sum(grad.astype(F32) * ratio_ref[span], -1, keepdims=True)
        low, fix_low = prob_ref[span, 0:seen], fixp_ref[span]
        back = mm(grad, v_ref[0:seen], NT)
        fix_back = mm(grad, fixed_values, NT)
        grad_raw = (low.astype(F32) * (back - delta) * factor).astype(BF16)
        fix_raw = (fix_low.astype(F32) * (fix_back - delta) * factor).astype(BF16)
        dq_out[span] = mm(grad_raw, k_ref[0:seen]) + mm(fix_raw, fixed_keys)
        dk, dv = mm(grad_raw, query, TN), mm(low, grad, TN)
        if seen == total:
            dk_out[...] = dk
            dv_out[...] = dv
        else:
            dk_out[0:seen] += dk
            dv_out[0:seen] += dv
        dfix_k += mm(fix_raw, query, TN)
        dfix_v += mm(fix_low, grad, TN)
        keys, values, gmem = k_ref[span], v_ref[span], gmem_ref[span]
        kernel = kmat_ref[0, i].astype(F32)
        near = (kernel * mm(query, keys, NT)).astype(BF16)
        cross = (kernel * mm(gmem, values, NT)).astype(BF16)
        dqm_out[span] = mm(cross, keys)
        dkm_out[span] = mm(cross, query, TN)
        dvm_out[span] = mm(near, gmem, TN)
    dfix_out[0] = dfix_k
    dfix_out[1] = dfix_v


def attend_back(qkv, fixed, prob, fixp, ratio, grads, gmem, kmat, head, heads):
    total = qkv.shape[0]
    count = total // MBLK
    fixed_count = fixed.shape[1]
    lanes = lambda c: pl.BlockSpec((total, DH), lambda *_: (0, c * heads + head))
    return call(
        attend_back_kernel,
        (1,),
        [
            lanes(0),
            lanes(1),
            lanes(2),
            pl.BlockSpec((2, fixed_count, DH), lambda *_: (0, 0, head)),
            whole((total, total)),
            whole((total, fixed_count)),
            whole((total, DH)),
            lanes(0),
            lanes(0),
            pl.BlockSpec((1, count, MBLK, MBLK), lambda *_: (head, 0, 0, 0)),
        ],
        [whole((total, DH))] * 3 + [whole((2, fixed_count, DH))] + [whole((total, DH))] * 3,
        [sds((total, DH), F32)] * 3
        + [sds((2, fixed_count, DH), F32)]
        + [sds((total, DH), F32)] * 3,
        flops=3e9,
        moved=10e6,
    )(qkv, qkv, qkv, fixed, prob, fixp, ratio, grads, gmem, kmat)


def merge_kernel(q_ref, *refs, heads):
    atts, intras = refs[:heads], refs[heads : 2 * heads]
    aux_ref, part_ref, state_ref, merged_out, normed_out, scale_out, state_low, state_sc = refs[
        2 * heads :
    ]
    rows = q_ref.shape[0]
    lane = iota((rows, DH), 1)
    scales = jnp.zeros((rows, DH), F32)

    @pl.when(pl.program_id(0) == 0)
    def _():
        state_sc[...] = state_ref[0 : state_sc.shape[0]]

    for h in range(heads):
        lo, mid = h * DH, (heads + h) * DH
        memory, momentum = state_sc[lo : lo + DH], state_sc[mid : mid + DH]
        memory_low, momentum_low = memory.astype(BF16), momentum.astype(BF16)
        state_low[0, lo : lo + DH] = memory_low
        state_low[0, mid : mid + DH] = momentum_low
        query = q_ref[:, lo : lo + DH]
        keep = aux_ref[:, h : h + 1]
        cross = aux_ref[:, heads + h : heads + h + 1]
        carry = aux_ref[:, 2 * heads + h : 2 * heads + h + 1]
        out = (
            intras[h][...]
            + keep * mm(query, memory_low, NT)
            + cross * mm(query, momentum_low, NT)
        )
        scale = lax.rsqrt(jnp.mean(out * out, -1, keepdims=True) + MEMORY_FLOOR)
        normed = out * scale
        normed_out[:, lo : lo + DH] = normed
        scales = jnp.where(lane == h, scale, scales)
        merged_out[:, lo : lo + DH] = (atts[h][...] + normed).astype(BF16)
        end = slice(rows - 1, rows)
        state_sc[lo : lo + DH] = (
            keep[end] * memory + cross[end] * momentum + part_ref[0, lo : lo + DH]
        )
        state_sc[mid : mid + DH] = carry[end] * momentum + part_ref[0, mid : mid + DH]
    scale_out[...] = scales


def merge(qkv, atts, intras, aux, parts, state, heads, after):
    total = qkv.shape[0]
    count = total // MBLK
    local = heads * DH
    scal = 2 * local
    at = lambda b, *_: (b, 0)
    by_block = pl.BlockSpec((1, scal, DH), lambda b, *_: (b, 0, 0))
    return call(
        functools.partial(merge_kernel, heads=heads),
        (count,),
        [pl.BlockSpec((MBLK, local), at)]
        + [pl.BlockSpec((MBLK, DH), at)] * (2 * heads + 1)
        + [by_block, whole(state.shape)],
        [
            pl.BlockSpec((MBLK, local), at),
            pl.BlockSpec((MBLK, local), at),
            pl.BlockSpec((MBLK, DH), at),
            by_block,
        ],
        [
            sds((total, local), BF16),
            sds((total, local), F32),
            sds((total, DH), F32),
            sds((count, scal, DH), BF16),
        ],
        [pltpu.VMEM((scal, DH), F32)],
        flops=3e8,
        moved=6e6,
        after=after,
    )(qkv, *atts, *intras, aux, parts, state)


def middle_kernel(rank_ref, *refs):
    merged, weights = refs[:REL], refs[REL : 2 * REL]
    (
        x_ref,
        gain_ref,
        hid_out,
        normed_out,
        scale_out,
        share_out,
        mid_sc,
        merged_sc,
        weight_sc,
    ) = refs[2 * REL :]
    width = share_out.shape[1]
    local = merged[0].shape[1]

    @pl.when(pl.program_id(0) == 0)
    def _():
        for k in range(REL):
            weight_sc[k * local : (k + 1) * local] = weights[k][...]

    for k in range(REL):
        merged_sc[:, k * local : (k + 1) * local] = merged[k][...]
    middle = x_ref[...].astype(F32) + mm(merged_sc[...], weight_sc[...])
    mid_sc[...] = middle
    scale = lax.rsqrt(jnp.mean(middle * middle, -1, keepdims=True) + EPSILON)
    normed = middle * scale
    normed_out[...] = normed.astype(BF16)
    hid_out[...] = (normed * gain_ref[9:10]).astype(BF16)
    scale_out[...] = scale
    share_out[...] = mid_sc[:, pl.ds(pl.multiple_of(rank_ref[0] * width, width), width)]


def middle(rank, merged, weights, x, gains, after):
    total, model = x.shape
    local = merged[0].shape[1]
    width = model // REL
    at = lambda b, *_: (b, 0)
    return call(
        middle_kernel,
        (total // MBLK,),
        [pl.BlockSpec((MBLK, local), at)] * REL
        + [whole(weights[0].shape)] * REL
        + [pl.BlockSpec((MBLK, model), at), whole(gains.shape)],
        [
            pl.BlockSpec((MBLK, model), at),
            pl.BlockSpec((MBLK, model), at),
            pl.BlockSpec((MBLK, 1), at),
            pl.BlockSpec((MBLK, width), at),
        ],
        [
            sds((total, model), BF16),
            sds((total, model), BF16),
            sds((total, 1), F32),
            sds((total, width), F32),
        ],
        [
            pltpu.VMEM((MBLK, model), F32),
            pltpu.VMEM((MBLK, REL * local), BF16),
            pltpu.VMEM((REL * local, model), BF16),
        ],
        flops=2.2e9,
        moved=10e6,
        prefetch=1,
        after=after,
    )(rank, *merged, *weights, x, gains)


def recall_kernel(rank_ref, *refs):
    cots = refs[:REL]
    down_ref, act_out, cot_out = refs[REL:]
    rank = rank_ref[0]
    width = cots[0].shape[1]
    for k in range(REL):
        span = pl.ds(pl.multiple_of((rank ^ k) * width, width), width)
        cot_out[:, span] = cots[k][...]
    act_out[...] = mm(cot_out[...], down_ref[...], NT).astype(BF16)


def recall(rank, cots, down, after):
    total, width = cots[0].shape
    units, model = down.shape
    at = lambda b, *_: (b, 0)
    return call(
        recall_kernel,
        (total // MBLK,),
        [pl.BlockSpec((MBLK, width), at)] * REL + [whole(down.shape)],
        [pl.BlockSpec((MBLK, units), at), pl.BlockSpec((MBLK, model), at)],
        [sds((total, units), BF16), sds((total, model), BF16)],
        flops=1.5e9,
        moved=7e6,
        prefetch=1,
        after=after,
    )(rank, *cots, down)


def ffn_kernel(rank_ref, hid_ref, grad_ref, gate_ref, *outs):
    act_out, gg_out, gu_out, send_out, far_out, keep_out = outs
    step = pl.program_id(0)
    hidden = hid_ref[...]
    gate = mm(hidden, gate_ref[0], NT)
    up = mm(hidden, gate_ref[1], NT)
    grad_act = grad_ref[...].astype(F32)
    sig = jax.nn.sigmoid(gate)
    silu = gate * sig
    act_out[...] = (silu * up).astype(BF16)
    grad_gate = (grad_act * up * (sig * (1.0 + gate * (1.0 - sig)))).astype(BF16)
    grad_up = (grad_act * silu).astype(BF16)
    gg_out[...] = grad_gate
    gu_out[...] = grad_up
    back = (mm(grad_gate, gate_ref[0]) + mm(grad_up, gate_ref[1])).astype(BF16)

    @pl.when(step < 2)
    def _():
        send_out[0] = back

    @pl.when(step == 2)
    def _():
        far_out[0] = back

    @pl.when(step == 3)
    def _():
        keep_out[0] = back


def ffn(rank, hidden, grad_act, gate_up):
    total, model = hidden.shape
    units = grad_act.shape[1]
    rows = total // REL

    def tok(s, rank_ref):
        g = (s + 1) & 3
        return (rank_ref[0] ^ (g ^ (g >> 1)), 0)

    return call(
        ffn_kernel,
        (REL,),
        [
            pl.BlockSpec((rows, model), tok),
            pl.BlockSpec((rows, units), tok),
            whole(gate_up.shape),
        ],
        [pl.BlockSpec((rows, units), tok)] * 3
        + [
            pl.BlockSpec((1, rows, model), lambda s, r: (jnp.minimum(s, 1), 0, 0)),
            whole((1, rows, model)),
            whole((1, rows, model)),
        ],
        [sds((total, units), BF16)] * 3
        + [
            sds((2, rows, model), BF16),
            sds((1, rows, model), BF16),
            sds((1, rows, model), BF16),
        ],
        flops=6e9,
        moved=16e6,
        prefetch=1,
    )(rank, hidden, grad_act, gate_up)


def answer_kernel(rank_ref, act_ref, down_ref, send_out, far_out, keep_out):
    rank = rank_ref[0]
    width = keep_out.shape[1]
    spans = [pl.ds(pl.multiple_of((rank ^ k) * width, width), width) for k in range(REL)]
    act = act_ref[...]
    keep_out[...] = mm(act, down_ref[:, spans[0]]).astype(BF16)
    send_out[0] = mm(act, down_ref[:, spans[1]]).astype(BF16)
    far_out[...] = mm(act, down_ref[:, spans[2]]).astype(BF16)
    send_out[1] = mm(act, down_ref[:, spans[3]]).astype(BF16)


def answer(rank, act, down):
    total, units = act.shape
    width = down.shape[1] // REL
    at = lambda b, *_: (b, 0)
    return call(
        answer_kernel,
        (total // MBLK,),
        [pl.BlockSpec((MBLK, units), at), whole(down.shape)],
        [
            pl.BlockSpec((2, MBLK, width), lambda b, *_: (0, b, 0)),
            pl.BlockSpec((MBLK, width), at),
            pl.BlockSpec((MBLK, width), at),
        ],
        [sds((2, total, width), BF16), sds((total, width), BF16), sds((total, width), BF16)],
        flops=1.5e9,
        moved=5e6,
        prefetch=1,
    )(rank, act, down)


def seats(bits):
    levels = [[0]]
    for bit in reversed(bits):
        levels.insert(0, [bit | r for level in levels for r in level])
    return levels


def harvest_kernel(seat_ref, *refs, count, bits, by_rows):
    pairs = [(refs[2 * i], refs[2 * i + 1]) for i in range(count)]
    outs, acc = refs[2 * count : -1], refs[-1]
    seat = seat_ref[0]
    chunk = outs[0].shape[2 if by_rows else 3]
    for i, (left, right) in enumerate(pairs):
        acc[...] = mm(left[...], right[...], TN)
        for out, level in zip(outs, seats(bits)):
            for slot, r in enumerate(level):
                span = pl.ds(pl.multiple_of((seat ^ r) * chunk, chunk), chunk)
                out[slot, i] = (acc[span] if by_rows else acc[:, span]).astype(BF16)


def harvest(seat, pairs, bits, by_rows, after=()):
    total = pairs[0][0].shape[0]
    rows, columns = pairs[0][0].shape[1], pairs[0][1].shape[1]
    places = 2 ** len(bits)
    chunk = (rows // places, columns) if by_rows else (rows, columns // places)
    shapes = [(len(level), len(pairs)) + chunk for level in seats(bits)]
    return call(
        functools.partial(harvest_kernel, count=len(pairs), bits=bits, by_rows=by_rows),
        (1,),
        [whole(a.shape) for pair in pairs for a in pair],
        [whole(shape) for shape in shapes],
        [sds(shape, BF16) for shape in shapes],
        [pltpu.VMEM((rows, columns), F32)],
        flops=2 * total * rows * columns * len(pairs),
        moved=6e6,
        prefetch=1,
        after=after,
    )(seat, *[a for pair in pairs for a in pair])


def collect(levels, bits, beside=()):
    parts = list(levels)
    parts[-1] = parts[-1].astype(F32)
    for i, bit in enumerate(bits):
        got = swap(parts[i], "seq", bit)
        if i < len(beside):
            got = lax.optimization_barrier((got, *beside[i]))[0]
        at = 0
        for m in range(i + 1, len(parts)):
            size = parts[m].shape[0]
            parts[m] = parts[m] + got[at : at + size].astype(parts[m].dtype)
            at += size
    return parts[-1][0]


def bend_kernel(rank_ref, keep_ref, near_ref, far_ref, cot_ref, normed_ref, scale_ref, gain_ref, *outs):
    low_out, dgain_out = outs
    grad = (
        keep_ref[0].astype(F32) + near_ref[0].astype(F32) + far_ref[0].astype(F32)
    )
    normed = normed_ref[...].astype(F32)
    dgain_out[...] = jnp.broadcast_to(jnp.sum(grad * normed, 0, keepdims=True), dgain_out.shape)
    g = grad * gain_ref[9:10]
    mean = jnp.mean(g * normed, -1, keepdims=True)
    low_out[...] = (cot_ref[...].astype(F32) + scale_ref[...] * (g - normed * mean)).astype(BF16)


def bend(rank, keep, near, far, cot, normed, scale, gains, after):
    total, model = cot.shape
    rows = total // REL
    own = lambda s, r: (r[0], 0)
    one = pl.BlockSpec((1, rows, model), lambda *_: (0, 0, 0))
    return call(
        bend_kernel,
        (1,),
        [
            one,
            one,
            one,
            pl.BlockSpec((rows, model), own),
            pl.BlockSpec((rows, model), own),
            pl.BlockSpec((rows, 1), own),
            whole(gains.shape),
        ],
        [whole((rows, model)), whole((8, model))],
        [sds((rows, model), BF16), sds((8, model), F32)],
        flops=5e6,
        moved=4e6,
        prefetch=1,
        after=after,
    )(rank, keep, near, far, cot, normed, scale, gains)


def turn_kernel(rank_ref, *refs, heads):
    lows = refs[:REL]
    (
        w_ref,
        q_ref,
        normed_ref,
        scale_ref,
        aux_ref,
        dev_ref,
        ga_out,
        gm_out,
        part_out,
        low_out,
        share_out,
        load_out,
        low_sc,
        state_sc,
    ) = refs[REL:]
    step = pl.program_id(0)
    last = pl.num_programs(0) - 1
    block = last - step
    rank = rank_ref[0]
    rows = q_ref.shape[0]
    scal = 2 * heads * DH
    for k in range(REL):

        @pl.when((rank ^ k) == block)
        def _():
            low_sc[...] = lows[k][...]

    @pl.when(step == 0)
    def _():
        state_sc[...] = jnp.zeros_like(state_sc)

    low = low_sc[...]
    low_out[...] = low
    width = share_out.shape[1]
    share_out[...] = low_sc[:, pl.ds(pl.multiple_of(rank * width, width), width)]
    grad_merged = mm(low, w_ref[...], NT)
    ga_out[...] = grad_merged.astype(BF16)
    end = slice(rows - 1, rows)
    for h in range(heads):
        lo, mid = h * DH, (heads + h) * DH
        g = grad_merged[:, lo : lo + DH]
        normed = normed_ref[:, lo : lo + DH]
        scale = scale_ref[:, h : h + 1]
        grad = scale * (g - normed * jnp.mean(g * normed, -1, keepdims=True))
        gm_out[:, lo : lo + DH] = grad.astype(BF16)
        query = q_ref[:, lo : lo + DH]
        keep = aux_ref[:, h : h + 1]
        cross = aux_ref[:, heads + h : heads + h + 1]
        carry = aux_ref[:, 2 * heads + h : 2 * heads + h + 1]
        mem_part = mm((keep * grad).astype(BF16), query, TN)
        mom_part = mm((cross * grad).astype(BF16), query, TN)
        part_out[0, lo : lo + DH] = mem_part
        part_out[0, mid : mid + DH] = mom_part
        memory, momentum = state_sc[lo : lo + DH], state_sc[mid : mid + DH]
        state_sc[lo : lo + DH] = keep[end] * memory + mem_part
        state_sc[mid : mid + DH] = cross[end] * memory + carry[end] * momentum + mom_part

    @pl.when(step == last)
    def _():
        state_sc[scal : scal + 8] = dev_ref[scal : scal + 8]
        pack_load(load_out, state_sc[...], scal)


def turn(rank, lows, weight, qkv, normed, scales, aux, dev, heads, after):
    total = qkv.shape[0]
    count = total // MBLK
    local, model = weight.shape
    width = model // REL
    scal = 2 * local
    at = lambda b, *_: (count - 1 - b, 0)
    return call(
        functools.partial(turn_kernel, heads=heads),
        (count,),
        [whole(lows[0].shape)] * REL
        + [
            whole(weight.shape),
            pl.BlockSpec((MBLK, local), at),
            pl.BlockSpec((MBLK, local), at),
            pl.BlockSpec((MBLK, DH), at),
            pl.BlockSpec((MBLK, DH), at),
            whole(dev.shape),
        ],
        [
            pl.BlockSpec((MBLK, local), at),
            pl.BlockSpec((MBLK, local), at),
            pl.BlockSpec((1, scal, DH), lambda b, *_: (count - 1 - b, 0, 0)),
            pl.BlockSpec((MBLK, model), at),
            pl.BlockSpec((MBLK, width), at),
            whole((scal + 16, DH)),
        ],
        [
            sds((total, local), BF16),
            sds((total, local), BF16),
            sds((count, scal, DH), F32),
            sds((total, model), BF16),
            sds((total, width), BF16),
            sds((scal + 16, DH), BF16),
        ],
        [
            pltpu.VMEM((MBLK, model), BF16),
            pltpu.VMEM((scal + 8, DH), F32),
        ],
        flops=8e8,
        moved=8e6,
        prefetch=1,
        after=after,
    )(rank, *lows, weight, qkv, normed, scales, aux, dev)


def settle_kernel(qkv_ref, *refs, heads):
    atts = refs[: 3 * heads]
    mems = refs[3 * heads : 6 * heads]
    (
        gm_ref,
        aux_ref,
        low_ref,
        part_ref,
        state_ref,
        proj_ref,
        halo_ref,
        conv_ref,
        starts_ref,
        gp_out,
        tail_out,
        head_out,
        gconv_out,
        state_sc,
        mix_sc,
        ext_sc,
        proj_sc,
    ) = refs[6 * heads :]
    step = pl.program_id(0)
    last = pl.num_programs(0) - 1
    block = last - step
    rows = qkv_ref.shape[0]
    local = heads * DH
    base = block * rows

    @pl.when(step == 0)
    def _():
        state_sc[...] = state_ref[0 : state_sc.shape[0]]
        ext_sc[0:8] = jnp.zeros((8, 3 * local), F32)
        gconv_out[...] = jnp.zeros_like(gconv_out)

    end = slice(rows - 1, rows)
    for h in range(heads):
        lo, mid = h * DH, (heads + h) * DH
        memory, momentum = state_sc[lo : lo + DH], state_sc[mid : mid + DH]
        memory_low, momentum_low = memory.astype(BF16), momentum.astype(BF16)
        keep = aux_ref[:, h : h + 1]
        cross = aux_ref[:, heads + h : heads + h + 1]
        carry = aux_ref[:, 2 * heads + h : 2 * heads + h + 1]
        end_kernel = aux_ref[:, 3 * heads + h : 3 * heads + h + 1]
        end_carry = aux_ref[:, 4 * heads + h : 4 * heads + h + 1]
        keys = qkv_ref[:, local + lo : local + lo + DH]
        values = qkv_ref[:, 2 * local + lo : 2 * local + lo + DH]
        gmem = gm_ref[:, lo : lo + DH]
        dq = keep * mm(gmem, low_ref[0, lo : lo + DH]) + cross * mm(
            gmem, low_ref[0, mid : mid + DH]
        )
        dk = end_kernel * mm(values, memory_low) + end_carry * mm(values, momentum_low)
        dv = end_kernel * mm(keys, memory_low, NT) + end_carry * mm(keys, momentum_low, NT)
        for c, extra in enumerate((dq, dk, dv)):
            mix_sc[:, c * local + lo : c * local + lo + DH] = (
                atts[c * heads + h][...] + mems[c * heads + h][...] + extra
            )
        state_sc[lo : lo + DH] = keep[end] * memory + part_ref[0, lo : lo + DH]
        state_sc[mid : mid + DH] = (
            cross[end] * memory + carry[end] * momentum + part_ref[0, mid : mid + DH]
        )
    before = proj_ref[pl.ds(pl.multiple_of(jnp.maximum(base - 16, 0), 16), 16)].astype(F32)[8:16]
    proj_sc[0:8] = jnp.where(block == 0, halo_ref[...], before)
    proj_sc[8 : 8 + rows] = proj_ref[pl.ds(pl.multiple_of(base, rows), rows)].astype(F32)
    ext_sc[rows : rows + 8] = ext_sc[0:8]
    ext_sc[0:rows] = jnp.zeros((rows, 3 * local), F32)
    place = base + iota((rows, 1), 0)
    starts = starts_ref[...]
    for j in range(KW):
        tap = mix_sc[...] * (place - j >= starts).astype(F32)
        ext_sc[8 - j : 8 - j + rows] += conv_ref[j : j + 1] * tap
        gconv_out[j : j + 1] += jnp.sum(tap * proj_sc[8 - j : 8 - j + rows], 0, keepdims=True)
    gp_out[...] = ext_sc[8 : 8 + rows].astype(BF16)

    @pl.when(step == 0)
    def _():
        tail_out[...] = ext_sc[rows - 8 : rows + 8]

    @pl.when(step == last)
    def _():
        head_out[...] = ext_sc[0:8]


def settle(qkv, att_grads, mem_grads, gm, aux, lows, parts, state, proj, halo, conv, starts, heads):
    total = qkv.shape[0]
    count = total // MBLK
    local = heads * DH
    scal = 2 * local
    at = lambda b, *_: (count - 1 - b, 0)
    by_block = pl.BlockSpec((1, scal, DH), lambda b, *_: (count - 1 - b, 0, 0))
    return call(
        functools.partial(settle_kernel, heads=heads),
        (count,),
        [pl.BlockSpec((MBLK, 3 * local), at)]
        + [pl.BlockSpec((MBLK, DH), at)] * (6 * heads)
        + [
            pl.BlockSpec((MBLK, local), at),
            pl.BlockSpec((MBLK, DH), at),
            by_block,
            by_block,
            whole(state.shape),
            whole(proj.shape),
            whole(halo.shape),
            whole(conv.shape),
            pl.BlockSpec((MBLK, 1), at),
        ],
        [
            pl.BlockSpec((MBLK, 3 * local), at),
            whole((16, 3 * local)),
            whole((8, 3 * local)),
            whole((8, 3 * local)),
        ],
        [
            sds((total, 3 * local), BF16),
            sds((16, 3 * local), F32),
            sds((8, 3 * local), F32),
            sds((8, 3 * local), F32),
        ],
        [
            pltpu.VMEM((scal, DH), F32),
            pltpu.VMEM((MBLK, 3 * local), F32),
            pltpu.VMEM((MBLK + 8, 3 * local), F32),
            pltpu.VMEM((MBLK + 8, 3 * local), F32),
        ],
        flops=6e8,
        moved=14e6,
    )(qkv, *att_grads, *mem_grads, gm, aux, lows, parts, state, proj, halo, conv, starts)


def back_kernel(rank_ref, gp_ref, w_ref, x_ref, scale_ref, gain_ref, *outs):
    send_out, far_out, keep_out, dgain_out, grad_sc = outs
    rank = rank_ref[0]
    width = keep_out.shape[1]
    local = w_ref.shape[2]

    @pl.when(pl.program_id(0) == 0)
    def _():
        dgain_out[...] = jnp.zeros_like(dgain_out)

    grad = mm(gp_ref[:, 0:local], w_ref[0], NT)
    for c in range(1, 3):
        grad = grad + mm(gp_ref[:, c * local : (c + 1) * local], w_ref[c], NT)
    scale = scale_ref[...]
    normed = x_ref[...].astype(F32) * scale
    dgain_out[...] += jnp.broadcast_to(jnp.sum(grad * normed, 0, keepdims=True), dgain_out.shape)
    g = grad * gain_ref[8:9]
    grad_sc[...] = (scale * (g - normed * jnp.mean(g * normed, -1, keepdims=True))).astype(BF16)
    spans = [pl.ds(pl.multiple_of((rank ^ k) * width, width), width) for k in range(REL)]
    keep_out[...] = grad_sc[:, spans[0]]
    send_out[0] = grad_sc[:, spans[1]]
    far_out[...] = grad_sc[:, spans[2]]
    send_out[1] = grad_sc[:, spans[3]]


def back(rank, gp, weight, x, scale, gains):
    total, model = x.shape
    width = model // REL
    at = lambda b, *_: (b, 0)
    return call(
        back_kernel,
        (total // MBLK,),
        [
            pl.BlockSpec((MBLK, gp.shape[1]), at),
            whole(weight.shape),
            pl.BlockSpec((MBLK, model), at),
            pl.BlockSpec((MBLK, 1), at),
            whole(gains.shape),
        ],
        [
            pl.BlockSpec((2, MBLK, width), lambda b, *_: (0, b, 0)),
            pl.BlockSpec((MBLK, width), at),
            pl.BlockSpec((MBLK, width), at),
            whole((8, model)),
        ],
        [
            sds((2, total, width), BF16),
            sds((total, width), BF16),
            sds((total, width), BF16),
            sds((8, model), F32),
        ],
        [pltpu.VMEM((MBLK, model), BF16)],
        flops=1.7e9,
        moved=8e6,
        prefetch=1,
    )(rank, gp, weight, x, scale, gains)


def scatter_rel(send, far, keep):
    got = swap(send, "head", 1)
    got_far = swap(far + got[1], "head", 2)
    return keep.astype(F32) + got[0].astype(F32) + got_far.astype(F32)


def per_device(
    inputs,
    cotangent,
    norm_gain,
    qkv_weight,
    conv_kernel,
    persistent,
    out_weight,
    ffn_gain,
    gate_up,
    down_weight,
    memory_decay,
    momentum_decay,
    doc_start,
):
    total, width = inputs.shape
    local = qkv_weight.shape[2]
    heads = local // DH
    model = width * REL
    rank = lax.axis_index("head").astype(jnp.int32).reshape(1)
    seat = lax.axis_index("seq").astype(jnp.int32).reshape(1)
    starts = (doc_start - lax.axis_index("seq") * total).reshape(total, 1)
    decays = jnp.concatenate(
        [memory_decay.T, momentum_decay.T, jnp.ones((8 - 2 * heads, total), F32)], 0
    )
    conv = conv_kernel.reshape(KW, 3 * local)

    halo_rows = shifted(inputs[total - 8 :], "seq", 1)
    small = jnp.concatenate(
        [halo_rows, norm_gain[None], ffn_gain[None], jnp.zeros((6, width), BF16)], 0
    )
    blocks = gather_rel(inputs)
    smalls = gather_rel(small)
    cots = gather_rel(cotangent)
    out_weights = gather_rel(out_weight)

    (
        x,
        hidden_one,
        scale_one,
        proj,
        qkv,
        kmat,
        aux,
        parts,
        halo,
        gains,
        dev_state,
        load,
    ) = front(rank, blocks, smalls, qkv_weight, conv, starts, decays, heads)

    atts, ratios, intras, probs, fixps = zip(
        *[attend(qkv, persistent, starts, kmat, h, heads) for h in range(heads)]
    )
    prefix = entering(load, heads, False, [atts[:1], atts[1:]])
    merged, normed_mem, mem_scales, state_lows = merge(
        qkv, atts, intras, aux, parts, prefix, heads, (*cots, *out_weights)
    )
    merged_rel = gather_rel(merged)
    grad_act, cot = recall(rank, cots, down_weight, (merged,))
    hidden_two, normed_two, scale_two, middle_share = middle(
        rank, merged_rel, out_weights, x, gains, (grad_act,)
    )
    act, grad_gate, grad_up, send, far, keep = ffn(
        rank, hidden_two, grad_act, gate_up.transpose(0, 2, 1)
    )
    near = swap(send, "head", 1)
    far_sum = swap(far + near[1:2], "head", 2)
    answers = answer(rank, act, down_weight)
    places = lax.axis_size("seq")
    cut = model // places == DH
    bits = tuple(2**i for i in range((places - 1).bit_length()))
    if cut:
        first = harvest(seat, [(act, cot), (grad_gate, hidden_two)], bits, False)
        second = harvest(seat, [(grad_up, hidden_two)], bits, False, first[:1])
        filler, later = (answers[0], first[0]), (second[0],)
    else:
        filler, later = (answers[0],), ()
    low_own, dgain_two = bend(
        rank, keep, near, far_sum, cot, normed_two, scale_two, gains, filler
    )
    lows = gather_rel(low_own)
    grad_att, grad_mem, mem_parts, low_full, low_share, back_load = turn(
        rank, lows, out_weight, qkv, normed_mem, mem_scales, aux, dev_state, heads, later
    )
    pieces = [
        attend_back(
            qkv, persistent, probs[h], fixps[h], ratios[h], grad_att, grad_mem, kmat, h, heads
        )
        for h in range(heads)
    ]
    suffix = entering(
        back_load, heads, True, [pieces[h][:1] for h in range(heads)]
    )
    output = (middle_share + scatter_rel(*answers)).astype(BF16)
    att_grads = [pieces[h][c] for c in range(3) for h in range(heads)]
    mem_grads = [pieces[h][4 + c] for c in range(3) for h in range(heads)]
    gp, tail, head_rows, gconv = settle(
        qkv,
        att_grads,
        mem_grads,
        grad_mem,
        aux,
        state_lows,
        mem_parts,
        suffix,
        proj,
        halo,
        conv,
        starts,
        heads,
    )
    returned = shifted(head_rows, "seq", -1)
    fixed_tail = jnp.concatenate([tail[:8], tail[8:] + returned], 0).astype(BF16)
    gp = lax.dynamic_update_slice(gp, fixed_tail, (total - 16, 0))
    if cut:
        third = harvest(seat, [(merged, low_full)], bits, False)
        steps = [(pieces[0][0],), (pieces[1][0],), (gp,)]
        down_grad, gate_grad = collect(first, bits, steps)
        up_grad = collect(second, bits, steps)[0]
        grad_gate_up = jnp.stack([gate_grad, up_grad], 0).transpose(0, 2, 1)
        grad_out = collect(third, bits, [(gp,)])[0]
        turned = bits[1:] + bits[:1]
        one = harvest(seat, [(hidden_one, gp[:, : 2 * local])], bits, True)
        two = harvest(seat, [(hidden_one, gp[:, 2 * local :])], turned, True)
        one, two = collect(one, bits)[0], collect(two, turned)[0]
        grad_qkv = jnp.stack([one[:, :local], one[:, local:], two], 0)
    else:
        times = lambda a, b: lax.dot_general(a, b, TN, preferred_element_type=F32).astype(BF16)
        scatter = lambda g, dim: lax.psum_scatter(
            g, "seq", scatter_dimension=dim, tiled=True
        ).astype(F32)
        down_grad = scatter(times(act, cot), 1)
        grad_gate_up = scatter(
            jnp.stack([times(hidden_two, grad_gate), times(hidden_two, grad_up)], 0), 1
        )
        grad_out = scatter(times(merged, low_full), 1)
        grad_qkv = scatter(
            jnp.stack(
                [times(hidden_one, gp[:, c * local : (c + 1) * local]) for c in range(3)], 0
            ),
            1,
        )
    bsend, bfar, bkeep, dgain_one = back(rank, gp, qkv_weight, x, scale_one, gains)
    input_grad = scatter_rel(bsend, bfar, bkeep) + low_share.astype(F32)

    grad_fixed = jnp.concatenate([p[3] for p in pieces], -1)
    gain_sums = sum_over(jnp.stack([dgain_one[0], dgain_two[0]], 0), "head")
    gain_own = lax.dynamic_slice_in_dim(
        gain_sums, lax.axis_index("head") * width, width, 1
    )
    fixed_count = persistent.shape[1]
    little = jnp.concatenate(
        [
            gain_own,
            gconv[:KW].reshape(3 * KW, local),
            grad_fixed.reshape(2 * fixed_count, local),
        ],
        0,
    )
    little = sum_over(little, "seq")
    return (
        output,
        input_grad,
        little[0],
        grad_qkv,
        little[2 : 2 + 3 * KW].reshape(KW, 3, local),
        little[2 + 3 * KW :].reshape(2, fixed_count, local),
        grad_out,
        little[1],
        grad_gate_up,
        down_grad,
    )


def solution(mesh):
    placed = (
        P("seq", "head"),
        P("seq", "head"),
        P("head"),
        P(None, None, "head"),
        P(None, None, "head"),
        P(None, None, "head"),
        P("head", None),
        P("head"),
        P(None, None, "head"),
        P("head", None),
        P("seq", "head"),
        P("seq", "head"),
        P("seq"),
    )
    return jax.shard_map(
        per_device,
        mesh=mesh,
        in_specs=placed,
        out_specs=(
            P("seq", "head"),
            P("seq", "head"),
            P("head"),
            P(None, "seq", "head"),
            P(None, None, "head"),
            P(None, None, "head"),
            P("head", "seq"),
            P("head"),
            P(None, "seq", "head"),
            P("head", "seq"),
        ),
        check_vma=False,
    )
```

```python
import functools

import jax
import jax.numpy as jnp
from jax import lax
from jax.experimental import pallas as pl
from jax.experimental.pallas import tpu as pltpu
from jax.sharding import PartitionSpec as P

DH = 128
KW = 4
SEG = 1024
MBLK = 256
EPSILON = 1e-06
MEMORY_FLOOR = 64.0
MASKED = -1e30
F32 = jnp.float32
BF16 = jnp.bfloat16
NN = (((1,), (0,)), ((), ()))
NT = (((1,), (1,)), ((), ()))
TN = (((0,), (0,)), ((), ()))
REL = 4
START_AT = 126


def mm(a, b, dims=NN):
    return lax.dot_general(a, b, dims, preferred_element_type=F32)


def exact(a, b, dims=NN):
    return lax.dot_general(
        a, b, dims, precision=lax.Precision.HIGHEST, preferred_element_type=F32
    )


def padded(shape, dtype):
    size = jnp.dtype(dtype).itemsize
    tile = 32 // size
    if len(shape) == 1:
        return -(-shape[0] // 1024) * 1024 * 4
    total = size * -(-shape[-1] // 128) * 128 * (-(-shape[-2] // tile) * tile)
    for n in shape[:-2]:
        total *= n
    return total


def call(
    kernel,
    grid,
    in_specs,
    out_specs,
    out_shape,
    scratch=(),
    flops=0,
    moved=0,
    prefetch=0,
    after=(),
    ins="",
    outs="",
    alias={},
    spare=5,
):
    taken = prefetch + len(in_specs)
    waits = len(after)

    def body(*refs):
        kernel(*refs[:taken], *refs[taken + waits :])

    spaces = {"v": pltpu.VMEM, "h": pltpu.HBM}
    results = out_shape if isinstance(out_shape, (list, tuple)) else [out_shape]
    out_blocks = out_specs if isinstance(out_specs, (list, tuple)) else [out_specs]
    held = sum(
        2 * padded(b.block_shape, s.dtype) for b, s in zip(out_blocks, results) if b.block_shape
    )
    held += sum(padded(m.shape, m.dtype) for m in scratch)
    if outs:
        out_shape = [
            spaces[c](s.shape, s.dtype) if c in spaces else s for c, s in zip(outs, results)
        ]
        assert len(outs) == len(results)

    spec = pltpu.PrefetchScalarGridSpec(
        num_scalar_prefetch=prefetch,
        grid=grid,
        in_specs=list(in_specs) + [pl.BlockSpec(memory_space=pl.ANY)] * waits,
        out_specs=out_specs,
        scratch_shapes=list(scratch),
    )

    def run(*operands):
        taking = held + sum(
            2 * padded(b.block_shape, a.dtype)
            for b, a in zip(in_specs, operands[prefetch:])
            if b.block_shape
        )
        made = pl.pallas_call(
            body,
            grid_spec=spec,
            out_shape=out_shape,
            input_output_aliases={prefetch + i: o for i, o in alias.items()},
            compiler_params=pltpu.CompilerParams(
                vmem_limit_bytes=min(taking + spare * 2**20, 24 * 2**20)
            ),
            cost_estimate=pl.CostEstimate(
                flops=int(flops), bytes_accessed=int(moved), transcendentals=0
            ),
        )
        if ins:
            assert len(ins) == len(operands) - prefetch
            operands = operands[:prefetch] + tuple(
                pltpu.with_memory_space_constraint(a, spaces[c]) if c in spaces else a
                for c, a in zip(ins, operands[prefetch:])
            )
        return made(*operands, *after)

    return run


def whole(shape):
    return pl.BlockSpec(shape, lambda *_: (0,) * len(shape))


def sds(shape, dtype):
    return jax.ShapeDtypeStruct(shape, dtype)


def iota(shape, dim):
    return lax.broadcasted_iota(jnp.int32, shape, dim)


def swap(x, axis, bit):
    count = lax.axis_size(axis)
    return lax.ppermute(x, axis, [(i, i ^ bit) for i in range(count)])


def shifted(x, axis, by):
    count = lax.axis_size(axis)
    return lax.ppermute(x, axis, [(i, i + by) for i in range(count) if 0 <= i + by < count])


def hold(x, *others):
    return lax.optimization_barrier((x, *others))[0]


def gather_rel(x, beside=(), before=()):
    far = swap(hold(x, *before) if before else x, "head", 2)
    near = swap(x, "head", 1)
    far = hold(far, *beside) if beside else far
    return [x, near, far, swap(far, "head", 1)]


def pack_kernel(halo_ref, one_ref, two_ref, out_ref):
    width = halo_ref.shape[1]
    rows = [
        halo_ref[...].astype(F32),
        one_ref[...].astype(F32).reshape(1, width),
        two_ref[...].astype(F32).reshape(1, width),
        jnp.zeros((6, width), F32),
    ]
    out_ref[...] = jnp.concatenate(rows, 0).astype(BF16)


def pack(halo, one, two, after):
    return call(
        pack_kernel,
        (1,),
        [whole(halo.shape), whole(one.shape), whole(two.shape)],
        whole((16, halo.shape[1])),
        sds((16, halo.shape[1]), BF16),
        moved=1e4,
        after=after,
        ins="hhh",
    )(halo, one, two)


def prepare_kernel(rank_ref, doc_ref, keep_ref, carry_ref, kmat_out, aux_out, *, heads):
    rows = doc_ref.shape[1]
    base = pl.program_id(0) * rows
    below = iota((rows, rows), 0)
    right = iota((rows, rows), 1)
    local_start = doc_ref[...] - rank_ref[1] * (rows * pl.num_programs(0))
    by_row = jnp.concatenate(
        [
            jnp.log(keep_ref[...]),
            jnp.log(carry_ref[...]),
            local_start.astype(F32),
            jnp.zeros((7 - 2 * heads, rows), F32),
        ],
        0,
    )
    first = by_row.astype(BF16).astype(F32)
    second = (by_row - first).astype(BF16).astype(F32)
    third = by_row - first - second
    split = jnp.concatenate([first, second, third, jnp.zeros((8, rows), F32)], 0).astype(BF16)
    upto = (right <= below).astype(BF16)
    same = (right == below).astype(BF16)
    rows_sum = mm(split, (below <= right).astype(BF16))
    rows_sum = rows_sum[0:8] + rows_sum[8:16] + rows_sum[16:24]
    cols_sum = mm(upto, split, NT)
    cols_sum = cols_sum[:, 0:8] + cols_sum[:, 8:16] + cols_sum[:, 16:24]
    at = 2 * heads
    starts = mm(same, split, NT)
    starts = starts[:, at : at + 1] + starts[:, at + 8 : at + 9] + starts[:, at + 16 : at + 17]
    start_at = starts.astype(jnp.int32)
    linked = (right <= below) & (base + right >= start_at)
    fresh = start_at < base
    reaches_end = base + iota((rows, 1), 0) >= start_at[rows - 1 : rows]
    lane = iota((rows, DH), 1)
    aux = jnp.where(lane == START_AT, starts, 0.0)
    for h in range(heads):
        keep_col, keep_row = cols_sum[:, h : h + 1], rows_sum[h : h + 1]
        carry_col = cols_sum[:, heads + h : heads + h + 1]
        carry_row = rows_sum[heads + h : heads + h + 1]
        keep_mat = jnp.where(linked, jnp.exp(jnp.minimum(keep_col - keep_row, 0.0)), 0.0)
        carry_mat = jnp.where(linked, jnp.exp(jnp.minimum(carry_col - carry_row, 0.0)), 0.0)
        keep_low = keep_mat.astype(BF16)
        kernel = mm(keep_low, carry_mat.astype(BF16))
        kmat_out[h, 0] = kernel.astype(BF16)
        keep_weight = jnp.where(fresh, jnp.exp(keep_col), 0.0)
        carried = jnp.where(fresh, jnp.exp(carry_col), 0.0)
        cross = mm(keep_low, jnp.broadcast_to(carried, (rows, DH)).astype(BF16))
        last = jnp.broadcast_to(kernel[rows - 1 : rows], (16, rows)).astype(BF16)
        end_kernel = mm(same, last, NT)[:, 0:1]
        end_carry = jnp.where(
            reaches_end, jnp.exp(jnp.minimum(carry_col[rows - 1 : rows] - carry_col, 0.0)), 0.0
        )
        for slot, column in enumerate((keep_weight, cross, carried, end_kernel, end_carry)):
            aux = jnp.where(lane == slot * heads + h, column, aux)
    aux_out[...] = aux


def prepare(rank, doc, keep, carry):
    heads, total = keep.shape
    count = total // MBLK
    by_token = lambda n: pl.BlockSpec((n, MBLK), lambda b, *_: (0, b))
    return call(
        functools.partial(prepare_kernel, heads=heads),
        (count,),
        [by_token(1), by_token(heads), by_token(heads)],
        [
            pl.BlockSpec((heads, 1, MBLK, MBLK), lambda b, *_: (0, b, 0, 0)),
            pl.BlockSpec((MBLK, DH), lambda b, *_: (b, 0)),
        ],
        [sds((heads, count, MBLK, MBLK), BF16), sds((total, DH), F32)],
        flops=4e8,
        moved=2e6,
        prefetch=1,
        ins="hhh",
    )(rank, doc, keep, carry)


def front_kernel(rank_ref, *refs, heads):
    blocks, smalls = refs[:REL], refs[REL : 2 * REL]
    (
        w_ref,
        conv_ref,
        aux_ref,
        x_out,
        hid_out,
        proj_out,
        qkv_out,
        part_out,
        halo_out,
        gain_out,
        state_out,
        load_out,
        small_sc,
        proj_sc,
        state_sc,
    ) = refs[2 * REL :]
    b = pl.program_id(0)
    rank = rank_ref[0]
    rows, width = blocks[0].shape
    local = heads * DH
    spans = [pl.ds(pl.multiple_of((rank ^ k) * width, width), width) for k in range(REL)]
    for k in range(REL):
        x_out[:, spans[k]] = blocks[k][...]
    scal = 2 * heads * DH

    @pl.when(b == 0)
    def _():
        for k in range(REL):
            small_sc[:, spans[k]] = smalls[k][...]
        small = small_sc[...].astype(F32)
        gain_out[...] = small
        scale = lax.rsqrt(jnp.mean(small * small, -1, keepdims=True) + EPSILON)
        hidden = (small * scale * small[8:9]).astype(BF16)
        for c in range(3):
            proj_sc[0:8, c * local : (c + 1) * local] = mm(hidden, w_ref[c])[0:8]
        halo_out[...] = proj_sc[0:8]
        state_sc[0:scal] = jnp.zeros((scal, DH), F32)
        row = iota((8, DH), 0)
        state_sc[scal : scal + 8] = jnp.where(
            (row < heads) | ((row >= 2 * heads) & (row < 3 * heads)), 1.0, 0.0
        ).astype(F32)

    gain = gain_out[8:9]
    x = x_out[...].astype(F32)
    scale = lax.rsqrt(jnp.mean(x * x, -1, keepdims=True) + EPSILON)
    hidden = (x * scale * gain).astype(BF16)
    hid_out[...] = hidden
    for c in range(3):
        proj_sc[8 : 8 + rows, c * local : (c + 1) * local] = mm(hidden, w_ref[c])
    place = b * rows + iota((rows, 1), 0)
    starts = aux_ref[:, START_AT : START_AT + 1].astype(jnp.int32)
    mixed = jnp.zeros((rows, 3 * local), F32)
    for j in range(KW):
        inside = (place - j >= starts).astype(F32)
        mixed = mixed + conv_ref[j : j + 1] * proj_sc[8 - j : 8 - j + rows] * inside
    rounded = mixed.astype(BF16)
    qkv_out[...] = rounded
    proj_out[...] = proj_sc[8 : 8 + rows].astype(BF16)
    proj_sc[0:8] = proj_sc[rows : rows + 8]
    end = slice(rows - 1, rows)
    for h in range(heads):
        column = lambda slot: aux_ref[:, slot * heads + h : slot * heads + h + 1]
        keys = rounded[:, local + h * DH : local + (h + 1) * DH]
        values = rounded[:, 2 * local + h * DH : 2 * local + (h + 1) * DH].astype(F32)
        weighted = jnp.concatenate([values * column(3), values * column(4)], 1).astype(BF16)
        part = mm(weighted, keys, TN)
        mem_part, mom_part = part[0:DH], part[DH : 2 * DH]
        lo, mid = h * DH, (heads + h) * DH
        part_out[0, lo : lo + DH] = mem_part.astype(BF16)
        part_out[0, mid : mid + DH] = mom_part.astype(BF16)
        keep_end, cross_end, carry_end = [
            jnp.broadcast_to(column(slot)[end], (1, DH)) for slot in range(3)
        ]
        memory, momentum = state_sc[lo : lo + DH], state_sc[mid : mid + DH]
        state_sc[lo : lo + DH] = keep_end * memory + cross_end * momentum + mem_part
        state_sc[mid : mid + DH] = carry_end * momentum + mom_part
        keep_at, cross_at, carry_at = scal + h, scal + heads + h, scal + 2 * heads + h
        keep_dev = state_sc[keep_at : keep_at + 1]
        cross_dev = state_sc[cross_at : cross_at + 1]
        carry_dev = state_sc[carry_at : carry_at + 1]
        state_sc[keep_at : keep_at + 1] = keep_end * keep_dev
        state_sc[cross_at : cross_at + 1] = keep_end * cross_dev + cross_end * carry_dev
        state_sc[carry_at : carry_at + 1] = carry_end * carry_dev

    @pl.when(b == pl.num_programs(0) - 1)
    def _():
        state_out[...] = state_sc[...]
        pack_load(load_out, state_sc[...], scal)


def pack_load(load_out, state, scal):
    load_out[0:scal] = state[0:scal].astype(BF16)
    tail = state[scal : scal + 8]
    high = tail.astype(BF16).astype(F32)
    load_out[scal : scal + 16] = jnp.concatenate([high, tail - high], 0).astype(BF16)


def front(rank, blocks, smalls, weight, conv, aux, heads):
    total, width = blocks[0].shape
    model = width * REL
    local = heads * DH
    count = total // MBLK
    scal = 2 * heads * DH
    at = lambda b, *_: (b, 0)
    return call(
        functools.partial(front_kernel, heads=heads),
        (count,),
        [pl.BlockSpec((MBLK, width), at)] * REL
        + [whole(smalls[0].shape)] * REL
        + [
            whole(weight.shape),
            whole(conv.shape),
            pl.BlockSpec((MBLK, DH), at),
        ],
        [
            pl.BlockSpec((MBLK, model), at),
            pl.BlockSpec((MBLK, model), at),
            pl.BlockSpec((MBLK, 3 * local), at),
            pl.BlockSpec((MBLK, 3 * local), at),
            pl.BlockSpec((1, scal, DH), lambda b, *_: (b, 0, 0)),
            whole((8, 3 * local)),
            whole((16, model)),
            whole((scal + 8, DH)),
            whole((scal + 16, DH)),
        ],
        [
            sds((total, model), BF16),
            sds((total, model), BF16),
            sds((total, 3 * local), BF16),
            sds((total, 3 * local), BF16),
            sds((count, scal, DH), BF16),
            sds((8, 3 * local), F32),
            sds((16, model), F32),
            sds((scal + 8, DH), F32),
            sds((scal + 16, DH), BF16),
        ],
        [
            pltpu.VMEM((16, model), BF16),
            pltpu.VMEM((MBLK + 8, 3 * local), F32),
            pltpu.VMEM((scal + 8, DH), F32),
        ],
        flops=2.2e9,
        moved=12e6,
        prefetch=1,
        ins="h" * (2 * REL) + "hho",
        outs="hhhoooooo",
    )(rank, *blocks, *smalls, weight, conv, aux)


def compose(first, second, heads, backward):
    scal = 2 * heads * DH
    memory, momentum, keeps, crosses, carries = [], [], [], [], []
    for h in range(heads):
        lo, mid = h * DH, (heads + h) * DH
        at = [scal + c * heads + h for c in range(3)]
        keep_one, cross_one, carry_one = [first[n : n + 1] for n in at]
        keep_two, cross_two, carry_two = [second[n : n + 1] for n in at]
        mem_one, mom_one = first[lo : lo + DH], first[mid : mid + DH]
        mem_two, mom_two = second[lo : lo + DH], second[mid : mid + DH]
        if backward:
            memory.append(mem_two + keep_two * mem_one)
            momentum.append(mom_two + cross_two * mem_one + carry_two * mom_one)
            crosses.append(cross_two * keep_one + carry_two * cross_one)
        else:
            memory.append(keep_two * mem_one + cross_two * mom_one + mem_two)
            momentum.append(carry_two * mom_one + mom_two)
            crosses.append(keep_two * cross_one + cross_two * carry_one)
        keeps.append(keep_two * keep_one)
        carries.append(carry_two * carry_one)
    rest = [jnp.zeros((8 - 3 * heads, DH), F32)]
    return jnp.concatenate(memory + momentum + keeps + crosses + carries + rest, 0)


def unpack(ref, scal):
    tail = ref[scal : scal + 16].astype(F32)
    return jnp.concatenate([ref[0:scal].astype(F32), tail[0:8] + tail[8:16]], 0)


def last_join_kernel(rank_ref, got_ref, prefix_ref, prefix_out, *, bit, heads, backward):
    later = (rank_ref[1] & bit) == (0 if backward else bit)

    @pl.when(later)
    def _():
        got = unpack(got_ref, 2 * heads * DH)
        prefix_out[...] = compose(got, prefix_ref[...], heads, backward)

    @pl.when(jnp.logical_not(later))
    def _():
        prefix_out[...] = prefix_ref[...]


def last_join(rank, got, prefix, bit, heads, backward, after):
    return call(
        functools.partial(last_join_kernel, bit=bit, heads=heads, backward=backward),
        (1,),
        [whole(got.shape), whole(prefix.shape)],
        [whole(prefix.shape)],
        [sds(prefix.shape, F32)],
        flops=1e6,
        moved=1e6,
        prefetch=1,
        after=after,
    )(rank, got, prefix)[0]


def join_kernel(rank_ref, got_ref, total_ref, prefix_ref, *outs, bit, heads, backward):
    total_out, prefix_out, load_out = outs
    scal = 2 * heads * DH
    later = (rank_ref[1] & bit) == (0 if backward else bit)
    got = unpack(got_ref, scal)

    @pl.when(later)
    def _():
        total_out[...] = compose(got, total_ref[...], heads, backward)
        prefix_out[...] = compose(got, prefix_ref[...], heads, backward)

    @pl.when(jnp.logical_not(later))
    def _():
        total_out[...] = compose(total_ref[...], got, heads, backward)
        prefix_out[...] = prefix_ref[...]

    pack_load(load_out, total_out[...], scal)


def join(rank, got, total, prefix, bit, heads, backward, after):
    scal = 2 * heads * DH
    state = (scal + 8, DH)
    return call(
        functools.partial(join_kernel, bit=bit, heads=heads, backward=backward),
        (1,),
        [whole(got.shape), whole(state), whole(state)],
        [whole(state), whole(state), whole((scal + 16, DH))],
        [sds(state, F32), sds(state, F32), sds((scal + 16, DH), BF16)],
        flops=1e6,
        moved=1e6,
        prefetch=1,
        after=after,
    )(rank, got, total, prefix)


def entering(rank, load, total, heads, backward, beside):
    count = lax.axis_size("seq")
    row = iota(total.shape, 0) - 2 * heads * DH
    one = ((row >= 0) & (row < heads)) | ((row >= 2 * heads) & (row < 3 * heads))
    prefix = one.astype(F32)
    bit, lap = 1, 0
    while bit < count:
        after = beside[lap](load) if lap < len(beside) else ()
        got = swap(load, "seq", bit)
        if 2 * bit >= count:
            return last_join(rank, got, prefix, bit, heads, backward, after)
        total, prefix, load = join(rank, got, total, prefix, bit, heads, backward, after)
        bit, lap = bit * 2, lap + 1


def attend_kernel(q_ref, k_ref, v_ref, fix_ref, aux_ref, *outs):
    for i in range(k_ref.shape[0] // MBLK):

        @pl.when(pl.program_id(0) == i)
        def _():
            attend_block(i, q_ref, k_ref, v_ref, fix_ref, aux_ref, *outs)


def attend_block(
    i,
    q_ref,
    k_ref,
    v_ref,
    fix_ref,
    aux_ref,
    att_out,
    ratio_out,
    prob_out,
    fixp_out,
):
    fixed_keys, fixed_values = fix_ref[0], fix_ref[1]
    factor = DH ** (-0.5)
    span = slice(i * MBLK, (i + 1) * MBLK)
    seen = (i + 1) * MBLK
    query = q_ref[...]
    starts = aux_ref[:, START_AT : START_AT + 1].astype(jnp.int32)
    raw = mm(query, k_ref[0:seen], NT)
    fixed = mm(query, fixed_keys, NT)
    key_at = iota((MBLK, seen), 1)
    ok = (key_at >= starts) & (key_at <= i * MBLK + iota((MBLK, seen), 0))
    raw = jnp.where(ok, raw, MASKED)
    top = jnp.maximum(jnp.max(raw, -1, keepdims=True), jnp.max(fixed, -1, keepdims=True))
    weights = jnp.exp((raw - top) * factor)
    fix_weights = jnp.exp((fixed - top) * factor)
    scale = 1.0 / (
        jnp.sum(weights, -1, keepdims=True) + jnp.sum(fix_weights, -1, keepdims=True)
    )
    low = (weights * scale).astype(BF16)
    fix_low = (fix_weights * scale).astype(BF16)
    prob_out[:, 0:seen] = low
    fixp_out[...] = fix_low
    attended = mm(low, v_ref[0:seen]) + mm(fix_low, fixed_values)
    held = jnp.sum(low.astype(F32), -1, keepdims=True) + jnp.sum(
        fix_low.astype(F32), -1, keepdims=True
    )
    att_out[...] = attended
    ratio_out[...] = attended / held


def attend(qkv, fixed, aux, head, heads, after):
    total = qkv.shape[0]
    count = total // MBLK
    fixed_count = fixed.shape[1]
    lanes = lambda c: pl.BlockSpec((total, DH), lambda i: (0, c * heads + head))
    at = lambda i: (i, 0)
    return call(
        attend_kernel,
        (count,),
        [
            pl.BlockSpec((MBLK, DH), lambda i: (i, head)),
            lanes(1),
            lanes(2),
            pl.BlockSpec((2, fixed_count, DH), lambda i: (0, 0, head)),
            pl.BlockSpec((MBLK, DH), at),
        ],
        [pl.BlockSpec((MBLK, DH), at)] * 2
        + [pl.BlockSpec((MBLK, total), at), pl.BlockSpec((MBLK, fixed_count), at)],
        [sds((total, DH), F32)] * 2
        + [sds((total, total), BF16), sds((total, fixed_count), BF16)],
        flops=1.5e9,
        moved=8e6,
        after=after,
        outs="ohhh",
    )(qkv, qkv, qkv, fixed, aux)


def within_kernel(qkv_ref, kmat_ref, out_ref, *, heads):
    local = heads * DH
    for h in range(heads):
        lo = h * DH
        near = mm(qkv_ref[:, lo : lo + DH], qkv_ref[:, local + lo : local + lo + DH], NT)
        weights = (kmat_ref[h, 0].astype(F32) * near).astype(BF16)
        out_ref[:, lo : lo + DH] = mm(weights, qkv_ref[:, 2 * local + lo : 2 * local + lo + DH])


def within(qkv, kmat, after):
    total = qkv.shape[0]
    heads, count = kmat.shape[:2]
    at = lambda b: (b, 0)
    return call(
        functools.partial(within_kernel, heads=heads),
        (count,),
        [
            pl.BlockSpec((MBLK, qkv.shape[1]), at),
            pl.BlockSpec((heads, 1, MBLK, MBLK), lambda b: (0, b, 0, 0)),
        ],
        [pl.BlockSpec((MBLK, heads * DH), at)],
        [sds((total, heads * DH), F32)],
        flops=3e8,
        moved=4e6,
        after=after,
    )(qkv, kmat)[0]


def within_back_kernel(qkv_ref, kmat_ref, gm_ref, out_ref, *, heads):
    local = heads * DH
    for h in range(heads):
        lo = h * DH
        query, keys, values = [
            qkv_ref[:, c * local + lo : c * local + lo + DH] for c in range(3)
        ]
        grad = gm_ref[:, lo : lo + DH]
        kernel = kmat_ref[h, 0].astype(F32)
        near = (kernel * mm(query, keys, NT)).astype(BF16)
        cross = (kernel * mm(grad, values, NT)).astype(BF16)
        out_ref[:, lo : lo + DH] = mm(cross, keys)
        out_ref[:, local + lo : local + lo + DH] = mm(cross, query, TN)
        out_ref[:, 2 * local + lo : 2 * local + lo + DH] = mm(near, grad, TN)


def within_back(qkv, kmat, gm, after):
    total, columns = qkv.shape
    heads, count = kmat.shape[:2]
    at = lambda b: (b, 0)
    return call(
        functools.partial(within_back_kernel, heads=heads),
        (count,),
        [
            pl.BlockSpec((MBLK, columns), at),
            pl.BlockSpec((heads, 1, MBLK, MBLK), lambda b: (0, b, 0, 0)),
            pl.BlockSpec((MBLK, heads * DH), at),
        ],
        [pl.BlockSpec((MBLK, columns), at)],
        [sds((total, columns), F32)],
        flops=6e8,
        moved=6e6,
        after=after,
    )(qkv, kmat, gm)[0]


def attend_back_kernel(*refs):
    count = pl.num_programs(0)
    total = refs[1].shape[0]
    for i in range(total // MBLK):

        @pl.when(count - 1 - pl.program_id(0) == i)
        def _():
            attend_back_block(i, *refs)


def attend_back_block(
    i,
    q_ref,
    k_ref,
    v_ref,
    fix_ref,
    prob_ref,
    fixp_ref,
    ratio_ref,
    grad_ref,
    dq_out,
    dk_out,
    dv_out,
    dfix_out,
):
    fixed_keys, fixed_values = fix_ref[0], fix_ref[1]
    factor = DH ** (-0.5)
    span = slice(i * MBLK, (i + 1) * MBLK)
    seen = (i + 1) * MBLK
    query, grad = q_ref[...], grad_ref[...]
    delta = jnp.sum(grad.astype(F32) * ratio_ref[...], -1, keepdims=True)
    low, fix_low = prob_ref[:, 0:seen], fixp_ref[...]
    back = mm(grad, v_ref[0:seen], NT)
    fix_back = mm(grad, fixed_values, NT)
    grad_raw = (low.astype(F32) * (back - delta) * factor).astype(BF16)
    fix_raw = (fix_low.astype(F32) * (fix_back - delta) * factor).astype(BF16)
    dk, dv = mm(grad_raw, query, TN), mm(low, grad, TN)
    dfix_k, dfix_v = mm(fix_raw, query, TN), mm(fix_low, grad, TN)
    if seen == k_ref.shape[0]:
        dk_out[...] = dk
        dv_out[...] = dv
        dfix_out[0] = dfix_k
        dfix_out[1] = dfix_v
    else:
        dk_out[0:seen] += dk
        dv_out[0:seen] += dv
        dfix_out[0] += dfix_k
        dfix_out[1] += dfix_v
    dq_out[...] = mm(grad_raw, k_ref[0:seen]) + mm(fix_raw, fixed_keys)


def attend_back(qkv, fixed, prob, fixp, ratio, grads, head, heads, after):
    total = qkv.shape[0]
    count = total // MBLK
    fixed_count = fixed.shape[1]
    lanes = lambda c: pl.BlockSpec((total, DH), lambda s: (0, c * heads + head))
    at = lambda s: (count - 1 - s, 0)
    of_head = pl.BlockSpec((MBLK, DH), lambda s: (count - 1 - s, head))
    return call(
        attend_back_kernel,
        (count,),
        [
            of_head,
            lanes(1),
            lanes(2),
            pl.BlockSpec((2, fixed_count, DH), lambda s: (0, 0, head)),
            pl.BlockSpec((MBLK, total), at),
            pl.BlockSpec((MBLK, fixed_count), at),
            pl.BlockSpec((MBLK, DH), at),
            of_head,
        ],
        [pl.BlockSpec((MBLK, DH), at)] + [whole((total, DH))] * 2 + [whole((2, fixed_count, DH))],
        [sds((total, DH), F32)] * 3 + [sds((2, fixed_count, DH), F32)],
        flops=3e9,
        moved=10e6,
        after=after,
        ins="oooohhho",
        outs="hhho",
    )(qkv, qkv, qkv, fixed, prob, fixp, ratio, grads)


def merge_kernel(q_ref, *refs, heads):
    atts = refs[:heads]
    (
        intra_ref,
        aux_ref,
        part_ref,
        state_ref,
        merged_out,
        normed_out,
        scale_out,
        state_low,
        state_sc,
    ) = refs[heads:]
    rows = q_ref.shape[0]
    lane = iota((rows, DH), 1)
    scales = jnp.zeros((rows, DH), F32)

    @pl.when(pl.program_id(0) == 0)
    def _():
        state_sc[...] = state_ref[0 : state_sc.shape[0]]

    for h in range(heads):
        lo, mid = h * DH, (heads + h) * DH
        memory, momentum = state_sc[lo : lo + DH], state_sc[mid : mid + DH]
        memory_low, momentum_low = memory.astype(BF16), momentum.astype(BF16)
        state_low[0, lo : lo + DH] = memory_low
        state_low[0, mid : mid + DH] = momentum_low
        query = q_ref[:, lo : lo + DH]
        keep = aux_ref[:, h : h + 1]
        cross = aux_ref[:, heads + h : heads + h + 1]
        carry = aux_ref[:, 2 * heads + h : 2 * heads + h + 1]
        out = (
            intra_ref[:, lo : lo + DH]
            + keep * mm(query, memory_low, NT)
            + cross * mm(query, momentum_low, NT)
        )
        scale = lax.rsqrt(jnp.mean(out * out, -1, keepdims=True) + MEMORY_FLOOR)
        normed = out * scale
        normed_out[:, lo : lo + DH] = normed.astype(BF16)
        scales = jnp.where(lane == h, scale, scales)
        merged_out[:, lo : lo + DH] = (atts[h][...] + normed).astype(BF16)
        end = slice(rows - 1, rows)
        state_sc[lo : lo + DH] = (
            keep[end] * memory + cross[end] * momentum + part_ref[0, lo : lo + DH].astype(F32)
        )
        state_sc[mid : mid + DH] = (
            carry[end] * momentum + part_ref[0, mid : mid + DH].astype(F32)
        )
    scale_out[...] = scales


def merge(qkv, atts, intra, aux, parts, state, heads, after):
    total = qkv.shape[0]
    count = total // MBLK
    local = heads * DH
    scal = 2 * local
    at = lambda b, *_: (b, 0)
    by_block = pl.BlockSpec((1, scal, DH), lambda b, *_: (b, 0, 0))
    return call(
        functools.partial(merge_kernel, heads=heads),
        (count,),
        [pl.BlockSpec((MBLK, local), at)]
        + [pl.BlockSpec((MBLK, DH), at)] * heads
        + [pl.BlockSpec((MBLK, local), at), pl.BlockSpec((MBLK, DH), at)]
        + [by_block, whole(state.shape)],
        [
            pl.BlockSpec((MBLK, local), at),
            pl.BlockSpec((MBLK, local), at),
            pl.BlockSpec((MBLK, DH), at),
            by_block,
        ],
        [
            sds((total, local), BF16),
            sds((total, local), BF16),
            sds((total, DH), F32),
            sds((count, scal, DH), BF16),
        ],
        [pltpu.VMEM((scal, DH), F32)],
        flops=3e8,
        moved=6e6,
        after=after,
        outs="ohhh",
    )(qkv, *atts, intra, aux, parts, state)


def quarter(p, rank_ref):
    return rank_ref[0] ^ ((1 - (p >> 1)) | ((p & 1) << 1))


def middle_kernel(rank_ref, *refs):
    merged, weights = refs[:REL], refs[REL : 2 * REL]
    (
        x_ref,
        gain_ref,
        hid_out,
        normed_out,
        scale_out,
        share_out,
        mid_sc,
        merged_sc,
        weight_sc,
    ) = refs[2 * REL :]
    width = share_out.shape[1]
    local = merged[0].shape[1]

    @pl.when(pl.program_id(0) == 0)
    def _():
        for k in range(REL):
            for q in range(REL):
                weight_sc[k * local : (k + 1) * local, q * width : (q + 1) * width] = weights[k][
                    q * local : (q + 1) * local
                ]

    for k in range(REL):
        merged_sc[:, k * local : (k + 1) * local] = merged[k][...]
    middle = x_ref[...].astype(F32) + mm(merged_sc[...], weight_sc[...])
    mid_sc[...] = middle
    scale = lax.rsqrt(jnp.mean(middle * middle, -1, keepdims=True) + EPSILON)
    normed = middle * scale
    hid_out[...] = (normed * gain_ref[9:10]).astype(BF16)

    @pl.when(pl.program_id(0) == REL // 2)
    def _():
        normed_out[...] = normed
        scale_out[...] = scale

    share_out[...] = mid_sc[:, pl.ds(pl.multiple_of(rank_ref[0] * width, width), width)]


def middle(rank, merged, weights, x, gains, after):
    total, model = x.shape
    local = merged[0].shape[1]
    width = model // REL
    rows = total // REL
    at = lambda p, r: (quarter(p, r), 0)
    return call(
        middle_kernel,
        (total // rows,),
        [pl.BlockSpec((rows, local), at)] * REL
        + [pl.BlockSpec((REL * local, width), lambda *_: (total // (REL * local), 0))] * REL
        + [pl.BlockSpec((rows, model), at), whole(gains.shape)],
        [
            pl.BlockSpec((rows, model), lambda p, r: (p, 0)),
            whole((rows, model)),
            whole((rows, 1)),
            pl.BlockSpec((rows, width), at),
        ],
        [
            sds((total, model), BF16),
            sds((rows, model), F32),
            sds((rows, 1), F32),
            sds((total, width), F32),
        ],
        [
            pltpu.VMEM((rows, model), F32),
            pltpu.VMEM((rows, REL * local), BF16),
            pltpu.VMEM((REL * local, model), BF16),
        ],
        flops=2.2e9,
        moved=10e6,
        prefetch=1,
        after=after,
        ins="o" * (2 * REL) + "ho",
        outs="ohhh",
    )(rank, *merged, *weights, x, gains)


def recall_kernel(rank_ref, *refs):
    cots = refs[:REL]
    down_ref, act_out, cot_out, _ = refs[REL:]
    rank = rank_ref[0]
    width = cots[0].shape[1]
    for k in range(REL):
        span = pl.ds(pl.multiple_of((rank ^ k) * width, width), width)
        cot_out[:, span] = cots[k][...]
    act_out[...] = mm(cot_out[...], down_ref[...], NT).astype(BF16)


def recall(rank, cots, total, down, after):
    width = cots[0].shape[1]
    units, model = down.shape
    rows = total // REL
    at = lambda p, r: (p, 0)
    return call(
        recall_kernel,
        (REL,),
        [pl.BlockSpec((rows, width), lambda p, r: (quarter(p, r), 0))] * REL + [whole(down.shape)],
        [
            pl.BlockSpec((rows, units), at),
            pl.BlockSpec((rows, model), at),
            pl.BlockSpec(memory_space=pl.ANY),
        ],
        [
            sds((total, units), BF16),
            sds((total, model), BF16),
            sds((3, total, units), BF16),
        ],
        flops=1.5e9,
        moved=7e6,
        prefetch=1,
        after=after,
        outs="ohh",
    )(rank, *cots, down)


def ffn_kernel(hid_ref, grad_ref, gate_ref, _, trio_out, back_out):
    rows = back_out.shape[1]
    hidden = hid_ref[...]
    gate = mm(hidden, gate_ref[0], NT)
    up = mm(hidden, gate_ref[1], NT)
    grad_act = grad_ref[...].astype(F32)
    sig = jax.nn.sigmoid(gate)
    silu = gate * sig
    trio_out[0] = (silu * up).astype(BF16)
    grad_gate = (grad_act * up * (sig * (1.0 + gate * (1.0 - sig)))).astype(BF16)
    grad_up = (grad_act * silu).astype(BF16)
    trio_out[1] = grad_gate
    trio_out[2] = grad_up
    back = mm(grad_gate, gate_ref[0]) + mm(grad_up, gate_ref[1])
    for i in range(2):
        back_out[i] = back[i * rows : (i + 1) * rows].astype(BF16)


def ffn(hidden, grad_act, gate_up, trio, part):
    total, model = hidden.shape
    units = grad_act.shape[1]
    rows = total // REL
    at = lambda s: (part, 0)
    return call(
        ffn_kernel,
        (1,),
        [
            pl.BlockSpec((2 * rows, model), at),
            pl.BlockSpec((2 * rows, units), at),
            whole(gate_up.shape),
            pl.BlockSpec(memory_space=pl.ANY),
        ],
        [pl.BlockSpec((3, 2 * rows, units), lambda s: (0, part, 0)), whole((2, rows, model))],
        [sds((3, total, units), BF16), sds((2, rows, model), BF16)],
        flops=3e9,
        moved=8e6,
        alias={3: 0},
        ins="oooh",
        outs="hh",
        spare=10,
    )(hidden, grad_act, gate_up, trio)


def answer_kernel(rank_ref, act_ref, down_ref, send_out, far_out, keep_out):
    rank = rank_ref[0]
    width = keep_out.shape[1]
    spans = [pl.ds(pl.multiple_of((rank ^ k) * width, width), width) for k in range(REL)]
    act = act_ref[0]
    keep_out[...] = mm(act, down_ref[:, spans[0]]).astype(BF16)
    send_out[0] = mm(act, down_ref[:, spans[1]]).astype(BF16)
    far_out[...] = mm(act, down_ref[:, spans[2]]).astype(BF16)
    send_out[1] = mm(act, down_ref[:, spans[3]]).astype(BF16)


def answer(rank, trio, down, after):
    _, total, units = trio.shape
    width = down.shape[1] // REL
    rows = total // REL
    at = lambda p, r: (quarter(p, r), 0)
    return call(
        answer_kernel,
        (REL,),
        [pl.BlockSpec((1, rows, units), lambda p, r: (0, p, 0)), whole(down.shape)],
        [
            pl.BlockSpec((2, rows, width), lambda p, r: (0, quarter(p, r), 0)),
            pl.BlockSpec((rows, width), at),
            pl.BlockSpec((rows, width), at),
        ],
        [sds((2, total, width), BF16), sds((total, width), BF16), sds((total, width), BF16)],
        flops=1.5e9,
        moved=5e6,
        prefetch=1,
        after=after,
        ins="ho",
        outs="hhh",
    )(rank, trio, down)


def seats(bits):
    levels = [[0]]
    for bit in reversed(bits):
        levels.insert(0, [bit | r for level in levels for r in level])
    return levels


def deal(product, outs, bits, seat, by_rows):
    for out, level in zip(outs, seats(bits)):
        chunk = out.shape[2 if by_rows else 3]
        for slot, r in enumerate(level):
            span = pl.ds(pl.multiple_of((seat ^ r) * chunk, chunk), chunk)
            out[slot, 0] = (product[span] if by_rows else product[:, span]).astype(BF16)


def harvest_kernel(rank_ref, cot_ref, hid_ref, trio_ref, *outs, orders, by_rows):
    acc = outs[-1]
    levels = len(orders[0]) + 1
    for i, bits in enumerate(orders):

        @pl.when(pl.program_id(0) == i)
        def _():
            wide = hid_ref[...] if i else cot_ref[...]
            acc[...] = mm(wide, trio_ref[0], TN) if by_rows else mm(trio_ref[0], wide, TN)
            deal(acc, outs[i * levels : (i + 1) * levels], bits, rank_ref[1], by_rows)


def harvest(rank, cot, hidden, trio, orders, after):
    _, total, units = trio.shape
    model = cot.shape[1]
    chunk = model // 2 ** len(orders[0])
    by_rows = chunk % DH != 0
    cut = (chunk, units) if by_rows else (units, chunk)
    shapes = [(len(level), 1) + cut for bits in orders for level in seats(bits)]
    outs = call(
        functools.partial(harvest_kernel, orders=orders, by_rows=by_rows),
        (len(orders),),
        [
            whole(cot.shape),
            whole(hidden.shape),
            pl.BlockSpec((1, total, units), lambda p, r: (p, 0, 0)),
        ],
        [whole(shape) for shape in shapes],
        [sds(shape, BF16) for shape in shapes],
        [pltpu.VMEM((model, units) if by_rows else (units, model), F32)],
        flops=6 * total * model * units,
        moved=1.2e7,
        prefetch=1,
        after=after,
        ins="hoh",
        outs="h" * len(shapes),
    )(rank, cot, hidden, trio)
    levels = len(orders[0]) + 1
    return [outs[i * levels : (i + 1) * levels] for i in range(len(orders))], by_rows


def reap_kernel(rank_ref, hid_ref, gp_ref, tail_ref, back_ref, *outs, cuts):
    gp_sc, acc = outs[-2:]
    outs = outs[:-2]
    seat = rank_ref[1]
    rows = gp_ref.shape[0]
    gp_sc[...] = gp_ref[...]
    gp_sc[rows - 16 : rows] = repaired(tail_ref, back_ref)
    acc[...] = mm(hid_ref[...], gp_sc[...], TN)
    cut_rows(acc, outs, seat, cuts)


def cut_rows(acc, outs, seat, cuts):
    for bits, lo, hi in cuts:
        levels = seats(bits)
        for out, level in zip(outs, levels):
            chunk = out.shape[1]
            for slot, r in enumerate(level):
                span = pl.ds(pl.multiple_of((seat ^ r) * chunk, chunk), chunk)
                out[slot] = acc[span, lo:hi].astype(BF16)
        outs = outs[len(levels) :]


def repaired(tail_ref, back_ref):
    tail = tail_ref[...]
    return jnp.concatenate([tail[:8], tail[8:] + back_ref[...]], 0).astype(BF16)


def reap(rank, hidden, gp, tail, returned, cuts):
    total, model = hidden.shape
    columns = gp.shape[1]
    shapes = [
        (len(level), model // 2 ** len(bits), hi - lo)
        for bits, lo, hi in cuts
        for level in seats(bits)
    ]
    outs = call(
        functools.partial(reap_kernel, cuts=cuts),
        (1,),
        [whole(a.shape) for a in (hidden, gp, tail, returned)],
        [whole(shape) for shape in shapes],
        [sds(shape, BF16) for shape in shapes],
        [pltpu.VMEM((total, columns), BF16), pltpu.VMEM((model, columns), F32)],
        flops=2 * total * model * columns,
        moved=6e6,
        prefetch=1,
        ins="oooo",
    )(rank, hidden, gp, tail, returned)
    split = len(seats(cuts[0][0]))
    return outs[:split], outs[split:]


def absorb(parts, lap, got):
    parts = list(parts)
    at = 0
    for m in range(lap + 1, len(parts)):
        size = parts[m].shape[0]
        kind = F32 if m == len(parts) - 1 else BF16
        parts[m] = parts[m].astype(kind) + got[at : at + size].astype(kind)
        at += size
    return parts


def bend_kernel(rank_ref, keep_ref, near_ref, far_ref, cot_ref, normed_ref, scale_ref, gain_ref, *outs):
    low_out, dgain_out = outs
    grad = (
        keep_ref[0].astype(F32) + near_ref[0].astype(F32) + far_ref[0].astype(F32)
    )
    normed = normed_ref[...]
    total = jnp.sum(grad * normed, 0, keepdims=True)
    dgain_out[...] = jnp.where(iota(dgain_out.shape, 0) == 1, total, 0.0)
    g = grad * gain_ref[9:10]
    mean = jnp.mean(g * normed, -1, keepdims=True)
    low_out[...] = (cot_ref[...].astype(F32) + scale_ref[...] * (g - normed * mean)).astype(BF16)


def bend(rank, keep, near, far, cot, normed, scale, gains, after):
    total, model = cot.shape
    rows = total // REL
    own = lambda s, r: (REL // 2, 0)
    one = pl.BlockSpec((1, rows, model), lambda *_: (0, 0, 0))
    return call(
        bend_kernel,
        (1,),
        [
            one,
            one,
            one,
            pl.BlockSpec((rows, model), own),
            whole((rows, model)),
            whole((rows, 1)),
            whole(gains.shape),
        ],
        [whole((rows, model)), whole((8, model))],
        [sds((rows, model), BF16), sds((8, model), F32)],
        flops=5e6,
        moved=4e6,
        prefetch=1,
        after=after,
        ins="hoohhhh",
    )(rank, keep, near, far, cot, normed, scale, gains)


def turn_kernel(rank_ref, *refs, heads, bits, by_rows):
    lows = refs[:REL]
    (
        w_ref,
        q_ref,
        normed_ref,
        scale_ref,
        aux_ref,
        merged_ref,
        dev_ref,
        ga_out,
        gm_out,
        part_out,
        share_out,
        state_out,
        load_out,
        *levels_out,
        low_sc,
        acc_sc,
        state_sc,
    ) = refs[REL:]
    step = pl.program_id(0)
    last = pl.num_programs(0) - 1
    block = last - step
    rank = rank_ref[0]
    rows = q_ref.shape[0]
    scal = 2 * heads * DH
    for k in range(REL):

        @pl.when((rank ^ k) == block)
        def _():
            low_sc[...] = lows[k][...]

    @pl.when(step == 0)
    def _():
        state_sc[...] = jnp.zeros_like(state_sc)
        acc_sc[...] = jnp.zeros_like(acc_sc)

    low = low_sc[...]
    if by_rows:
        acc_sc[...] += mm(low, merged_ref[...], TN)
    else:
        acc_sc[...] += mm(merged_ref[...], low, TN)
    width = share_out.shape[1]
    share_out[...] = low_sc[:, pl.ds(pl.multiple_of(rank * width, width), width)]
    grad_merged = mm(low, w_ref[...], NT)
    ga_out[...] = grad_merged.astype(BF16)
    end = slice(rows - 1, rows)
    for h in range(heads):
        lo, mid = h * DH, (heads + h) * DH
        g = grad_merged[:, lo : lo + DH]
        normed = normed_ref[:, lo : lo + DH].astype(F32)
        scale = scale_ref[:, h : h + 1]
        grad = scale * (g - normed * jnp.mean(g * normed, -1, keepdims=True))
        gm_out[:, lo : lo + DH] = grad.astype(BF16)
        query = q_ref[:, lo : lo + DH]
        keep = aux_ref[:, h : h + 1]
        cross = aux_ref[:, heads + h : heads + h + 1]
        carry = aux_ref[:, 2 * heads + h : 2 * heads + h + 1]
        mem_part = mm((keep * grad).astype(BF16), query, TN)
        mom_part = mm((cross * grad).astype(BF16), query, TN)
        part_out[0, lo : lo + DH] = mem_part.astype(BF16)
        part_out[0, mid : mid + DH] = mom_part.astype(BF16)
        memory, momentum = state_sc[lo : lo + DH], state_sc[mid : mid + DH]
        state_sc[lo : lo + DH] = keep[end] * memory + mem_part
        state_sc[mid : mid + DH] = cross[end] * memory + carry[end] * momentum + mom_part

    @pl.when(step == last)
    def _():
        state_sc[scal : scal + 8] = dev_ref[scal : scal + 8]
        state_out[...] = state_sc[...]
        pack_load(load_out, state_sc[...], scal)
        seat = rank_ref[1]
        for out, level in zip(levels_out, seats(bits)):
            chunk = out.shape[1 if by_rows else 2]
            for slot, r in enumerate(level):
                span = pl.ds(pl.multiple_of((seat ^ r) * chunk, chunk), chunk)
                out[slot] = (acc_sc[span] if by_rows else acc_sc[:, span]).astype(BF16)


def turn(rank, lows, weight, qkv, normed, scales, aux, merged, dev, bits, heads):
    total = qkv.shape[0]
    count = total // MBLK
    local, model = weight.shape
    width = model // REL
    scal = 2 * local
    at = lambda b, *_: (count - 1 - b, 0)
    chunk = model // 2 ** len(bits)
    by_rows = chunk % DH != 0
    cut = (chunk, local) if by_rows else (local, chunk)
    levels = [(len(level),) + cut for level in seats(bits)]
    out = call(
        functools.partial(turn_kernel, heads=heads, bits=bits, by_rows=by_rows),
        (count,),
        [whole(lows[0].shape)] * REL
        + [
            whole(weight.shape),
            pl.BlockSpec((MBLK, local), at),
            pl.BlockSpec((MBLK, local), at),
            pl.BlockSpec((MBLK, DH), at),
            pl.BlockSpec((MBLK, DH), at),
            pl.BlockSpec((MBLK, local), at),
            whole(dev.shape),
        ],
        [
            pl.BlockSpec((MBLK, local), at),
            pl.BlockSpec((MBLK, local), at),
            pl.BlockSpec((1, scal, DH), lambda b, *_: (count - 1 - b, 0, 0)),
            pl.BlockSpec((MBLK, width), at),
            whole((scal + 8, DH)),
            whole((scal + 16, DH)),
        ]
        + [whole(shape) for shape in levels],
        [
            sds((total, local), BF16),
            sds((total, local), BF16),
            sds((count, scal, DH), BF16),
            sds((total, width), BF16),
            sds((scal + 8, DH), F32),
            sds((scal + 16, DH), BF16),
        ]
        + [sds(shape, BF16) for shape in levels],
        [
            pltpu.VMEM((MBLK, model), BF16),
            pltpu.VMEM((model, local) if by_rows else (local, model), F32),
            pltpu.VMEM((scal + 8, DH), F32),
        ],
        flops=8e8,
        moved=8e6,
        prefetch=1,
        ins="o" * (REL + 2) + "hhooo",
        outs="ooohoo" + "o" * len(levels),
    )(rank, *lows, weight, qkv, normed, scales, aux, merged, dev)
    return out[:6], out[6:], by_rows


def settle_kernel(qkv_ref, *refs, heads):
    rests = refs[: 3 * heads]
    (
        within_ref,
        gm_ref,
        aux_ref,
        low_ref,
        part_ref,
        state_ref,
        proj_ref,
        halo_ref,
        conv_ref,
        gp_out,
        tail_out,
        head_out,
        gconv_out,
        _,
        _,
        _,
        state_sc,
        mix_sc,
        tap_sc,
        proj_sc,
    ) = refs[3 * heads :]
    step = pl.program_id(0)
    last = pl.num_programs(0) - 1
    block = last - step
    rows = qkv_ref.shape[0]
    local = heads * DH
    base = block * rows

    @pl.when(step == 0)
    def _():
        state_sc[...] = state_ref[0 : state_sc.shape[0]]
        tap_sc[...] = jnp.zeros_like(tap_sc)
        gconv_out[...] = jnp.zeros_like(gconv_out)

    end = slice(rows - 1, rows)
    for h in range(heads):
        lo, mid = h * DH, (heads + h) * DH
        memory, momentum = state_sc[lo : lo + DH], state_sc[mid : mid + DH]
        memory_low, momentum_low = memory.astype(BF16), momentum.astype(BF16)
        keep = aux_ref[:, h : h + 1]
        cross = aux_ref[:, heads + h : heads + h + 1]
        carry = aux_ref[:, 2 * heads + h : 2 * heads + h + 1]
        end_kernel = aux_ref[:, 3 * heads + h : 3 * heads + h + 1]
        end_carry = aux_ref[:, 4 * heads + h : 4 * heads + h + 1]
        keys = qkv_ref[:, local + lo : local + lo + DH]
        values = qkv_ref[:, 2 * local + lo : 2 * local + lo + DH]
        gmem = gm_ref[:, lo : lo + DH]
        both = lambda a, one, two: jnp.concatenate(
            [a.astype(F32) * one, a.astype(F32) * two], 1
        ).astype(BF16)
        states = jnp.concatenate([low_ref[0, lo : lo + DH], low_ref[0, mid : mid + DH]], 0)
        ends = jnp.concatenate([memory_low, momentum_low], 0)
        wide = jnp.concatenate([memory_low, momentum_low], 1)
        dq = mm(both(gmem, keep, cross), states)
        dk = mm(both(values, end_kernel, end_carry), ends)
        dv = mm(both(keys, end_kernel, end_carry), wide, NT)
        for c, extra in enumerate((dq, dk, dv)):
            mix_sc[:, c * local + lo : c * local + lo + DH] = (
                rests[c * heads + h][...]
                + within_ref[:, c * local + lo : c * local + lo + DH]
                + extra
            )
        state_sc[lo : lo + DH] = keep[end] * memory + part_ref[0, lo : lo + DH].astype(F32)
        state_sc[mid : mid + DH] = (
            cross[end] * memory
            + carry[end] * momentum
            + part_ref[0, mid : mid + DH].astype(F32)
        )
    before = proj_ref[pl.ds(pl.multiple_of(jnp.maximum(base - 16, 0), 16), 16)].astype(F32)[8:16]
    proj_sc[0:8] = jnp.where(block == 0, halo_ref[...], before)
    proj_sc[8 : 8 + rows] = proj_ref[pl.ds(pl.multiple_of(base, rows), rows)].astype(F32)
    place = base + iota((rows, 1), 0)
    starts = aux_ref[:, START_AT : START_AT + 1].astype(jnp.int32)
    mix = mix_sc[...]
    total = conv_ref[0:1] * mix
    gconv_out[0:1] += jnp.sum(mix * proj_sc[8 : 8 + rows], 0, keepdims=True)
    for j in range(1, KW):
        tap_sc[j - 1, 8 + rows : 16 + rows] = tap_sc[j - 1, 8:16]
        tap = mix * (place - j >= starts).astype(F32)
        tap_sc[j - 1, 8 : 8 + rows] = conv_ref[j : j + 1] * tap
        gconv_out[j : j + 1] += jnp.sum(tap * proj_sc[8 - j : 8 - j + rows], 0, keepdims=True)
        total = total + tap_sc[j - 1, 8 + j : 8 + j + rows]
    gp_out[...] = total.astype(BF16)

    @pl.when(step == 0)
    def _():
        tail_out[...] = total[rows - 16 : rows]

    @pl.when(step == last)
    def _():
        head_out[...] = tap_sc[0, 1:9] + tap_sc[1, 2:10] + tap_sc[2, 3:11]


def settle(qkv, grads, inner, gm, aux, lows, parts, state, proj, halo, conv, width, heads):
    total = qkv.shape[0]
    count = total // MBLK
    local = heads * DH
    scal = 2 * local
    at = lambda b, *_: (count - 1 - b, 0)
    by_block = pl.BlockSpec((1, scal, DH), lambda b, *_: (count - 1 - b, 0, 0))
    return call(
        functools.partial(settle_kernel, heads=heads),
        (count,),
        [pl.BlockSpec((MBLK, 3 * local), at)]
        + [pl.BlockSpec((MBLK, DH), at)] * (3 * heads)
        + [
            pl.BlockSpec((MBLK, 3 * local), at),
            pl.BlockSpec((MBLK, local), at),
            pl.BlockSpec((MBLK, DH), at),
            by_block,
            by_block,
            whole(state.shape),
            whole(proj.shape),
            whole(halo.shape),
            whole(conv.shape),
        ],
        [
            pl.BlockSpec((MBLK, 3 * local), at),
            whole((16, 3 * local)),
            whole((8, 3 * local)),
            whole((8, 3 * local)),
        ]
        + [pl.BlockSpec(memory_space=pl.ANY)] * 3,
        [
            sds((total, 3 * local), BF16),
            sds((16, 3 * local), F32),
            sds((8, 3 * local), F32),
            sds((8, 3 * local), F32),
            sds((2, total, width), BF16),
            sds((total, width), BF16),
            sds((total, width), BF16),
        ],
        [
            pltpu.VMEM((scal, DH), F32),
            pltpu.VMEM((MBLK, 3 * local), F32),
            pltpu.VMEM((KW - 1, MBLK + 16, 3 * local), F32),
            pltpu.VMEM((MBLK + 8, 3 * local), F32),
        ],
        flops=6e8,
        moved=14e6,
        ins="o" + "h" * (3 * heads) + "ooohoohoo",
        outs="oooohhh",
    )(qkv, *grads, inner, gm, aux, lows, parts, state, proj, halo, conv)


def back_kernel(
    rank_ref,
    gp_ref,
    tail_ref,
    back_ref,
    w_ref,
    x_ref,
    gain_ref,
    other_ref,
    send_in,
    far_in,
    keep_in,
    send_out,
    far_out,
    keep_out,
    dgain_out,
    grad_sc,
    gp_sc,
    w_sc,
    *,
    last,
):
    rank = rank_ref[0]
    width = keep_out.shape[1]
    local = w_ref.shape[2]

    @pl.when(pl.program_id(0) == 0)
    def _():
        dgain_out[...] = other_ref[...]
        for c in range(3):
            w_sc[:, c * local : (c + 1) * local] = w_ref[c]

    rows = gp_ref.shape[0]
    gp_sc[...] = gp_ref[...]
    if last:
        gp_sc[rows - 16 : rows] = repaired(tail_ref, back_ref)
    grad = mm(gp_sc[...], w_sc[...], NT)
    x = x_ref[...].astype(F32)
    scale = lax.rsqrt(jnp.mean(x * x, -1, keepdims=True) + EPSILON)
    normed = x * scale
    dgain_out[0:1] += jnp.sum(grad * normed, 0, keepdims=True)
    g = grad * gain_ref[8:9]
    grad_sc[...] = (scale * (g - normed * jnp.mean(g * normed, -1, keepdims=True))).astype(BF16)
    spans = [pl.ds(pl.multiple_of((rank ^ k) * width, width), width) for k in range(REL)]
    keep_out[...] = grad_sc[:, spans[0]]
    send_out[0] = grad_sc[:, spans[1]]
    far_out[...] = grad_sc[:, spans[2]]
    send_out[1] = grad_sc[:, spans[3]]


def back(rank, gp, tail, returned, weight, x, gains, dgain, rooms, last, after):
    total, model = x.shape
    width = model // REL
    count = total // MBLK
    first = count - 1 if last else 0
    at = lambda b, *_: (b + first, 0)
    columns = gp.shape[1]
    return call(
        functools.partial(back_kernel, last=last),
        (1 if last else count - 1,),
        [
            pl.BlockSpec((MBLK, columns), at),
            whole(tail.shape),
            whole(returned.shape),
            whole(weight.shape),
            pl.BlockSpec((MBLK, model), at),
            whole(gains.shape),
            whole(dgain.shape),
        ]
        + [pl.BlockSpec(memory_space=pl.ANY)] * 3,
        [
            pl.BlockSpec((2, MBLK, width), lambda b, *_: (0, b + first, 0)),
            pl.BlockSpec((MBLK, width), at),
            pl.BlockSpec((MBLK, width), at),
            whole((8, model)),
        ],
        [
            sds((2, total, width), BF16),
            sds((total, width), BF16),
            sds((total, width), BF16),
            sds((8, model), F32),
        ],
        [
            pltpu.VMEM((MBLK, model), BF16),
            pltpu.VMEM((MBLK, columns), BF16),
            pltpu.VMEM((model, columns), BF16),
        ],
        flops=4e8 if last else 1.3e9,
        moved=2e6 if last else 6e6,
        prefetch=1,
        after=after,
        alias={7: 0, 8: 1, 9: 2},
        ins="oooohoohhh",
        outs="hhho",
    )(rank, gp, tail, returned, weight, x, gains, dgain, *rooms)


def wrap_kernel(little_ref, got_ref, one_out, two_out, conv_out, fixed_out):
    total = little_ref[...] + got_ref[...]
    one_out[...] = total[0:1]
    two_out[...] = total[1:2]
    taps, parts, _ = conv_out.shape
    for j in range(taps):
        conv_out[j] = total[2 + parts * j : 2 + parts * (j + 1)]
    rest = 2 + taps * parts
    rows = fixed_out.shape[1]
    for c in range(fixed_out.shape[0]):
        fixed_out[c] = total[rest + c * rows : rest + (c + 1) * rows]


def wrap(little, got, fixed_count):
    local = little.shape[1]
    shapes = [(1, local), (1, local), (KW, 3, local), (2, fixed_count, local)]
    return call(
        wrap_kernel,
        (1,),
        [whole(little.shape)] * 2,
        [whole(shape) for shape in shapes],
        [sds(shape, F32) for shape in shapes],
        moved=1e5,
    )(little, got)


def lay_kernel(own_ref, got_ref, last_ref, out_ref):
    local = out_ref.shape[2]
    both = own_ref[0] + got_ref[0].astype(F32)
    for c in range(2):
        out_ref[c] = both[:, c * local : (c + 1) * local]
    out_ref[2] = last_ref[0]


def lay(own, got, last):
    _, rows, columns = last.shape
    return call(
        lay_kernel,
        (1,),
        [whole(own.shape), whole(got.shape), whole(last.shape)],
        [whole((3, rows, columns))],
        [sds((3, rows, columns), F32)],
        moved=1e6,
    )(own, got, last)[0]


def per_device(
    inputs,
    cotangent,
    norm_gain,
    qkv_weight,
    conv_kernel,
    persistent,
    out_weight,
    ffn_gain,
    gate_up,
    down_weight,
    memory_decay,
    momentum_decay,
    doc_start,
):
    total, width = inputs.shape
    local = qkv_weight.shape[2]
    heads = local // DH
    model = width * REL
    rank = jnp.stack([lax.axis_index("head"), lax.axis_index("seq")]).astype(jnp.int32)
    conv = conv_kernel.reshape(KW, 3 * local)

    kmat, aux = prepare(rank, doc_start.reshape(1, total), memory_decay.T, momentum_decay.T)
    columns = out_weight.reshape(local, REL, width).transpose(1, 0, 2).reshape(-1, width)
    pair = jnp.concatenate([cotangent, columns], 0)
    small = pack(shifted(inputs[total - 8 :], "seq", 1), norm_gain, ffn_gain, ())
    smalls = gather_rel(small)
    blocks = gather_rel(inputs, beside=(kmat, smalls[2]))
    pair_far = swap(hold(pair, blocks[2], smalls[2]), "head", 2)

    (
        x,
        hidden_one,
        proj,
        qkv,
        parts,
        halo,
        gains,
        dev_state,
        load,
    ) = front(
        rank,
        blocks,
        smalls,
        qkv_weight,
        conv,
        aux,
        heads,
    )

    ahead = []

    def attend_head(sent):
        ahead.append(attend(qkv, persistent, aux, len(ahead), heads, (sent,)))
        return ahead[-1][:1]

    def inside_blocks(sent):
        ahead.append(within(qkv, kmat, (sent,)))
        return ahead[-1:]


    prefix = entering(
        rank, load, dev_state, heads, False, [attend_head] * heads + [inside_blocks]
    )
    intra = ahead.pop()
    atts, ratios, probs, fixps = zip(*ahead)
    pair_far = hold(pair_far, prefix)
    pairs = [pair, swap(pair, "head", 1), pair_far, swap(pair_far, "head", 1)]
    merged, normed_mem, mem_scales, state_lows = merge(
        qkv, atts, intra, aux, parts, prefix, heads, ()
    )
    grad_act, cot, trio = recall(rank, pairs, total, down_weight, (merged,))
    merged_rel = gather_rel(merged, beside=(grad_act,))
    hidden_two, normed_two, scale_two, middle_share = middle(
        rank, merged_rel, pairs, x, gains, (grad_act,)
    )
    gate_weights = gate_up.transpose(0, 2, 1)
    trio, send = ffn(hidden_two, grad_act, gate_weights, trio, 0)
    trio, rest = ffn(hidden_two, grad_act, gate_weights, trio, 1)
    places = lax.axis_size("seq")
    bits = tuple(2**i for i in range((places - 1).bit_length()))
    laps = len(bits)
    turned = bits[1:] + bits[:1]

    near = hold(swap(send, "head", 1), rest)
    half = rest[1:2] + near[1:2]
    turned = bits[1:] + bits[:1]
    ffn_levels, ffn_rows = harvest(
        rank, cot, hidden_two, trio, (turned, bits, bits), (half,)
    )
    far_sum = hold(swap(half, "head", 2), ffn_levels[-1][-1])
    (down, gate, up), _ = lax.optimization_barrier((ffn_levels, far_sum))
    low_own, dgain_two = bend(
        rank, rest, near, far_sum, cot, normed_two, scale_two, gains, ()
    )
    ans_send, ans_far, ans_keep = answer(rank, trio, down_weight, (low_own,))
    down = absorb(down, 0, hold(swap(down[0], "seq", turned[0]), ans_keep))
    lows = gather_rel(low_own, beside=(ans_keep, *down[1:]))

    (grad_att, grad_mem, mem_parts, low_share, back_state, back_load), three, by_rows = turn(
        rank,
        lows,
        out_weight,
        qkv,
        normed_mem,
        mem_scales,
        aux,
        merged,
        dev_state,
        bits,
        heads,
    )
    pieces, extra = [], {"three": three, "down": down, "gate": gate, "up": up}

    def later(name, lap, mark):
        extra[name] = list(extra[name])
        extra[name][lap] = hold(extra[name][lap], mark)


    def exchanged(name, lap, mark):
        order = turned if name == "down" else bits
        got = hold(swap(extra[name][lap], "seq", order[lap]), mark)
        extra[name] = absorb(extra[name], lap, got)
        return extra[name][lap + 1 :]

    def attend_back_head(sent):
        h = len(pieces)
        pieces.append(
            attend_back(
                qkv, persistent, probs[h], fixps[h], ratios[h], grad_att, h, heads, (sent,)
            )
        )
        if h == 0:
            return [pieces[-1][3], *exchanged("gate", 0, sent)]
        later("gate", 1, sent)
        later("up", 0, sent)
        extra["ans_near"] = hold(swap(ans_send, "head", 1), sent)
        extra["ans_half"] = ans_far + extra["ans_near"][1]
        return [
            pieces[-1][3],
            extra["ans_half"],
            *exchanged("down", 1, sent),
            *exchanged("three", 0, sent),
        ]

    def back_inside(sent):
        extra["inner"] = within_back(qkv, kmat, grad_mem, (sent,))
        extra["ans_sum"] = swap(extra["ans_half"], "head", 2)
        return [
            extra["inner"],
            extra["ans_sum"],
            *exchanged("three", 1, sent),
        ]

    suffix = entering(
        rank, back_load, back_state, heads, True, [attend_back_head] * heads + [back_inside]
    )
    inner = extra["inner"]
    suffix = hold(suffix, *exchanged("gate", 1, suffix), *exchanged("up", 0, suffix))
    gp, tail, head_rows, gconv, *rooms = settle(
        qkv,
        [pieces[h][c] for c in range(3) for h in range(heads)],
        inner,
        grad_mem,
        aux,
        state_lows,
        mem_parts,
        suffix,
        proj,
        halo,
        conv,
        width,
        heads,
    )
    returned = shifted(head_rows, "seq", -1)
    for lap in range(2, laps):
        exchanged("three", lap, gp)
        exchanged("down", lap, gp)
        exchanged("gate", lap, gp)
    exchanged("up", 1, gp)
    three, down = extra["three"], extra["down"]
    ans_near, ans_sum = extra["ans_near"], extra["ans_sum"]
    *rooms, dgain = back(
        rank, gp, tail, head_rows, qkv_weight, x, gains, dgain_two, rooms, False, (head_rows,)
    )
    returned = hold(returned, three[-1], down[-1], extra["gate"][-1], extra["up"][2], dgain)
    one, two = reap(
        rank,
        hidden_one,
        gp,
        tail,
        returned,
        ((bits, 0, 2 * local), (turned, 2 * local, 3 * local)),
    )
    bsend, bfar, bkeep, dgain = back(
        rank, gp, tail, returned, qkv_weight, x, gains, dgain, rooms, True, (two[-1],)
    )

    def take(x, mark, axis, bit):
        return hold(swap(x, axis, bit), *mark)

    gain_half = dgain + swap(dgain, "head", 1)
    bnear = take(bsend, (gain_half,), "head", 1)
    bhalf = bfar + bnear[1]
    output = (
        middle_share
        + ans_keep.astype(F32)
        + ans_near[0].astype(F32)
        + hold(ans_sum, bhalf).astype(F32)
    ).astype(BF16)
    two = absorb(two, 0, take(two[0], (output,), "seq", turned[0]))
    gain_sums = gain_half + take(gain_half, (two[1],), "head", 2)
    gain_own = lax.dynamic_slice_in_dim(
        gain_sums, lax.axis_index("head") * width, width, 1
    )
    fixed_count = persistent.shape[1]
    little = jnp.concatenate(
        [
            gain_own[:2],
            gconv[:KW].reshape(3 * KW, local),
            jnp.concatenate([p[3] for p in pieces], -1).reshape(2 * fixed_count, local),
        ],
        0,
    )
    one = absorb(one, 0, take(one[0], (little,), "seq", bits[0]))
    mark = (one[1],)
    for lap in range(1, laps):
        little = little + take(little, mark, "seq", bits[lap - 1])
        two = absorb(two, lap, take(two[lap], (little,), "seq", turned[lap]))
        mark = (two[lap + 1],)
        if lap + 1 < laps:
            one = absorb(one, lap, take(one[lap], mark, "seq", bits[lap]))
            mark = (one[lap + 1],)
    for lap in range(2, laps):
        exchanged("up", lap, mark[0])
    flip = (lambda a: a.transpose(0, 2, 1)) if ffn_rows else (lambda a: a)
    grad_down = flip(down[-1][0])[0]
    grad_gate_up = flip(jnp.concatenate([extra["gate"][-1][0], extra["up"][-1][0]], 0))
    grad_gate_up = grad_gate_up.transpose(0, 2, 1)
    mark = (grad_gate_up,)
    input_grad = (
        bkeep.astype(F32)
        + bnear[0].astype(F32)
        + take(bhalf, mark, "head", 2).astype(F32)
        + low_share.astype(F32)
    )
    got = take(little, (input_grad,), "seq", bits[-1])
    gain_one, gain_two, grad_conv, grad_fixed = wrap(little, got, fixed_count)
    got = take(one[-2], (grad_conv,), "seq", bits[-1])
    grad_qkv = lay(one[-1], got, two[-1])
    grad_out = three[-1][0].T if by_rows else three[-1][0]
    return (
        output,
        input_grad,
        gain_one[0],
        grad_qkv,
        grad_conv,
        grad_fixed,
        grad_out,
        gain_two[0],
        grad_gate_up,
        grad_down,
    )


def solution(mesh):
    placed = (
        P("seq", "head"),
        P("seq", "head"),
        P("head"),
        P(None, None, "head"),
        P(None, None, "head"),
        P(None, None, "head"),
        P("head", None),
        P("head"),
        P(None, None, "head"),
        P("head", None),
        P("seq", "head"),
        P("seq", "head"),
        P("seq"),
    )
    return jax.shard_map(
        per_device,
        mesh=mesh,
        in_specs=placed,
        out_specs=(
            P("seq", "head"),
            P("seq", "head"),
            P("head"),
            P(None, "seq", "head"),
            P(None, None, "head"),
            P(None, None, "head"),
            P("head", "seq"),
            P("head"),
            P(None, "seq", "head"),
            P("head", "seq"),
        ),
        check_vma=False,
    )
```

```python
import functools

import jax
import jax.numpy as jnp
from jax import lax
from jax.experimental import pallas as pl
from jax.experimental.pallas import tpu as pltpu
from jax.sharding import PartitionSpec as P

DH = 128
KW = 4
SEG = 1024
MBLK = 256
EPSILON = 1e-06
MEMORY_FLOOR = 64.0
MASKED = -1e30
F32 = jnp.float32
BF16 = jnp.bfloat16
NN = (((1,), (0,)), ((), ()))
NT = (((1,), (1,)), ((), ()))
TN = (((0,), (0,)), ((), ()))
REL = 4
START_AT = 126


def mm(a, b, dims=NN):
    return lax.dot_general(a, b, dims, preferred_element_type=F32)


def exact(a, b, dims=NN):
    return lax.dot_general(
        a, b, dims, precision=lax.Precision.HIGHEST, preferred_element_type=F32
    )


def padded(shape, dtype):
    size = jnp.dtype(dtype).itemsize
    tile = 32 // size
    if len(shape) == 1:
        return -(-shape[0] // 1024) * 1024 * 4
    total = size * -(-shape[-1] // 128) * 128 * (-(-shape[-2] // tile) * tile)
    for n in shape[:-2]:
        total *= n
    return total


def call(
    kernel,
    grid,
    in_specs,
    out_specs,
    out_shape,
    scratch=(),
    flops=0,
    moved=0,
    prefetch=0,
    after=(),
    ins="",
    outs="",
    alias={},
    spare=5,
):
    taken = prefetch + len(in_specs)
    waits = len(after)

    def body(*refs):
        kernel(*refs[:taken], *refs[taken + waits :])

    spaces = {"v": pltpu.VMEM, "h": pltpu.HBM}
    results = out_shape if isinstance(out_shape, (list, tuple)) else [out_shape]
    out_blocks = out_specs if isinstance(out_specs, (list, tuple)) else [out_specs]
    held = sum(
        2 * padded(b.block_shape, s.dtype) for b, s in zip(out_blocks, results) if b.block_shape
    )
    held += sum(padded(m.shape, m.dtype) for m in scratch)
    if outs:
        out_shape = [
            spaces[c](s.shape, s.dtype) if c in spaces else s for c, s in zip(outs, results)
        ]
        assert len(outs) == len(results)

    spec = pltpu.PrefetchScalarGridSpec(
        num_scalar_prefetch=prefetch,
        grid=grid,
        in_specs=list(in_specs) + [pl.BlockSpec(memory_space=pl.ANY)] * waits,
        out_specs=out_specs,
        scratch_shapes=list(scratch),
    )

    def run(*operands):
        taking = held + sum(
            2 * padded(b.block_shape, a.dtype)
            for b, a in zip(in_specs, operands[prefetch:])
            if b.block_shape
        )
        made = pl.pallas_call(
            body,
            grid_spec=spec,
            out_shape=out_shape,
            input_output_aliases={prefetch + i: o for i, o in alias.items()},
            compiler_params=pltpu.CompilerParams(
                vmem_limit_bytes=min(taking + spare * 2**20, 24 * 2**20)
            ),
            cost_estimate=pl.CostEstimate(
                flops=int(flops), bytes_accessed=int(moved), transcendentals=0
            ),
        )
        if ins:
            assert len(ins) == len(operands) - prefetch
            operands = operands[:prefetch] + tuple(
                pltpu.with_memory_space_constraint(a, spaces[c]) if c in spaces else a
                for c, a in zip(ins, operands[prefetch:])
            )
        return made(*operands, *after)

    return run


def whole(shape):
    return pl.BlockSpec(shape, lambda *_: (0,) * len(shape))


def sds(shape, dtype):
    return jax.ShapeDtypeStruct(shape, dtype)


def iota(shape, dim):
    return lax.broadcasted_iota(jnp.int32, shape, dim)


def swap(x, axis, bit):
    count = lax.axis_size(axis)
    return lax.ppermute(x, axis, [(i, i ^ bit) for i in range(count)])


def shifted(x, axis, by):
    count = lax.axis_size(axis)
    return lax.ppermute(x, axis, [(i, i + by) for i in range(count) if 0 <= i + by < count])


def hold(x, *others):
    return lax.optimization_barrier((x, *others))[0]


def gather_rel(x, beside=(), before=()):
    far = swap(hold(x, *before) if before else x, "head", 2)
    near = swap(x, "head", 1)
    far = hold(far, *beside) if beside else far
    return [x, near, far, swap(far, "head", 1)]


def pack_kernel(halo_ref, one_ref, two_ref, out_ref):
    width = halo_ref.shape[1]
    rows = [
        halo_ref[...].astype(F32),
        one_ref[...].astype(F32).reshape(1, width),
        two_ref[...].astype(F32).reshape(1, width),
        jnp.zeros((6, width), F32),
    ]
    out_ref[...] = jnp.concatenate(rows, 0).astype(BF16)


def pack(halo, one, two, after):
    return call(
        pack_kernel,
        (1,),
        [whole(halo.shape), whole(one.shape), whole(two.shape)],
        whole((16, halo.shape[1])),
        sds((16, halo.shape[1]), BF16),
        moved=1e4,
        after=after,
        ins="hhh",
    )(halo, one, two)


def prepare_kernel(rank_ref, doc_ref, keep_ref, carry_ref, kmat_out, aux_out, *, heads):
    rows = doc_ref.shape[1]
    base = pl.program_id(0) * rows
    below = iota((rows, rows), 0)
    right = iota((rows, rows), 1)
    local_start = doc_ref[...] - rank_ref[1] * (rows * pl.num_programs(0))
    by_row = jnp.concatenate(
        [
            jnp.log(keep_ref[...]),
            jnp.log(carry_ref[...]),
            local_start.astype(F32),
            jnp.zeros((7 - 2 * heads, rows), F32),
        ],
        0,
    )
    first = by_row.astype(BF16).astype(F32)
    second = (by_row - first).astype(BF16).astype(F32)
    third = by_row - first - second
    split = jnp.concatenate([first, second, third, jnp.zeros((8, rows), F32)], 0).astype(BF16)
    upto = (right <= below).astype(BF16)
    same = (right == below).astype(BF16)
    rows_sum = mm(split, (below <= right).astype(BF16))
    rows_sum = rows_sum[0:8] + rows_sum[8:16] + rows_sum[16:24]
    cols_sum = mm(upto, split, NT)
    cols_sum = cols_sum[:, 0:8] + cols_sum[:, 8:16] + cols_sum[:, 16:24]
    at = 2 * heads
    starts = mm(same, split, NT)
    starts = starts[:, at : at + 1] + starts[:, at + 8 : at + 9] + starts[:, at + 16 : at + 17]
    start_at = starts.astype(jnp.int32)
    linked = (right <= below) & (base + right >= start_at)
    fresh = start_at < base
    reaches_end = base + iota((rows, 1), 0) >= start_at[rows - 1 : rows]
    lane = iota((rows, DH), 1)
    aux = jnp.where(lane == START_AT, starts, 0.0)
    for h in range(heads):
        keep_col, keep_row = cols_sum[:, h : h + 1], rows_sum[h : h + 1]
        carry_col = cols_sum[:, heads + h : heads + h + 1]
        carry_row = rows_sum[heads + h : heads + h + 1]
        keep_mat = jnp.where(linked, jnp.exp(jnp.minimum(keep_col - keep_row, 0.0)), 0.0)
        carry_mat = jnp.where(linked, jnp.exp(jnp.minimum(carry_col - carry_row, 0.0)), 0.0)
        keep_low = keep_mat.astype(BF16)
        kernel = mm(keep_low, carry_mat.astype(BF16))
        kmat_out[h, 0] = kernel.astype(BF16)
        keep_weight = jnp.where(fresh, jnp.exp(keep_col), 0.0)
        carried = jnp.where(fresh, jnp.exp(carry_col), 0.0)
        cross = mm(keep_low, jnp.broadcast_to(carried, (rows, DH)).astype(BF16))
        last = jnp.broadcast_to(kernel[rows - 1 : rows], (16, rows)).astype(BF16)
        end_kernel = mm(same, last, NT)[:, 0:1]
        end_carry = jnp.where(
            reaches_end, jnp.exp(jnp.minimum(carry_col[rows - 1 : rows] - carry_col, 0.0)), 0.0
        )
        for slot, column in enumerate((keep_weight, cross, carried, end_kernel, end_carry)):
            aux = jnp.where(lane == slot * heads + h, column, aux)
    aux_out[...] = aux


def prepare(rank, doc, keep, carry):
    heads, total = keep.shape
    count = total // MBLK
    by_token = lambda n: pl.BlockSpec((n, MBLK), lambda b, *_: (0, b))
    return call(
        functools.partial(prepare_kernel, heads=heads),
        (count,),
        [by_token(1), by_token(heads), by_token(heads)],
        [
            pl.BlockSpec((heads, 1, MBLK, MBLK), lambda b, *_: (0, b, 0, 0)),
            pl.BlockSpec((MBLK, DH), lambda b, *_: (b, 0)),
        ],
        [sds((heads, count, MBLK, MBLK), BF16), sds((total, DH), F32)],
        flops=4e8,
        moved=2e6,
        prefetch=1,
        ins="hhh",
    )(rank, doc, keep, carry)


def front_kernel(rank_ref, *refs, heads):
    blocks, smalls = refs[:REL], refs[REL : 2 * REL]
    (
        w_ref,
        conv_ref,
        aux_ref,
        x_out,
        hid_out,
        proj_out,
        qkv_out,
        part_out,
        halo_out,
        gain_out,
        state_out,
        load_out,
        small_sc,
        proj_sc,
        state_sc,
    ) = refs[2 * REL :]
    b = pl.program_id(0)
    rank = rank_ref[0]
    rows, width = blocks[0].shape
    local = heads * DH
    spans = [pl.ds(pl.multiple_of((rank ^ k) * width, width), width) for k in range(REL)]
    for k in range(REL):
        x_out[:, spans[k]] = blocks[k][...]
    scal = 2 * heads * DH

    @pl.when(b == 0)
    def _():
        for k in range(REL):
            small_sc[:, spans[k]] = smalls[k][...]
        small = small_sc[...].astype(F32)
        gain_out[...] = small
        scale = lax.rsqrt(jnp.mean(small * small, -1, keepdims=True) + EPSILON)
        hidden = (small * scale * small[8:9]).astype(BF16)
        for c in range(3):
            proj_sc[0:8, c * local : (c + 1) * local] = mm(hidden, w_ref[c])[0:8]
        halo_out[...] = proj_sc[0:8]
        state_sc[0:scal] = jnp.zeros((scal, DH), F32)
        row = iota((8, DH), 0)
        state_sc[scal : scal + 8] = jnp.where(
            (row < heads) | ((row >= 2 * heads) & (row < 3 * heads)), 1.0, 0.0
        ).astype(F32)

    gain = gain_out[8:9]
    x = x_out[...].astype(F32)
    scale = lax.rsqrt(jnp.mean(x * x, -1, keepdims=True) + EPSILON)
    hidden = (x * scale * gain).astype(BF16)
    hid_out[...] = hidden
    for c in range(3):
        proj_sc[8 : 8 + rows, c * local : (c + 1) * local] = mm(hidden, w_ref[c])
    place = b * rows + iota((rows, 1), 0)
    starts = aux_ref[:, START_AT : START_AT + 1].astype(jnp.int32)
    mixed = jnp.zeros((rows, 3 * local), F32)
    for j in range(KW):
        inside = (place - j >= starts).astype(F32)
        mixed = mixed + conv_ref[j : j + 1] * proj_sc[8 - j : 8 - j + rows] * inside
    rounded = mixed.astype(BF16)
    qkv_out[...] = rounded
    proj_out[...] = proj_sc[8 : 8 + rows].astype(BF16)
    proj_sc[0:8] = proj_sc[rows : rows + 8]
    end = slice(rows - 1, rows)
    for h in range(heads):
        column = lambda slot: aux_ref[:, slot * heads + h : slot * heads + h + 1]
        keys = rounded[:, local + h * DH : local + (h + 1) * DH]
        values = rounded[:, 2 * local + h * DH : 2 * local + (h + 1) * DH].astype(F32)
        weighted = jnp.concatenate([values * column(3), values * column(4)], 1).astype(BF16)
        part = mm(weighted, keys, TN)
        mem_part, mom_part = part[0:DH], part[DH : 2 * DH]
        lo, mid = h * DH, (heads + h) * DH
        part_out[0, lo : lo + DH] = mem_part.astype(BF16)
        part_out[0, mid : mid + DH] = mom_part.astype(BF16)
        keep_end, cross_end, carry_end = [
            jnp.broadcast_to(column(slot)[end], (1, DH)) for slot in range(3)
        ]
        memory, momentum = state_sc[lo : lo + DH], state_sc[mid : mid + DH]
        state_sc[lo : lo + DH] = keep_end * memory + cross_end * momentum + mem_part
        state_sc[mid : mid + DH] = carry_end * momentum + mom_part
        keep_at, cross_at, carry_at = scal + h, scal + heads + h, scal + 2 * heads + h
        keep_dev = state_sc[keep_at : keep_at + 1]
        cross_dev = state_sc[cross_at : cross_at + 1]
        carry_dev = state_sc[carry_at : carry_at + 1]
        state_sc[keep_at : keep_at + 1] = keep_end * keep_dev
        state_sc[cross_at : cross_at + 1] = keep_end * cross_dev + cross_end * carry_dev
        state_sc[carry_at : carry_at + 1] = carry_end * carry_dev

    @pl.when(b == pl.num_programs(0) - 1)
    def _():
        state_out[...] = state_sc[...]
        pack_load(load_out, state_sc[...], scal)


def pack_load(load_out, state, scal):
    load_out[0:scal] = state[0:scal].astype(BF16)
    tail = state[scal : scal + 8]
    high = tail.astype(BF16).astype(F32)
    load_out[scal : scal + 16] = jnp.concatenate([high, tail - high], 0).astype(BF16)


def front(rank, blocks, smalls, weight, conv, aux, heads):
    total, width = blocks[0].shape
    model = width * REL
    local = heads * DH
    count = total // MBLK
    scal = 2 * heads * DH
    at = lambda b, *_: (b, 0)
    return call(
        functools.partial(front_kernel, heads=heads),
        (count,),
        [pl.BlockSpec((MBLK, width), at)] * REL
        + [whole(smalls[0].shape)] * REL
        + [
            whole(weight.shape),
            whole(conv.shape),
            pl.BlockSpec((MBLK, DH), at),
        ],
        [
            pl.BlockSpec((MBLK, model), at),
            pl.BlockSpec((MBLK, model), at),
            pl.BlockSpec((MBLK, 3 * local), at),
            pl.BlockSpec((MBLK, 3 * local), at),
            pl.BlockSpec((1, scal, DH), lambda b, *_: (b, 0, 0)),
            whole((8, 3 * local)),
            whole((16, model)),
            whole((scal + 8, DH)),
            whole((scal + 16, DH)),
        ],
        [
            sds((total, model), BF16),
            sds((total, model), BF16),
            sds((total, 3 * local), BF16),
            sds((total, 3 * local), BF16),
            sds((count, scal, DH), BF16),
            sds((8, 3 * local), F32),
            sds((16, model), F32),
            sds((scal + 8, DH), F32),
            sds((scal + 16, DH), BF16),
        ],
        [
            pltpu.VMEM((16, model), BF16),
            pltpu.VMEM((MBLK + 8, 3 * local), F32),
            pltpu.VMEM((scal + 8, DH), F32),
        ],
        flops=2.2e9,
        moved=12e6,
        prefetch=1,
        ins="h" * (2 * REL) + "hho",
        outs="hhhoooooo",
    )(rank, *blocks, *smalls, weight, conv, aux)


def compose(first, second, heads, backward):
    scal = 2 * heads * DH
    memory, momentum, keeps, crosses, carries = [], [], [], [], []
    for h in range(heads):
        lo, mid = h * DH, (heads + h) * DH
        at = [scal + c * heads + h for c in range(3)]
        keep_one, cross_one, carry_one = [first[n : n + 1] for n in at]
        keep_two, cross_two, carry_two = [second[n : n + 1] for n in at]
        mem_one, mom_one = first[lo : lo + DH], first[mid : mid + DH]
        mem_two, mom_two = second[lo : lo + DH], second[mid : mid + DH]
        if backward:
            memory.append(mem_two + keep_two * mem_one)
            momentum.append(mom_two + cross_two * mem_one + carry_two * mom_one)
            crosses.append(cross_two * keep_one + carry_two * cross_one)
        else:
            memory.append(keep_two * mem_one + cross_two * mom_one + mem_two)
            momentum.append(carry_two * mom_one + mom_two)
            crosses.append(keep_two * cross_one + cross_two * carry_one)
        keeps.append(keep_two * keep_one)
        carries.append(carry_two * carry_one)
    rest = [jnp.zeros((8 - 3 * heads, DH), F32)]
    return jnp.concatenate(memory + momentum + keeps + crosses + carries + rest, 0)


def unpack(ref, scal):
    tail = ref[scal : scal + 16].astype(F32)
    return jnp.concatenate([ref[0:scal].astype(F32), tail[0:8] + tail[8:16]], 0)


def last_join_kernel(rank_ref, got_ref, prefix_ref, prefix_out, *, bit, heads, backward):
    later = (rank_ref[1] & bit) == (0 if backward else bit)

    @pl.when(later)
    def _():
        got = unpack(got_ref, 2 * heads * DH)
        prefix_out[...] = compose(got, prefix_ref[...], heads, backward)

    @pl.when(jnp.logical_not(later))
    def _():
        prefix_out[...] = prefix_ref[...]


def last_join(rank, got, prefix, bit, heads, backward, after):
    return call(
        functools.partial(last_join_kernel, bit=bit, heads=heads, backward=backward),
        (1,),
        [whole(got.shape), whole(prefix.shape)],
        [whole(prefix.shape)],
        [sds(prefix.shape, F32)],
        flops=1e6,
        moved=1e6,
        prefetch=1,
        after=after,
    )(rank, got, prefix)[0]


def join_kernel(rank_ref, got_ref, total_ref, prefix_ref, *outs, bit, heads, backward):
    total_out, prefix_out, load_out = outs
    scal = 2 * heads * DH
    later = (rank_ref[1] & bit) == (0 if backward else bit)
    got = unpack(got_ref, scal)

    @pl.when(later)
    def _():
        total_out[...] = compose(got, total_ref[...], heads, backward)
        prefix_out[...] = compose(got, prefix_ref[...], heads, backward)

    @pl.when(jnp.logical_not(later))
    def _():
        total_out[...] = compose(total_ref[...], got, heads, backward)
        prefix_out[...] = prefix_ref[...]

    pack_load(load_out, total_out[...], scal)


def join(rank, got, total, prefix, bit, heads, backward, after):
    scal = 2 * heads * DH
    state = (scal + 8, DH)
    return call(
        functools.partial(join_kernel, bit=bit, heads=heads, backward=backward),
        (1,),
        [whole(got.shape), whole(state), whole(state)],
        [whole(state), whole(state), whole((scal + 16, DH))],
        [sds(state, F32), sds(state, F32), sds((scal + 16, DH), BF16)],
        flops=1e6,
        moved=1e6,
        prefetch=1,
        after=after,
    )(rank, got, total, prefix)


def entering(rank, load, total, heads, backward, beside):
    count = lax.axis_size("seq")
    row = iota(total.shape, 0) - 2 * heads * DH
    one = ((row >= 0) & (row < heads)) | ((row >= 2 * heads) & (row < 3 * heads))
    prefix = one.astype(F32)
    bit, lap = 1, 0
    while bit < count:
        after = beside[lap](load) if lap < len(beside) else ()
        got = swap(load, "seq", bit)
        if 2 * bit >= count:
            return last_join(rank, got, prefix, bit, heads, backward, after)
        total, prefix, load = join(rank, got, total, prefix, bit, heads, backward, after)
        bit, lap = bit * 2, lap + 1


def attend_kernel(q_ref, k_ref, v_ref, fix_ref, aux_ref, *outs):
    for i in range(k_ref.shape[0] // MBLK):

        @pl.when(pl.program_id(0) == i)
        def _():
            attend_block(i, q_ref, k_ref, v_ref, fix_ref, aux_ref, *outs)


def attend_block(
    i,
    q_ref,
    k_ref,
    v_ref,
    fix_ref,
    aux_ref,
    att_out,
    ratio_out,
    prob_out,
    fixp_out,
):
    fixed_keys, fixed_values = fix_ref[0], fix_ref[1]
    factor = DH ** (-0.5)
    span = slice(i * MBLK, (i + 1) * MBLK)
    seen = (i + 1) * MBLK
    query = q_ref[...]
    starts = aux_ref[:, START_AT : START_AT + 1].astype(jnp.int32)
    raw = mm(query, k_ref[0:seen], NT)
    fixed = mm(query, fixed_keys, NT)
    key_at = iota((MBLK, seen), 1)
    ok = (key_at >= starts) & (key_at <= i * MBLK + iota((MBLK, seen), 0))
    raw = jnp.where(ok, raw, MASKED)
    top = jnp.maximum(jnp.max(raw, -1, keepdims=True), jnp.max(fixed, -1, keepdims=True))
    weights = jnp.exp((raw - top) * factor)
    fix_weights = jnp.exp((fixed - top) * factor)
    scale = 1.0 / (
        jnp.sum(weights, -1, keepdims=True) + jnp.sum(fix_weights, -1, keepdims=True)
    )
    low = (weights * scale).astype(BF16)
    fix_low = (fix_weights * scale).astype(BF16)
    prob_out[:, 0:seen] = low
    fixp_out[...] = fix_low
    attended = mm(low, v_ref[0:seen]) + mm(fix_low, fixed_values)
    held = jnp.sum(low.astype(F32), -1, keepdims=True) + jnp.sum(
        fix_low.astype(F32), -1, keepdims=True
    )
    att_out[...] = attended
    ratio_out[...] = attended / held


def attend(qkv, fixed, aux, head, heads, after):
    total = qkv.shape[0]
    count = total // MBLK
    fixed_count = fixed.shape[1]
    lanes = lambda c: pl.BlockSpec((total, DH), lambda i: (0, c * heads + head))
    at = lambda i: (i, 0)
    return call(
        attend_kernel,
        (count,),
        [
            pl.BlockSpec((MBLK, DH), lambda i: (i, head)),
            lanes(1),
            lanes(2),
            pl.BlockSpec((2, fixed_count, DH), lambda i: (0, 0, head)),
            pl.BlockSpec((MBLK, DH), at),
        ],
        [pl.BlockSpec((MBLK, DH), at)] * 2
        + [pl.BlockSpec((MBLK, total), at), pl.BlockSpec((MBLK, fixed_count), at)],
        [sds((total, DH), F32)] * 2
        + [sds((total, total), BF16), sds((total, fixed_count), BF16)],
        flops=1.5e9,
        moved=8e6,
        after=after,
        outs="ohhh",
    )(qkv, qkv, qkv, fixed, aux)


def within_kernel(qkv_ref, kmat_ref, out_ref, *, heads):
    local = heads * DH
    for h in range(heads):
        lo = h * DH
        near = mm(qkv_ref[:, lo : lo + DH], qkv_ref[:, local + lo : local + lo + DH], NT)
        weights = (kmat_ref[h, 0].astype(F32) * near).astype(BF16)
        out_ref[:, lo : lo + DH] = mm(weights, qkv_ref[:, 2 * local + lo : 2 * local + lo + DH])


def within(qkv, kmat, after):
    total = qkv.shape[0]
    heads, count = kmat.shape[:2]
    at = lambda b: (b, 0)
    return call(
        functools.partial(within_kernel, heads=heads),
        (count,),
        [
            pl.BlockSpec((MBLK, qkv.shape[1]), at),
            pl.BlockSpec((heads, 1, MBLK, MBLK), lambda b: (0, b, 0, 0)),
        ],
        [pl.BlockSpec((MBLK, heads * DH), at)],
        [sds((total, heads * DH), F32)],
        flops=3e8,
        moved=4e6,
        after=after,
    )(qkv, kmat)[0]


def within_back_kernel(qkv_ref, kmat_ref, gm_ref, out_ref, *, heads):
    local = heads * DH
    for h in range(heads):
        lo = h * DH
        query, keys, values = [
            qkv_ref[:, c * local + lo : c * local + lo + DH] for c in range(3)
        ]
        grad = gm_ref[:, lo : lo + DH]
        kernel = kmat_ref[h, 0].astype(F32)
        near = (kernel * mm(query, keys, NT)).astype(BF16)
        cross = (kernel * mm(grad, values, NT)).astype(BF16)
        out_ref[:, lo : lo + DH] = mm(cross, keys)
        out_ref[:, local + lo : local + lo + DH] = mm(cross, query, TN)
        out_ref[:, 2 * local + lo : 2 * local + lo + DH] = mm(near, grad, TN)


def within_back(qkv, kmat, gm, after):
    total, columns = qkv.shape
    heads, count = kmat.shape[:2]
    at = lambda b: (b, 0)
    return call(
        functools.partial(within_back_kernel, heads=heads),
        (count,),
        [
            pl.BlockSpec((MBLK, columns), at),
            pl.BlockSpec((heads, 1, MBLK, MBLK), lambda b: (0, b, 0, 0)),
            pl.BlockSpec((MBLK, heads * DH), at),
        ],
        [pl.BlockSpec((MBLK, columns), at)],
        [sds((total, columns), F32)],
        flops=6e8,
        moved=6e6,
        after=after,
    )(qkv, kmat, gm)[0]


def attend_back_kernel(*refs):
    count = pl.num_programs(0)
    total = refs[1].shape[0]
    for i in range(total // MBLK):

        @pl.when(count - 1 - pl.program_id(0) == i)
        def _():
            attend_back_block(i, *refs)


def attend_back_block(
    i,
    q_ref,
    k_ref,
    v_ref,
    fix_ref,
    prob_ref,
    fixp_ref,
    ratio_ref,
    grad_ref,
    dq_out,
    dk_out,
    dv_out,
    dfix_out,
):
    fixed_keys, fixed_values = fix_ref[0], fix_ref[1]
    factor = DH ** (-0.5)
    span = slice(i * MBLK, (i + 1) * MBLK)
    seen = (i + 1) * MBLK
    query, grad = q_ref[...], grad_ref[...]
    delta = jnp.sum(grad.astype(F32) * ratio_ref[...], -1, keepdims=True)
    low, fix_low = prob_ref[:, 0:seen], fixp_ref[...]
    back = mm(grad, v_ref[0:seen], NT)
    fix_back = mm(grad, fixed_values, NT)
    grad_raw = (low.astype(F32) * (back - delta) * factor).astype(BF16)
    fix_raw = (fix_low.astype(F32) * (fix_back - delta) * factor).astype(BF16)
    dk, dv = mm(grad_raw, query, TN), mm(low, grad, TN)
    dfix_k, dfix_v = mm(fix_raw, query, TN), mm(fix_low, grad, TN)
    if seen == k_ref.shape[0]:
        dk_out[...] = dk
        dv_out[...] = dv
        dfix_out[0] = dfix_k
        dfix_out[1] = dfix_v
    else:
        dk_out[0:seen] += dk
        dv_out[0:seen] += dv
        dfix_out[0] += dfix_k
        dfix_out[1] += dfix_v
    dq_out[...] = mm(grad_raw, k_ref[0:seen]) + mm(fix_raw, fixed_keys)


def attend_back(qkv, fixed, prob, fixp, ratio, grads, head, heads, after):
    total = qkv.shape[0]
    count = total // MBLK
    fixed_count = fixed.shape[1]
    lanes = lambda c: pl.BlockSpec((total, DH), lambda s: (0, c * heads + head))
    at = lambda s: (count - 1 - s, 0)
    of_head = pl.BlockSpec((MBLK, DH), lambda s: (count - 1 - s, head))
    return call(
        attend_back_kernel,
        (count,),
        [
            of_head,
            lanes(1),
            lanes(2),
            pl.BlockSpec((2, fixed_count, DH), lambda s: (0, 0, head)),
            pl.BlockSpec((MBLK, total), at),
            pl.BlockSpec((MBLK, fixed_count), at),
            pl.BlockSpec((MBLK, DH), at),
            of_head,
        ],
        [pl.BlockSpec((MBLK, DH), at)] + [whole((total, DH))] * 2 + [whole((2, fixed_count, DH))],
        [sds((total, DH), F32)] * 3 + [sds((2, fixed_count, DH), F32)],
        flops=3e9,
        moved=10e6,
        after=after,
        ins="oooohhho",
        outs="hhho",
    )(qkv, qkv, qkv, fixed, prob, fixp, ratio, grads)


def merge_kernel(q_ref, *refs, heads):
    atts = refs[:heads]
    (
        intra_ref,
        aux_ref,
        part_ref,
        state_ref,
        merged_out,
        normed_out,
        scale_out,
        state_low,
        state_sc,
    ) = refs[heads:]
    rows = q_ref.shape[0]
    lane = iota((rows, DH), 1)
    scales = jnp.zeros((rows, DH), F32)

    @pl.when(pl.program_id(0) == 0)
    def _():
        state_sc[...] = state_ref[0 : state_sc.shape[0]]

    for h in range(heads):
        lo, mid = h * DH, (heads + h) * DH
        memory, momentum = state_sc[lo : lo + DH], state_sc[mid : mid + DH]
        memory_low, momentum_low = memory.astype(BF16), momentum.astype(BF16)
        state_low[0, lo : lo + DH] = memory_low
        state_low[0, mid : mid + DH] = momentum_low
        query = q_ref[:, lo : lo + DH]
        keep = aux_ref[:, h : h + 1]
        cross = aux_ref[:, heads + h : heads + h + 1]
        carry = aux_ref[:, 2 * heads + h : 2 * heads + h + 1]
        out = (
            intra_ref[:, lo : lo + DH]
            + keep * mm(query, memory_low, NT)
            + cross * mm(query, momentum_low, NT)
        )
        scale = lax.rsqrt(jnp.mean(out * out, -1, keepdims=True) + MEMORY_FLOOR)
        normed = out * scale
        normed_out[:, lo : lo + DH] = normed.astype(BF16)
        scales = jnp.where(lane == h, scale, scales)
        merged_out[:, lo : lo + DH] = (atts[h][...] + normed).astype(BF16)
        end = slice(rows - 1, rows)
        state_sc[lo : lo + DH] = (
            keep[end] * memory + cross[end] * momentum + part_ref[0, lo : lo + DH].astype(F32)
        )
        state_sc[mid : mid + DH] = (
            carry[end] * momentum + part_ref[0, mid : mid + DH].astype(F32)
        )
    scale_out[...] = scales


def merge(qkv, atts, intra, aux, parts, state, heads, after):
    total = qkv.shape[0]
    count = total // MBLK
    local = heads * DH
    scal = 2 * local
    at = lambda b, *_: (b, 0)
    by_block = pl.BlockSpec((1, scal, DH), lambda b, *_: (b, 0, 0))
    return call(
        functools.partial(merge_kernel, heads=heads),
        (count,),
        [pl.BlockSpec((MBLK, local), at)]
        + [pl.BlockSpec((MBLK, DH), at)] * heads
        + [pl.BlockSpec((MBLK, local), at), pl.BlockSpec((MBLK, DH), at)]
        + [by_block, whole(state.shape)],
        [
            pl.BlockSpec((MBLK, local), at),
            pl.BlockSpec((MBLK, local), at),
            pl.BlockSpec((MBLK, DH), at),
            by_block,
        ],
        [
            sds((total, local), BF16),
            sds((total, local), BF16),
            sds((total, DH), F32),
            sds((count, scal, DH), BF16),
        ],
        [pltpu.VMEM((scal, DH), F32)],
        flops=3e8,
        moved=6e6,
        after=after,
        outs="ohhh",
    )(qkv, *atts, intra, aux, parts, state)


def quarter(p, rank_ref):
    return rank_ref[0] ^ ((1 - (p >> 1)) | ((p & 1) << 1))


def middle_kernel(rank_ref, *refs):
    merged, weights = refs[:REL], refs[REL : 2 * REL]
    (
        x_ref,
        gain_ref,
        hid_out,
        normed_out,
        scale_out,
        share_out,
        mid_sc,
        merged_sc,
        weight_sc,
    ) = refs[2 * REL :]
    width = share_out.shape[1]
    local = merged[0].shape[1]

    @pl.when(pl.program_id(0) == 0)
    def _():
        for k in range(REL):
            for q in range(REL):
                weight_sc[k * local : (k + 1) * local, q * width : (q + 1) * width] = weights[k][
                    q * local : (q + 1) * local
                ]

    for k in range(REL):
        merged_sc[:, k * local : (k + 1) * local] = merged[k][...]
    middle = x_ref[...].astype(F32) + mm(merged_sc[...], weight_sc[...])
    mid_sc[...] = middle
    scale = lax.rsqrt(jnp.mean(middle * middle, -1, keepdims=True) + EPSILON)
    normed = middle * scale
    hid_out[...] = (normed * gain_ref[9:10]).astype(BF16)

    @pl.when(pl.program_id(0) == REL // 2)
    def _():
        normed_out[...] = normed
        scale_out[...] = scale

    share_out[...] = mid_sc[:, pl.ds(pl.multiple_of(rank_ref[0] * width, width), width)]


def middle(rank, merged, weights, x, gains, after):
    total, model = x.shape
    local = merged[0].shape[1]
    width = model // REL
    rows = total // REL
    at = lambda p, r: (quarter(p, r), 0)
    return call(
        middle_kernel,
        (total // rows,),
        [pl.BlockSpec((rows, local), at)] * REL
        + [pl.BlockSpec((REL * local, width), lambda *_: (total // (REL * local), 0))] * REL
        + [pl.BlockSpec((rows, model), at), whole(gains.shape)],
        [
            pl.BlockSpec((rows, model), lambda p, r: (p, 0)),
            whole((rows, model)),
            whole((rows, 1)),
            pl.BlockSpec((rows, width), at),
        ],
        [
            sds((total, model), BF16),
            sds((rows, model), F32),
            sds((rows, 1), F32),
            sds((total, width), F32),
        ],
        [
            pltpu.VMEM((rows, model), F32),
            pltpu.VMEM((rows, REL * local), BF16),
            pltpu.VMEM((REL * local, model), BF16),
        ],
        flops=2.2e9,
        moved=10e6,
        prefetch=1,
        after=after,
        ins="o" * (2 * REL) + "ho",
        outs="ohhh",
    )(rank, *merged, *weights, x, gains)


def recall_kernel(rank_ref, *refs):
    cots = refs[:REL]
    down_ref, act_out, cot_out, _ = refs[REL:]
    rank = rank_ref[0]
    width = cots[0].shape[1]
    for k in range(REL):
        span = pl.ds(pl.multiple_of((rank ^ k) * width, width), width)
        cot_out[:, span] = cots[k][...]
    act_out[...] = mm(cot_out[...], down_ref[...], NT).astype(BF16)


def recall(rank, cots, total, down, after):
    width = cots[0].shape[1]
    units, model = down.shape
    rows = total // REL
    at = lambda p, r: (p, 0)
    return call(
        recall_kernel,
        (REL,),
        [pl.BlockSpec((rows, width), lambda p, r: (quarter(p, r), 0))] * REL + [whole(down.shape)],
        [
            pl.BlockSpec((rows, units), at),
            pl.BlockSpec((rows, model), at),
            pl.BlockSpec(memory_space=pl.ANY),
        ],
        [
            sds((total, units), BF16),
            sds((total, model), BF16),
            sds((3, total, units), BF16),
        ],
        flops=1.5e9,
        moved=7e6,
        prefetch=1,
        after=after,
        outs="ohh",
    )(rank, *cots, down)


def ffn_kernel(hid_ref, grad_ref, gate_ref, _, trio_out, back_out):
    rows = back_out.shape[1]
    hidden = hid_ref[...]
    gate = mm(hidden, gate_ref[0], NT)
    up = mm(hidden, gate_ref[1], NT)
    grad_act = grad_ref[...].astype(F32)
    sig = jax.nn.sigmoid(gate)
    silu = gate * sig
    trio_out[0] = (silu * up).astype(BF16)
    grad_gate = (grad_act * up * (sig * (1.0 + gate * (1.0 - sig)))).astype(BF16)
    grad_up = (grad_act * silu).astype(BF16)
    trio_out[1] = grad_gate
    trio_out[2] = grad_up
    back = mm(grad_gate, gate_ref[0]) + mm(grad_up, gate_ref[1])
    for i in range(2):
        back_out[i] = back[i * rows : (i + 1) * rows].astype(BF16)


def ffn(hidden, grad_act, gate_up, trio, part):
    total, model = hidden.shape
    units = grad_act.shape[1]
    rows = total // REL
    at = lambda s: (part, 0)
    return call(
        ffn_kernel,
        (1,),
        [
            pl.BlockSpec((2 * rows, model), at),
            pl.BlockSpec((2 * rows, units), at),
            whole(gate_up.shape),
            pl.BlockSpec(memory_space=pl.ANY),
        ],
        [pl.BlockSpec((3, 2 * rows, units), lambda s: (0, part, 0)), whole((2, rows, model))],
        [sds((3, total, units), BF16), sds((2, rows, model), BF16)],
        flops=3e9,
        moved=8e6,
        alias={3: 0},
        ins="oooh",
        outs="hh",
        spare=10,
    )(hidden, grad_act, gate_up, trio)


def answer_kernel(rank_ref, act_ref, down_ref, send_out, far_out, keep_out):
    rank = rank_ref[0]
    width = keep_out.shape[1]
    spans = [pl.ds(pl.multiple_of((rank ^ k) * width, width), width) for k in range(REL)]
    act = act_ref[0]
    keep_out[...] = mm(act, down_ref[:, spans[0]]).astype(BF16)
    send_out[0] = mm(act, down_ref[:, spans[1]]).astype(BF16)
    far_out[...] = mm(act, down_ref[:, spans[2]]).astype(BF16)
    send_out[1] = mm(act, down_ref[:, spans[3]]).astype(BF16)


def answer(rank, trio, down, after):
    _, total, units = trio.shape
    width = down.shape[1] // REL
    rows = total // REL
    at = lambda p, r: (quarter(p, r), 0)
    return call(
        answer_kernel,
        (REL,),
        [pl.BlockSpec((1, rows, units), lambda p, r: (0, p, 0)), whole(down.shape)],
        [
            pl.BlockSpec((2, rows, width), lambda p, r: (0, quarter(p, r), 0)),
            pl.BlockSpec((rows, width), at),
            pl.BlockSpec((rows, width), at),
        ],
        [sds((2, total, width), BF16), sds((total, width), BF16), sds((total, width), BF16)],
        flops=1.5e9,
        moved=5e6,
        prefetch=1,
        after=after,
        ins="ho",
        outs="hhh",
    )(rank, trio, down)


def seats(bits):
    levels = [[0]]
    for bit in reversed(bits):
        levels.insert(0, [bit | r for level in levels for r in level])
    return levels


def deal(product, outs, bits, seat, by_rows):
    for out, level in zip(outs, seats(bits)):
        chunk = out.shape[2 if by_rows else 3]
        for slot, r in enumerate(level):
            span = pl.ds(pl.multiple_of((seat ^ r) * chunk, chunk), chunk)
            out[slot, 0] = (product[span] if by_rows else product[:, span]).astype(BF16)


def harvest_kernel(rank_ref, cot_ref, hid_ref, trio_ref, *outs, orders, by_rows):
    acc = outs[-1]
    levels = len(orders[0]) + 1
    for i, bits in enumerate(orders):

        @pl.when(pl.program_id(0) == i)
        def _():
            wide = hid_ref[...] if i else cot_ref[...]
            acc[...] = mm(wide, trio_ref[0], TN) if by_rows else mm(trio_ref[0], wide, TN)
            deal(acc, outs[i * levels : (i + 1) * levels], bits, rank_ref[1], by_rows)


def harvest(rank, cot, hidden, trio, orders, after):
    _, total, units = trio.shape
    model = cot.shape[1]
    chunk = model // 2 ** len(orders[0])
    by_rows = chunk % DH != 0
    cut = (chunk, units) if by_rows else (units, chunk)
    shapes = [(len(level), 1) + cut for bits in orders for level in seats(bits)]
    outs = call(
        functools.partial(harvest_kernel, orders=orders, by_rows=by_rows),
        (len(orders),),
        [
            whole(cot.shape),
            whole(hidden.shape),
            pl.BlockSpec((1, total, units), lambda p, r: (p, 0, 0)),
        ],
        [whole(shape) for shape in shapes],
        [sds(shape, BF16) for shape in shapes],
        [pltpu.VMEM((model, units) if by_rows else (units, model), F32)],
        flops=6 * total * model * units,
        moved=1.2e7,
        prefetch=1,
        after=after,
        ins="hoh",
        outs="h" * len(shapes),
    )(rank, cot, hidden, trio)
    levels = len(orders[0]) + 1
    return [outs[i * levels : (i + 1) * levels] for i in range(len(orders))], by_rows


def reap_kernel(rank_ref, hid_ref, gp_ref, tail_ref, back_ref, *outs, cuts):
    gp_sc, acc = outs[-2:]
    outs = outs[:-2]
    seat = rank_ref[1]
    rows = gp_ref.shape[0]
    gp_sc[...] = gp_ref[...]
    gp_sc[rows - 16 : rows] = repaired(tail_ref, back_ref)
    acc[...] = mm(hid_ref[...], gp_sc[...], TN)
    cut_rows(acc, outs, seat, cuts)


def cut_rows(acc, outs, seat, cuts):
    for bits, lo, hi in cuts:
        levels = seats(bits)
        for out, level in zip(outs, levels):
            chunk = out.shape[1]
            for slot, r in enumerate(level):
                span = pl.ds(pl.multiple_of((seat ^ r) * chunk, chunk), chunk)
                out[slot] = acc[span, lo:hi].astype(BF16)
        outs = outs[len(levels) :]


def repaired(tail_ref, back_ref):
    tail = tail_ref[...]
    return jnp.concatenate([tail[:8], tail[8:] + back_ref[...]], 0).astype(BF16)


def reap(rank, hidden, gp, tail, returned, cuts):
    total, model = hidden.shape
    columns = gp.shape[1]
    shapes = [
        (len(level), model // 2 ** len(bits), hi - lo)
        for bits, lo, hi in cuts
        for level in seats(bits)
    ]
    outs = call(
        functools.partial(reap_kernel, cuts=cuts),
        (1,),
        [whole(a.shape) for a in (hidden, gp, tail, returned)],
        [whole(shape) for shape in shapes],
        [sds(shape, BF16) for shape in shapes],
        [pltpu.VMEM((total, columns), BF16), pltpu.VMEM((model, columns), F32)],
        flops=2 * total * model * columns,
        moved=6e6,
        prefetch=1,
        ins="oooo",
    )(rank, hidden, gp, tail, returned)
    split = len(seats(cuts[0][0]))
    return outs[:split], outs[split:]


def absorb(parts, lap, got):
    parts = list(parts)
    at = 0
    for m in range(lap + 1, len(parts)):
        size = parts[m].shape[0]
        kind = F32 if m == len(parts) - 1 else BF16
        parts[m] = parts[m].astype(kind) + got[at : at + size].astype(kind)
        at += size
    return parts


def bend_kernel(rank_ref, keep_ref, near_ref, far_ref, cot_ref, normed_ref, scale_ref, gain_ref, *outs):
    low_out, dgain_out = outs
    grad = (
        keep_ref[0].astype(F32) + near_ref[0].astype(F32) + far_ref[0].astype(F32)
    )
    normed = normed_ref[...]
    total = jnp.sum(grad * normed, 0, keepdims=True)
    dgain_out[...] = jnp.where(iota(dgain_out.shape, 0) == 1, total, 0.0)
    g = grad * gain_ref[9:10]
    mean = jnp.mean(g * normed, -1, keepdims=True)
    low_out[...] = (cot_ref[...].astype(F32) + scale_ref[...] * (g - normed * mean)).astype(BF16)


def bend(rank, keep, near, far, cot, normed, scale, gains, after):
    total, model = cot.shape
    rows = total // REL
    own = lambda s, r: (REL // 2, 0)
    one = pl.BlockSpec((1, rows, model), lambda *_: (0, 0, 0))
    return call(
        bend_kernel,
        (1,),
        [
            one,
            one,
            one,
            pl.BlockSpec((rows, model), own),
            whole((rows, model)),
            whole((rows, 1)),
            whole(gains.shape),
        ],
        [whole((rows, model)), whole((8, model))],
        [sds((rows, model), BF16), sds((8, model), F32)],
        flops=5e6,
        moved=4e6,
        prefetch=1,
        after=after,
        ins="hoohhhh",
    )(rank, keep, near, far, cot, normed, scale, gains)


def turn_kernel(rank_ref, *refs, heads, bits, by_rows):
    lows = refs[:REL]
    (
        w_ref,
        q_ref,
        normed_ref,
        scale_ref,
        aux_ref,
        merged_ref,
        dev_ref,
        ga_out,
        gm_out,
        part_out,
        share_out,
        state_out,
        load_out,
        *levels_out,
        low_sc,
        acc_sc,
        state_sc,
    ) = refs[REL:]
    step = pl.program_id(0)
    last = pl.num_programs(0) - 1
    block = last - step
    rank = rank_ref[0]
    rows = q_ref.shape[0]
    scal = 2 * heads * DH
    for k in range(REL):

        @pl.when((rank ^ k) == block)
        def _():
            low_sc[...] = lows[k][...]

    @pl.when(step == 0)
    def _():
        state_sc[...] = jnp.zeros_like(state_sc)
        acc_sc[...] = jnp.zeros_like(acc_sc)

    low = low_sc[...]
    if by_rows:
        acc_sc[...] += mm(low, merged_ref[...], TN)
    else:
        acc_sc[...] += mm(merged_ref[...], low, TN)
    width = share_out.shape[1]
    share_out[...] = low_sc[:, pl.ds(pl.multiple_of(rank * width, width), width)]
    grad_merged = mm(low, w_ref[...], NT)
    ga_out[...] = grad_merged.astype(BF16)
    end = slice(rows - 1, rows)
    for h in range(heads):
        lo, mid = h * DH, (heads + h) * DH
        g = grad_merged[:, lo : lo + DH]
        normed = normed_ref[:, lo : lo + DH].astype(F32)
        scale = scale_ref[:, h : h + 1]
        grad = scale * (g - normed * jnp.mean(g * normed, -1, keepdims=True))
        gm_out[:, lo : lo + DH] = grad.astype(BF16)
        query = q_ref[:, lo : lo + DH]
        keep = aux_ref[:, h : h + 1]
        cross = aux_ref[:, heads + h : heads + h + 1]
        carry = aux_ref[:, 2 * heads + h : 2 * heads + h + 1]
        mem_part = mm((keep * grad).astype(BF16), query, TN)
        mom_part = mm((cross * grad).astype(BF16), query, TN)
        part_out[0, lo : lo + DH] = mem_part.astype(BF16)
        part_out[0, mid : mid + DH] = mom_part.astype(BF16)
        memory, momentum = state_sc[lo : lo + DH], state_sc[mid : mid + DH]
        state_sc[lo : lo + DH] = keep[end] * memory + mem_part
        state_sc[mid : mid + DH] = cross[end] * memory + carry[end] * momentum + mom_part

    @pl.when(step == last)
    def _():
        state_sc[scal : scal + 8] = dev_ref[scal : scal + 8]
        state_out[...] = state_sc[...]
        pack_load(load_out, state_sc[...], scal)
        seat = rank_ref[1]
        for out, level in zip(levels_out, seats(bits)):
            chunk = out.shape[1 if by_rows else 2]
            for slot, r in enumerate(level):
                span = pl.ds(pl.multiple_of((seat ^ r) * chunk, chunk), chunk)
                out[slot] = (acc_sc[span] if by_rows else acc_sc[:, span]).astype(BF16)


def turn(rank, lows, weight, qkv, normed, scales, aux, merged, dev, bits, heads):
    total = qkv.shape[0]
    count = total // MBLK
    local, model = weight.shape
    width = model // REL
    scal = 2 * local
    at = lambda b, *_: (count - 1 - b, 0)
    chunk = model // 2 ** len(bits)
    by_rows = chunk % DH != 0
    cut = (chunk, local) if by_rows else (local, chunk)
    levels = [(len(level),) + cut for level in seats(bits)]
    out = call(
        functools.partial(turn_kernel, heads=heads, bits=bits, by_rows=by_rows),
        (count,),
        [whole(lows[0].shape)] * REL
        + [
            whole(weight.shape),
            pl.BlockSpec((MBLK, local), at),
            pl.BlockSpec((MBLK, local), at),
            pl.BlockSpec((MBLK, DH), at),
            pl.BlockSpec((MBLK, DH), at),
            pl.BlockSpec((MBLK, local), at),
            whole(dev.shape),
        ],
        [
            pl.BlockSpec((MBLK, local), at),
            pl.BlockSpec((MBLK, local), at),
            pl.BlockSpec((1, scal, DH), lambda b, *_: (count - 1 - b, 0, 0)),
            pl.BlockSpec((MBLK, width), at),
            whole((scal + 8, DH)),
            whole((scal + 16, DH)),
        ]
        + [whole(shape) for shape in levels],
        [
            sds((total, local), BF16),
            sds((total, local), BF16),
            sds((count, scal, DH), BF16),
            sds((total, width), BF16),
            sds((scal + 8, DH), F32),
            sds((scal + 16, DH), BF16),
        ]
        + [sds(shape, BF16) for shape in levels],
        [
            pltpu.VMEM((MBLK, model), BF16),
            pltpu.VMEM((model, local) if by_rows else (local, model), F32),
            pltpu.VMEM((scal + 8, DH), F32),
        ],
        flops=8e8,
        moved=8e6,
        prefetch=1,
        ins="o" * (REL + 2) + "hhooo",
        outs="ooohoo" + "o" * len(levels),
    )(rank, *lows, weight, qkv, normed, scales, aux, merged, dev)
    return out[:6], out[6:], by_rows


def settle_kernel(qkv_ref, *refs, heads):
    rests = refs[: 3 * heads]
    (
        within_ref,
        gm_ref,
        aux_ref,
        low_ref,
        part_ref,
        state_ref,
        proj_ref,
        halo_ref,
        conv_ref,
        gp_out,
        tail_out,
        head_out,
        gconv_out,
        _,
        _,
        _,
        state_sc,
        mix_sc,
        tap_sc,
        proj_sc,
    ) = refs[3 * heads :]
    step = pl.program_id(0)
    last = pl.num_programs(0) - 1
    block = last - step
    rows = qkv_ref.shape[0]
    local = heads * DH
    base = block * rows

    @pl.when(step == 0)
    def _():
        state_sc[...] = state_ref[0 : state_sc.shape[0]]
        tap_sc[...] = jnp.zeros_like(tap_sc)
        gconv_out[...] = jnp.zeros_like(gconv_out)

    end = slice(rows - 1, rows)
    for h in range(heads):
        lo, mid = h * DH, (heads + h) * DH
        memory, momentum = state_sc[lo : lo + DH], state_sc[mid : mid + DH]
        memory_low, momentum_low = memory.astype(BF16), momentum.astype(BF16)
        keep = aux_ref[:, h : h + 1]
        cross = aux_ref[:, heads + h : heads + h + 1]
        carry = aux_ref[:, 2 * heads + h : 2 * heads + h + 1]
        end_kernel = aux_ref[:, 3 * heads + h : 3 * heads + h + 1]
        end_carry = aux_ref[:, 4 * heads + h : 4 * heads + h + 1]
        keys = qkv_ref[:, local + lo : local + lo + DH]
        values = qkv_ref[:, 2 * local + lo : 2 * local + lo + DH]
        gmem = gm_ref[:, lo : lo + DH]
        both = lambda a, one, two: jnp.concatenate(
            [a.astype(F32) * one, a.astype(F32) * two], 1
        ).astype(BF16)
        states = jnp.concatenate([low_ref[0, lo : lo + DH], low_ref[0, mid : mid + DH]], 0)
        ends = jnp.concatenate([memory_low, momentum_low], 0)
        wide = jnp.concatenate([memory_low, momentum_low], 1)
        dq = mm(both(gmem, keep, cross), states)
        dk = mm(both(values, end_kernel, end_carry), ends)
        dv = mm(both(keys, end_kernel, end_carry), wide, NT)
        for c, extra in enumerate((dq, dk, dv)):
            mix_sc[:, c * local + lo : c * local + lo + DH] = (
                rests[c * heads + h][...]
                + within_ref[:, c * local + lo : c * local + lo + DH]
                + extra
            )
        state_sc[lo : lo + DH] = keep[end] * memory + part_ref[0, lo : lo + DH].astype(F32)
        state_sc[mid : mid + DH] = (
            cross[end] * memory
            + carry[end] * momentum
            + part_ref[0, mid : mid + DH].astype(F32)
        )
    before = proj_ref[pl.ds(pl.multiple_of(jnp.maximum(base - 16, 0), 16), 16)].astype(F32)[8:16]
    proj_sc[0:8] = jnp.where(block == 0, halo_ref[...], before)
    proj_sc[8 : 8 + rows] = proj_ref[pl.ds(pl.multiple_of(base, rows), rows)].astype(F32)
    place = base + iota((rows, 1), 0)
    starts = aux_ref[:, START_AT : START_AT + 1].astype(jnp.int32)
    mix = mix_sc[...]
    total = conv_ref[0:1] * mix
    gconv_out[0:1] += jnp.sum(mix * proj_sc[8 : 8 + rows], 0, keepdims=True)
    for j in range(1, KW):
        tap_sc[j - 1, 8 + rows : 16 + rows] = tap_sc[j - 1, 8:16]
        tap = mix * (place - j >= starts).astype(F32)
        tap_sc[j - 1, 8 : 8 + rows] = conv_ref[j : j + 1] * tap
        gconv_out[j : j + 1] += jnp.sum(tap * proj_sc[8 - j : 8 - j + rows], 0, keepdims=True)
        total = total + tap_sc[j - 1, 8 + j : 8 + j + rows]
    gp_out[...] = total.astype(BF16)

    @pl.when(step == 0)
    def _():
        tail_out[...] = total[rows - 16 : rows]

    @pl.when(step == last)
    def _():
        head_out[...] = tap_sc[0, 1:9] + tap_sc[1, 2:10] + tap_sc[2, 3:11]


def settle(qkv, grads, inner, gm, aux, lows, parts, state, proj, halo, conv, width, heads):
    total = qkv.shape[0]
    count = total // MBLK
    local = heads * DH
    scal = 2 * local
    at = lambda b, *_: (count - 1 - b, 0)
    by_block = pl.BlockSpec((1, scal, DH), lambda b, *_: (count - 1 - b, 0, 0))
    return call(
        functools.partial(settle_kernel, heads=heads),
        (count,),
        [pl.BlockSpec((MBLK, 3 * local), at)]
        + [pl.BlockSpec((MBLK, DH), at)] * (3 * heads)
        + [
            pl.BlockSpec((MBLK, 3 * local), at),
            pl.BlockSpec((MBLK, local), at),
            pl.BlockSpec((MBLK, DH), at),
            by_block,
            by_block,
            whole(state.shape),
            whole(proj.shape),
            whole(halo.shape),
            whole(conv.shape),
        ],
        [
            pl.BlockSpec((MBLK, 3 * local), at),
            whole((16, 3 * local)),
            whole((8, 3 * local)),
            whole((8, 3 * local)),
        ]
        + [pl.BlockSpec(memory_space=pl.ANY)] * 3,
        [
            sds((total, 3 * local), BF16),
            sds((16, 3 * local), F32),
            sds((8, 3 * local), F32),
            sds((8, 3 * local), F32),
            sds((2, total, width), BF16),
            sds((total, width), BF16),
            sds((total, width), BF16),
        ],
        [
            pltpu.VMEM((scal, DH), F32),
            pltpu.VMEM((MBLK, 3 * local), F32),
            pltpu.VMEM((KW - 1, MBLK + 16, 3 * local), F32),
            pltpu.VMEM((MBLK + 8, 3 * local), F32),
        ],
        flops=6e8,
        moved=14e6,
        ins="o" + "h" * (3 * heads) + "ooohoohoo",
        outs="oooohhh",
    )(qkv, *grads, inner, gm, aux, lows, parts, state, proj, halo, conv)


def back_kernel(
    rank_ref,
    gp_ref,
    tail_ref,
    back_ref,
    w_ref,
    x_ref,
    gain_ref,
    other_ref,
    send_in,
    far_in,
    keep_in,
    send_out,
    far_out,
    keep_out,
    dgain_out,
    grad_sc,
    gp_sc,
    w_sc,
    *,
    last,
):
    rank = rank_ref[0]
    width = keep_out.shape[1]
    local = w_ref.shape[2]

    @pl.when(pl.program_id(0) == 0)
    def _():
        dgain_out[...] = other_ref[...]
        for c in range(3):
            w_sc[:, c * local : (c + 1) * local] = w_ref[c]

    rows = gp_ref.shape[0]
    gp_sc[...] = gp_ref[...]
    if last:
        gp_sc[rows - 16 : rows] = repaired(tail_ref, back_ref)
    grad = mm(gp_sc[...], w_sc[...], NT)
    x = x_ref[...].astype(F32)
    scale = lax.rsqrt(jnp.mean(x * x, -1, keepdims=True) + EPSILON)
    normed = x * scale
    dgain_out[0:1] += jnp.sum(grad * normed, 0, keepdims=True)
    g = grad * gain_ref[8:9]
    grad_sc[...] = (scale * (g - normed * jnp.mean(g * normed, -1, keepdims=True))).astype(BF16)
    spans = [pl.ds(pl.multiple_of((rank ^ k) * width, width), width) for k in range(REL)]
    keep_out[...] = grad_sc[:, spans[0]]
    send_out[0] = grad_sc[:, spans[1]]
    far_out[...] = grad_sc[:, spans[2]]
    send_out[1] = grad_sc[:, spans[3]]


def back(rank, gp, tail, returned, weight, x, gains, dgain, rooms, last, after):
    total, model = x.shape
    width = model // REL
    count = total // MBLK
    first = count - 1 if last else 0
    at = lambda b, *_: (b + first, 0)
    columns = gp.shape[1]
    return call(
        functools.partial(back_kernel, last=last),
        (1 if last else count - 1,),
        [
            pl.BlockSpec((MBLK, columns), at),
            whole(tail.shape),
            whole(returned.shape),
            whole(weight.shape),
            pl.BlockSpec((MBLK, model), at),
            whole(gains.shape),
            whole(dgain.shape),
        ]
        + [pl.BlockSpec(memory_space=pl.ANY)] * 3,
        [
            pl.BlockSpec((2, MBLK, width), lambda b, *_: (0, b + first, 0)),
            pl.BlockSpec((MBLK, width), at),
            pl.BlockSpec((MBLK, width), at),
            whole((8, model)),
        ],
        [
            sds((2, total, width), BF16),
            sds((total, width), BF16),
            sds((total, width), BF16),
            sds((8, model), F32),
        ],
        [
            pltpu.VMEM((MBLK, model), BF16),
            pltpu.VMEM((MBLK, columns), BF16),
            pltpu.VMEM((model, columns), BF16),
        ],
        flops=4e8 if last else 1.3e9,
        moved=2e6 if last else 6e6,
        prefetch=1,
        after=after,
        alias={7: 0, 8: 1, 9: 2},
        ins="oooohoohhh",
        outs="hhho",
    )(rank, gp, tail, returned, weight, x, gains, dgain, *rooms)


def wrap_kernel(little_ref, got_ref, one_out, two_out, conv_out, fixed_out):
    total = little_ref[...] + got_ref[...]
    one_out[...] = total[0:1]
    two_out[...] = total[1:2]
    taps, parts, _ = conv_out.shape
    for j in range(taps):
        conv_out[j] = total[2 + parts * j : 2 + parts * (j + 1)]
    rest = 2 + taps * parts
    rows = fixed_out.shape[1]
    for c in range(fixed_out.shape[0]):
        fixed_out[c] = total[rest + c * rows : rest + (c + 1) * rows]


def wrap(little, got, fixed_count):
    local = little.shape[1]
    shapes = [(1, local), (1, local), (KW, 3, local), (2, fixed_count, local)]
    return call(
        wrap_kernel,
        (1,),
        [whole(little.shape)] * 2,
        [whole(shape) for shape in shapes],
        [sds(shape, F32) for shape in shapes],
        moved=1e5,
    )(little, got)


def lay_kernel(own_ref, got_ref, last_ref, out_ref):
    local = out_ref.shape[2]
    both = own_ref[0] + got_ref[0].astype(F32)
    for c in range(2):
        out_ref[c] = both[:, c * local : (c + 1) * local]
    out_ref[2] = last_ref[0]


def lay(own, got, last):
    _, rows, columns = last.shape
    return call(
        lay_kernel,
        (1,),
        [whole(own.shape), whole(got.shape), whole(last.shape)],
        [whole((3, rows, columns))],
        [sds((3, rows, columns), F32)],
        moved=1e6,
    )(own, got, last)[0]


def per_device(
    inputs,
    cotangent,
    norm_gain,
    qkv_weight,
    conv_kernel,
    persistent,
    out_weight,
    ffn_gain,
    gate_up,
    down_weight,
    memory_decay,
    momentum_decay,
    doc_start,
):
    total, width = inputs.shape
    local = qkv_weight.shape[2]
    heads = local // DH
    model = width * REL
    rank = jnp.stack([lax.axis_index("head"), lax.axis_index("seq")]).astype(jnp.int32)
    conv = conv_kernel.reshape(KW, 3 * local)

    kmat, aux = prepare(rank, doc_start.reshape(1, total), memory_decay.T, momentum_decay.T)
    columns = out_weight.reshape(local, REL, width).transpose(1, 0, 2).reshape(-1, width)
    pair = jnp.concatenate([cotangent, columns], 0)
    small = pack(shifted(inputs[total - 8 :], "seq", 1), norm_gain, ffn_gain, ())
    smalls = gather_rel(small)
    blocks = gather_rel(inputs, beside=(kmat, smalls[2]))
    pair_far = swap(hold(pair, blocks[2], smalls[2]), "head", 2)

    (
        x,
        hidden_one,
        proj,
        qkv,
        parts,
        halo,
        gains,
        dev_state,
        load,
    ) = front(
        rank,
        blocks,
        smalls,
        qkv_weight,
        conv,
        aux,
        heads,
    )

    ahead = []

    def attend_head(sent):
        ahead.append(attend(qkv, persistent, aux, len(ahead), heads, (sent,)))
        return ahead[-1][:1]

    def inside_blocks(sent):
        ahead.append(within(qkv, kmat, (sent,)))
        return ahead[-1:]


    prefix = entering(
        rank, load, dev_state, heads, False, [attend_head] * heads + [inside_blocks]
    )
    intra = ahead.pop()
    atts, ratios, probs, fixps = zip(*ahead)
    pair_far = hold(pair_far, prefix)
    pairs = [pair, swap(pair, "head", 1), pair_far, swap(pair_far, "head", 1)]
    merged, normed_mem, mem_scales, state_lows = merge(
        qkv, atts, intra, aux, parts, prefix, heads, ()
    )
    grad_act, cot, trio = recall(rank, pairs, total, down_weight, (merged,))
    merged_rel = gather_rel(merged, beside=(grad_act,))
    hidden_two, normed_two, scale_two, middle_share = middle(
        rank, merged_rel, pairs, x, gains, (grad_act,)
    )
    gate_weights = gate_up.transpose(0, 2, 1)
    trio, send = ffn(hidden_two, grad_act, gate_weights, trio, 0)
    trio, rest = ffn(hidden_two, grad_act, gate_weights, trio, 1)
    places = lax.axis_size("seq")
    bits = tuple(2**i for i in range((places - 1).bit_length()))
    laps = len(bits)
    turned = bits[1:] + bits[:1]

    near = hold(swap(send, "head", 1), rest)
    half = rest[1:2] + near[1:2]
    turned = bits[1:] + bits[:1]
    ffn_levels, ffn_rows = harvest(
        rank, cot, hidden_two, trio, (turned, bits, bits), (half,)
    )
    far_sum = hold(swap(half, "head", 2), ffn_levels[-1][-1])
    (down, gate, up), _ = lax.optimization_barrier((ffn_levels, far_sum))
    low_own, dgain_two = bend(
        rank, rest, near, far_sum, cot, normed_two, scale_two, gains, ()
    )
    ans_send, ans_far, ans_keep = answer(rank, trio, down_weight, (low_own,))
    down = absorb(down, 0, hold(swap(down[0], "seq", turned[0]), ans_keep))
    lows = gather_rel(low_own, beside=(ans_keep, *down[1:]))

    (grad_att, grad_mem, mem_parts, low_share, back_state, back_load), three, by_rows = turn(
        rank,
        lows,
        out_weight,
        qkv,
        normed_mem,
        mem_scales,
        aux,
        merged,
        dev_state,
        bits,
        heads,
    )
    pieces, extra = [], {"three": three, "down": down, "gate": gate, "up": up}

    def later(name, lap, mark):
        extra[name] = list(extra[name])
        extra[name][lap] = hold(extra[name][lap], mark)


    def exchanged(name, lap, mark):
        order = turned if name == "down" else bits
        got = hold(swap(extra[name][lap], "seq", order[lap]), mark)
        extra[name] = absorb(extra[name], lap, got)
        return extra[name][lap + 1 :]

    def attend_back_head(sent):
        h = len(pieces)
        pieces.append(
            attend_back(
                qkv, persistent, probs[h], fixps[h], ratios[h], grad_att, h, heads, (sent,)
            )
        )
        if h == 0:
            return [pieces[-1][3], *exchanged("gate", 0, sent)]
        later("gate", 1, sent)
        later("up", 0, sent)
        extra["ans_near"] = hold(swap(ans_send, "head", 1), sent)
        extra["ans_half"] = ans_far + extra["ans_near"][1]
        return [
            pieces[-1][3],
            extra["ans_half"],
            *exchanged("down", 1, sent),
            *exchanged("three", 0, sent),
        ]

    def back_inside(sent):
        extra["inner"] = within_back(qkv, kmat, grad_mem, (sent,))
        extra["ans_sum"] = swap(extra["ans_half"], "head", 2)
        return [
            extra["inner"],
            extra["ans_sum"],
            *exchanged("three", 1, sent),
        ]

    suffix = entering(
        rank, back_load, back_state, heads, True, [attend_back_head] * heads + [back_inside]
    )
    inner = extra["inner"]
    suffix = hold(suffix, *exchanged("gate", 1, suffix), *exchanged("up", 0, suffix))
    gp, tail, head_rows, gconv, *rooms = settle(
        qkv,
        [pieces[h][c] for c in range(3) for h in range(heads)],
        inner,
        grad_mem,
        aux,
        state_lows,
        mem_parts,
        suffix,
        proj,
        halo,
        conv,
        width,
        heads,
    )
    returned = shifted(head_rows, "seq", -1)
    for lap in range(2, laps):
        exchanged("three", lap, gp)
        exchanged("down", lap, gp)
        exchanged("gate", lap, gp)
    exchanged("up", 1, gp)
    three, down = extra["three"], extra["down"]
    ans_near, ans_sum = extra["ans_near"], extra["ans_sum"]
    *rooms, dgain = back(
        rank, gp, tail, head_rows, qkv_weight, x, gains, dgain_two, rooms, False, (head_rows,)
    )
    returned = hold(returned, three[-1], down[-1], extra["gate"][-1], extra["up"][2], dgain)
    one, two = reap(
        rank,
        hidden_one,
        gp,
        tail,
        returned,
        ((bits, 0, 2 * local), (turned, 2 * local, 3 * local)),
    )
    bsend, bfar, bkeep, dgain = back(
        rank, gp, tail, returned, qkv_weight, x, gains, dgain, rooms, True, (two[-1],)
    )

    def take(x, mark, axis, bit):
        return hold(swap(x, axis, bit), *mark)

    gain_half = dgain + swap(dgain, "head", 1)
    bnear = take(bsend, (gain_half,), "head", 1)
    bhalf = bfar + bnear[1]
    output = (
        middle_share
        + ans_keep.astype(F32)
        + ans_near[0].astype(F32)
        + hold(ans_sum, bhalf).astype(F32)
    ).astype(BF16)
    gain_sums = gain_half + take(gain_half, (output,), "head", 2)
    gain_own = lax.dynamic_slice_in_dim(
        gain_sums, lax.axis_index("head") * width, width, 1
    )
    fixed_count = persistent.shape[1]
    little = jnp.concatenate(
        [
            gain_own[:2],
            gconv[:KW].reshape(3 * KW, local),
            jnp.concatenate([p[3] for p in pieces], -1).reshape(2 * fixed_count, local),
        ],
        0,
    )
    two = absorb(two, 0, take(two[0], (little,), "seq", turned[0]))
    one = absorb(one, 0, take(one[0], (two[1],), "seq", bits[0]))
    mark = (one[1],)
    for lap in range(1, laps):
        little = little + take(little, mark, "seq", bits[lap - 1])
        two = absorb(two, lap, take(two[lap], (little,), "seq", turned[lap]))
        mark = (two[lap + 1],)
        if lap + 1 < laps:
            one = absorb(one, lap, take(one[lap], mark, "seq", bits[lap]))
            mark = (one[lap + 1],)
    for lap in range(2, laps):
        exchanged("up", lap, mark[0])
    flip = (lambda a: a.transpose(0, 2, 1)) if ffn_rows else (lambda a: a)
    grad_down = flip(down[-1][0])[0]
    grad_gate_up = flip(jnp.concatenate([extra["gate"][-1][0], extra["up"][-1][0]], 0))
    grad_gate_up = grad_gate_up.transpose(0, 2, 1)
    mark = (grad_gate_up,)
    input_grad = (
        bkeep.astype(F32)
        + bnear[0].astype(F32)
        + take(bhalf, mark, "head", 2).astype(F32)
        + low_share.astype(F32)
    )
    got = take(little, (input_grad,), "seq", bits[-1])
    gain_one, gain_two, grad_conv, grad_fixed = wrap(little, got, fixed_count)
    got = take(one[-2], (grad_conv,), "seq", bits[-1])
    grad_qkv = lay(one[-1], got, two[-1])
    grad_out = three[-1][0].T if by_rows else three[-1][0]
    return (
        output,
        input_grad,
        gain_one[0],
        grad_qkv,
        grad_conv,
        grad_fixed,
        grad_out,
        gain_two[0],
        grad_gate_up,
        grad_down,
    )


def solution(mesh):
    placed = (
        P("seq", "head"),
        P("seq", "head"),
        P("head"),
        P(None, None, "head"),
        P(None, None, "head"),
        P(None, None, "head"),
        P("head", None),
        P("head"),
        P(None, None, "head"),
        P("head", None),
        P("seq", "head"),
        P("seq", "head"),
        P("seq"),
    )
    return jax.shard_map(
        per_device,
        mesh=mesh,
        in_specs=placed,
        out_specs=(
            P("seq", "head"),
            P("seq", "head"),
            P("head"),
            P(None, "seq", "head"),
            P(None, None, "head"),
            P(None, None, "head"),
            P("head", "seq"),
            P("head"),
            P(None, "seq", "head"),
            P("head", "seq"),
        ),
        check_vma=False,
    )
```

```python
import functools

import jax
import jax.numpy as jnp
from jax import lax
from jax.experimental import pallas as pl
from jax.experimental.pallas import tpu as pltpu
from jax.sharding import PartitionSpec as P

DH = 128
KW = 4
SEG = 1024
MBLK = 256
EPSILON = 1e-06
MEMORY_FLOOR = 64.0
MASKED = -1e30
F32 = jnp.float32
BF16 = jnp.bfloat16
NN = (((1,), (0,)), ((), ()))
NT = (((1,), (1,)), ((), ()))
TN = (((0,), (0,)), ((), ()))
REL = 4
START_AT = 126


def mm(a, b, dims=NN):
    return lax.dot_general(a, b, dims, preferred_element_type=F32)


def exact(a, b, dims=NN):
    return lax.dot_general(
        a, b, dims, precision=lax.Precision.HIGHEST, preferred_element_type=F32
    )


def padded(shape, dtype):
    size = jnp.dtype(dtype).itemsize
    tile = 32 // size
    if len(shape) == 1:
        return -(-shape[0] // 1024) * 1024 * 4
    total = size * -(-shape[-1] // 128) * 128 * (-(-shape[-2] // tile) * tile)
    for n in shape[:-2]:
        total *= n
    return total


def call(
    kernel,
    grid,
    in_specs,
    out_specs,
    out_shape,
    scratch=(),
    flops=0,
    moved=0,
    prefetch=0,
    after=(),
    ins="",
    outs="",
    alias={},
    spare=5,
):
    taken = prefetch + len(in_specs)
    waits = len(after)

    def body(*refs):
        kernel(*refs[:taken], *refs[taken + waits :])

    spaces = {"v": pltpu.VMEM, "h": pltpu.HBM}
    results = out_shape if isinstance(out_shape, (list, tuple)) else [out_shape]
    out_blocks = out_specs if isinstance(out_specs, (list, tuple)) else [out_specs]
    held = sum(
        2 * padded(b.block_shape, s.dtype) for b, s in zip(out_blocks, results) if b.block_shape
    )
    held += sum(padded(m.shape, m.dtype) for m in scratch)
    if outs:
        out_shape = [
            spaces[c](s.shape, s.dtype) if c in spaces else s for c, s in zip(outs, results)
        ]
        assert len(outs) == len(results)

    spec = pltpu.PrefetchScalarGridSpec(
        num_scalar_prefetch=prefetch,
        grid=grid,
        in_specs=list(in_specs) + [pl.BlockSpec(memory_space=pl.ANY)] * waits,
        out_specs=out_specs,
        scratch_shapes=list(scratch),
    )

    def run(*operands):
        taking = held + sum(
            2 * padded(b.block_shape, a.dtype)
            for b, a in zip(in_specs, operands[prefetch:])
            if b.block_shape
        )
        made = pl.pallas_call(
            body,
            grid_spec=spec,
            out_shape=out_shape,
            input_output_aliases={prefetch + i: o for i, o in alias.items()},
            compiler_params=pltpu.CompilerParams(
                vmem_limit_bytes=min(taking + spare * 2**20, 24 * 2**20)
            ),
            cost_estimate=pl.CostEstimate(
                flops=int(flops), bytes_accessed=int(moved), transcendentals=0
            ),
        )
        if ins:
            assert len(ins) == len(operands) - prefetch
            operands = operands[:prefetch] + tuple(
                pltpu.with_memory_space_constraint(a, spaces[c]) if c in spaces else a
                for c, a in zip(ins, operands[prefetch:])
            )
        return made(*operands, *after)

    return run


def whole(shape):
    return pl.BlockSpec(shape, lambda *_: (0,) * len(shape))


def sds(shape, dtype):
    return jax.ShapeDtypeStruct(shape, dtype)


def iota(shape, dim):
    return lax.broadcasted_iota(jnp.int32, shape, dim)


def swap(x, axis, bit):
    count = lax.axis_size(axis)
    return lax.ppermute(x, axis, [(i, i ^ bit) for i in range(count)])


def shifted(x, axis, by):
    count = lax.axis_size(axis)
    return lax.ppermute(x, axis, [(i, i + by) for i in range(count) if 0 <= i + by < count])


def hold(x, *others):
    return lax.optimization_barrier((x, *others))[0]


def gather_rel(x, beside=(), before=()):
    far = swap(hold(x, *before) if before else x, "head", 2)
    near = swap(x, "head", 1)
    far = hold(far, *beside) if beside else far
    return [x, near, far, swap(far, "head", 1)]


def pack_kernel(halo_ref, one_ref, two_ref, out_ref):
    width = halo_ref.shape[1]
    rows = [
        halo_ref[...].astype(F32),
        one_ref[...].astype(F32).reshape(1, width),
        two_ref[...].astype(F32).reshape(1, width),
        jnp.zeros((6, width), F32),
    ]
    out_ref[...] = jnp.concatenate(rows, 0).astype(BF16)


def pack(halo, one, two, after):
    return call(
        pack_kernel,
        (1,),
        [whole(halo.shape), whole(one.shape), whole(two.shape)],
        whole((16, halo.shape[1])),
        sds((16, halo.shape[1]), BF16),
        moved=1e4,
        after=after,
        ins="hhh",
    )(halo, one, two)


def prepare_kernel(rank_ref, doc_ref, keep_ref, carry_ref, kmat_out, aux_out, *, heads):
    rows = doc_ref.shape[1]
    base = pl.program_id(0) * rows
    below = iota((rows, rows), 0)
    right = iota((rows, rows), 1)
    local_start = doc_ref[...] - rank_ref[1] * (rows * pl.num_programs(0))
    by_row = jnp.concatenate(
        [
            jnp.log(keep_ref[...]),
            jnp.log(carry_ref[...]),
            local_start.astype(F32),
            jnp.zeros((7 - 2 * heads, rows), F32),
        ],
        0,
    )
    first = by_row.astype(BF16).astype(F32)
    second = (by_row - first).astype(BF16).astype(F32)
    third = by_row - first - second
    split = jnp.concatenate([first, second, third, jnp.zeros((8, rows), F32)], 0).astype(BF16)
    upto = (right <= below).astype(BF16)
    same = (right == below).astype(BF16)
    rows_sum = mm(split, (below <= right).astype(BF16))
    rows_sum = rows_sum[0:8] + rows_sum[8:16] + rows_sum[16:24]
    cols_sum = mm(upto, split, NT)
    cols_sum = cols_sum[:, 0:8] + cols_sum[:, 8:16] + cols_sum[:, 16:24]
    at = 2 * heads
    starts = mm(same, split, NT)
    starts = starts[:, at : at + 1] + starts[:, at + 8 : at + 9] + starts[:, at + 16 : at + 17]
    start_at = starts.astype(jnp.int32)
    linked = (right <= below) & (base + right >= start_at)
    fresh = start_at < base
    reaches_end = base + iota((rows, 1), 0) >= start_at[rows - 1 : rows]
    lane = iota((rows, DH), 1)
    aux = jnp.where(lane == START_AT, starts, 0.0)
    for h in range(heads):
        keep_col, keep_row = cols_sum[:, h : h + 1], rows_sum[h : h + 1]
        carry_col = cols_sum[:, heads + h : heads + h + 1]
        carry_row = rows_sum[heads + h : heads + h + 1]
        keep_mat = jnp.where(linked, jnp.exp(jnp.minimum(keep_col - keep_row, 0.0)), 0.0)
        carry_mat = jnp.where(linked, jnp.exp(jnp.minimum(carry_col - carry_row, 0.0)), 0.0)
        keep_low = keep_mat.astype(BF16)
        kernel = mm(keep_low, carry_mat.astype(BF16))
        kmat_out[h, 0] = kernel.astype(BF16)
        keep_weight = jnp.where(fresh, jnp.exp(keep_col), 0.0)
        carried = jnp.where(fresh, jnp.exp(carry_col), 0.0)
        cross = mm(keep_low, jnp.broadcast_to(carried, (rows, DH)).astype(BF16))
        last = jnp.broadcast_to(kernel[rows - 1 : rows], (16, rows)).astype(BF16)
        end_kernel = mm(same, last, NT)[:, 0:1]
        end_carry = jnp.where(
            reaches_end, jnp.exp(jnp.minimum(carry_col[rows - 1 : rows] - carry_col, 0.0)), 0.0
        )
        for slot, column in enumerate((keep_weight, cross, carried, end_kernel, end_carry)):
            aux = jnp.where(lane == slot * heads + h, column, aux)
    aux_out[...] = aux


def prepare(rank, doc, keep, carry):
    heads, total = keep.shape
    count = total // MBLK
    by_token = lambda n: pl.BlockSpec((n, MBLK), lambda b, *_: (0, b))
    return call(
        functools.partial(prepare_kernel, heads=heads),
        (count,),
        [by_token(1), by_token(heads), by_token(heads)],
        [
            pl.BlockSpec((heads, 1, MBLK, MBLK), lambda b, *_: (0, b, 0, 0)),
            pl.BlockSpec((MBLK, DH), lambda b, *_: (b, 0)),
        ],
        [sds((heads, count, MBLK, MBLK), BF16), sds((total, DH), F32)],
        flops=4e8,
        moved=2e6,
        prefetch=1,
        ins="hhh",
    )(rank, doc, keep, carry)


def front_kernel(rank_ref, *refs, heads):
    blocks, smalls = refs[:REL], refs[REL : 2 * REL]
    (
        w_ref,
        conv_ref,
        aux_ref,
        x_out,
        hid_out,
        proj_out,
        qkv_out,
        part_out,
        halo_out,
        gain_out,
        state_out,
        load_out,
        small_sc,
        proj_sc,
        state_sc,
    ) = refs[2 * REL :]
    b = pl.program_id(0)
    rank = rank_ref[0]
    rows, width = blocks[0].shape
    local = heads * DH
    spans = [pl.ds(pl.multiple_of((rank ^ k) * width, width), width) for k in range(REL)]
    for k in range(REL):
        x_out[:, spans[k]] = blocks[k][...]
    scal = 2 * heads * DH

    @pl.when(b == 0)
    def _():
        for k in range(REL):
            small_sc[:, spans[k]] = smalls[k][...]
        small = small_sc[...].astype(F32)
        gain_out[...] = small
        scale = lax.rsqrt(jnp.mean(small * small, -1, keepdims=True) + EPSILON)
        hidden = (small * scale * small[8:9]).astype(BF16)
        for c in range(3):
            proj_sc[0:8, c * local : (c + 1) * local] = mm(hidden, w_ref[c])[0:8]
        halo_out[...] = proj_sc[0:8]
        state_sc[0:scal] = jnp.zeros((scal, DH), F32)
        row = iota((8, DH), 0)
        state_sc[scal : scal + 8] = jnp.where(
            (row < heads) | ((row >= 2 * heads) & (row < 3 * heads)), 1.0, 0.0
        ).astype(F32)

    gain = gain_out[8:9]
    x = x_out[...].astype(F32)
    scale = lax.rsqrt(jnp.mean(x * x, -1, keepdims=True) + EPSILON)
    hidden = (x * scale * gain).astype(BF16)
    hid_out[...] = hidden
    for c in range(3):
        proj_sc[8 : 8 + rows, c * local : (c + 1) * local] = mm(hidden, w_ref[c])
    place = b * rows + iota((rows, 1), 0)
    starts = aux_ref[:, START_AT : START_AT + 1].astype(jnp.int32)
    mixed = jnp.zeros((rows, 3 * local), F32)
    for j in range(KW):
        inside = (place - j >= starts).astype(F32)
        mixed = mixed + conv_ref[j : j + 1] * proj_sc[8 - j : 8 - j + rows] * inside
    rounded = mixed.astype(BF16)
    qkv_out[...] = rounded
    proj_out[...] = proj_sc[8 : 8 + rows].astype(BF16)
    proj_sc[0:8] = proj_sc[rows : rows + 8]
    end = slice(rows - 1, rows)
    for h in range(heads):
        column = lambda slot: aux_ref[:, slot * heads + h : slot * heads + h + 1]
        keys = rounded[:, local + h * DH : local + (h + 1) * DH]
        values = rounded[:, 2 * local + h * DH : 2 * local + (h + 1) * DH].astype(F32)
        weighted = jnp.concatenate([values * column(3), values * column(4)], 1).astype(BF16)
        part = mm(weighted, keys, TN)
        mem_part, mom_part = part[0:DH], part[DH : 2 * DH]
        lo, mid = h * DH, (heads + h) * DH
        part_out[0, lo : lo + DH] = mem_part.astype(BF16)
        part_out[0, mid : mid + DH] = mom_part.astype(BF16)
        keep_end, cross_end, carry_end = [
            jnp.broadcast_to(column(slot)[end], (1, DH)) for slot in range(3)
        ]
        memory, momentum = state_sc[lo : lo + DH], state_sc[mid : mid + DH]
        state_sc[lo : lo + DH] = keep_end * memory + cross_end * momentum + mem_part
        state_sc[mid : mid + DH] = carry_end * momentum + mom_part
        keep_at, cross_at, carry_at = scal + h, scal + heads + h, scal + 2 * heads + h
        keep_dev = state_sc[keep_at : keep_at + 1]
        cross_dev = state_sc[cross_at : cross_at + 1]
        carry_dev = state_sc[carry_at : carry_at + 1]
        state_sc[keep_at : keep_at + 1] = keep_end * keep_dev
        state_sc[cross_at : cross_at + 1] = keep_end * cross_dev + cross_end * carry_dev
        state_sc[carry_at : carry_at + 1] = carry_end * carry_dev

    @pl.when(b == pl.num_programs(0) - 1)
    def _():
        state_out[...] = state_sc[...]
        pack_load(load_out, state_sc[...], scal)


def pack_load(load_out, state, scal):
    load_out[0:scal] = state[0:scal].astype(BF16)
    tail = state[scal : scal + 8]
    high = tail.astype(BF16).astype(F32)
    load_out[scal : scal + 16] = jnp.concatenate([high, tail - high], 0).astype(BF16)


def front(rank, blocks, smalls, weight, conv, aux, heads):
    total, width = blocks[0].shape
    model = width * REL
    local = heads * DH
    count = total // MBLK
    scal = 2 * heads * DH
    at = lambda b, *_: (b, 0)
    return call(
        functools.partial(front_kernel, heads=heads),
        (count,),
        [pl.BlockSpec((MBLK, width), at)] * REL
        + [whole(smalls[0].shape)] * REL
        + [
            whole(weight.shape),
            whole(conv.shape),
            pl.BlockSpec((MBLK, DH), at),
        ],
        [
            pl.BlockSpec((MBLK, model), at),
            pl.BlockSpec((MBLK, model), at),
            pl.BlockSpec((MBLK, 3 * local), at),
            pl.BlockSpec((MBLK, 3 * local), at),
            pl.BlockSpec((1, scal, DH), lambda b, *_: (b, 0, 0)),
            whole((8, 3 * local)),
            whole((16, model)),
            whole((scal + 8, DH)),
            whole((scal + 16, DH)),
        ],
        [
            sds((total, model), BF16),
            sds((total, model), BF16),
            sds((total, 3 * local), BF16),
            sds((total, 3 * local), BF16),
            sds((count, scal, DH), BF16),
            sds((8, 3 * local), F32),
            sds((16, model), F32),
            sds((scal + 8, DH), F32),
            sds((scal + 16, DH), BF16),
        ],
        [
            pltpu.VMEM((16, model), BF16),
            pltpu.VMEM((MBLK + 8, 3 * local), F32),
            pltpu.VMEM((scal + 8, DH), F32),
        ],
        flops=2.2e9,
        moved=12e6,
        prefetch=1,
        ins="h" * (2 * REL) + "hho",
        outs="hhhoooooo",
    )(rank, *blocks, *smalls, weight, conv, aux)


def compose(first, second, heads, backward):
    scal = 2 * heads * DH
    memory, momentum, keeps, crosses, carries = [], [], [], [], []
    for h in range(heads):
        lo, mid = h * DH, (heads + h) * DH
        at = [scal + c * heads + h for c in range(3)]
        keep_one, cross_one, carry_one = [first[n : n + 1] for n in at]
        keep_two, cross_two, carry_two = [second[n : n + 1] for n in at]
        mem_one, mom_one = first[lo : lo + DH], first[mid : mid + DH]
        mem_two, mom_two = second[lo : lo + DH], second[mid : mid + DH]
        if backward:
            memory.append(mem_two + keep_two * mem_one)
            momentum.append(mom_two + cross_two * mem_one + carry_two * mom_one)
            crosses.append(cross_two * keep_one + carry_two * cross_one)
        else:
            memory.append(keep_two * mem_one + cross_two * mom_one + mem_two)
            momentum.append(carry_two * mom_one + mom_two)
            crosses.append(keep_two * cross_one + cross_two * carry_one)
        keeps.append(keep_two * keep_one)
        carries.append(carry_two * carry_one)
    rest = [jnp.zeros((8 - 3 * heads, DH), F32)]
    return jnp.concatenate(memory + momentum + keeps + crosses + carries + rest, 0)


def unpack(ref, scal):
    tail = ref[scal : scal + 16].astype(F32)
    return jnp.concatenate([ref[0:scal].astype(F32), tail[0:8] + tail[8:16]], 0)


def last_join_kernel(rank_ref, got_ref, prefix_ref, prefix_out, *, bit, heads, backward):
    later = (rank_ref[1] & bit) == (0 if backward else bit)

    @pl.when(later)
    def _():
        got = unpack(got_ref, 2 * heads * DH)
        prefix_out[...] = compose(got, prefix_ref[...], heads, backward)

    @pl.when(jnp.logical_not(later))
    def _():
        prefix_out[...] = prefix_ref[...]


def last_join(rank, got, prefix, bit, heads, backward, after):
    return call(
        functools.partial(last_join_kernel, bit=bit, heads=heads, backward=backward),
        (1,),
        [whole(got.shape), whole(prefix.shape)],
        [whole(prefix.shape)],
        [sds(prefix.shape, F32)],
        flops=1e6,
        moved=1e6,
        prefetch=1,
        after=after,
    )(rank, got, prefix)[0]


def join_kernel(rank_ref, got_ref, total_ref, prefix_ref, *outs, bit, heads, backward):
    total_out, prefix_out, load_out = outs
    scal = 2 * heads * DH
    later = (rank_ref[1] & bit) == (0 if backward else bit)
    got = unpack(got_ref, scal)

    @pl.when(later)
    def _():
        total_out[...] = compose(got, total_ref[...], heads, backward)
        prefix_out[...] = compose(got, prefix_ref[...], heads, backward)

    @pl.when(jnp.logical_not(later))
    def _():
        total_out[...] = compose(total_ref[...], got, heads, backward)
        prefix_out[...] = prefix_ref[...]

    pack_load(load_out, total_out[...], scal)


def join(rank, got, total, prefix, bit, heads, backward, after):
    scal = 2 * heads * DH
    state = (scal + 8, DH)
    return call(
        functools.partial(join_kernel, bit=bit, heads=heads, backward=backward),
        (1,),
        [whole(got.shape), whole(state), whole(state)],
        [whole(state), whole(state), whole((scal + 16, DH))],
        [sds(state, F32), sds(state, F32), sds((scal + 16, DH), BF16)],
        flops=1e6,
        moved=1e6,
        prefetch=1,
        after=after,
    )(rank, got, total, prefix)


def entering(rank, load, total, heads, backward, beside):
    count = lax.axis_size("seq")
    row = iota(total.shape, 0) - 2 * heads * DH
    one = ((row >= 0) & (row < heads)) | ((row >= 2 * heads) & (row < 3 * heads))
    prefix = one.astype(F32)
    bit, lap = 1, 0
    while bit < count:
        after = beside[lap](load) if lap < len(beside) else ()
        got = swap(load, "seq", bit)
        if 2 * bit >= count:
            return last_join(rank, got, prefix, bit, heads, backward, after)
        total, prefix, load = join(rank, got, total, prefix, bit, heads, backward, after)
        bit, lap = bit * 2, lap + 1


def attend_kernel(q_ref, k_ref, v_ref, fix_ref, aux_ref, *outs):
    for i in range(k_ref.shape[0] // MBLK):

        @pl.when(pl.program_id(0) == i)
        def _():
            attend_block(i, q_ref, k_ref, v_ref, fix_ref, aux_ref, *outs)


def attend_block(
    i,
    q_ref,
    k_ref,
    v_ref,
    fix_ref,
    aux_ref,
    att_out,
    ratio_out,
    prob_out,
    fixp_out,
):
    fixed_keys, fixed_values = fix_ref[0], fix_ref[1]
    factor = DH ** (-0.5)
    span = slice(i * MBLK, (i + 1) * MBLK)
    seen = (i + 1) * MBLK
    query = q_ref[...]
    starts = aux_ref[:, START_AT : START_AT + 1].astype(jnp.int32)
    raw = mm(query, k_ref[0:seen], NT)
    fixed = mm(query, fixed_keys, NT)
    key_at = iota((MBLK, seen), 1)
    ok = (key_at >= starts) & (key_at <= i * MBLK + iota((MBLK, seen), 0))
    raw = jnp.where(ok, raw, MASKED)
    top = jnp.maximum(jnp.max(raw, -1, keepdims=True), jnp.max(fixed, -1, keepdims=True))
    weights = jnp.exp((raw - top) * factor)
    fix_weights = jnp.exp((fixed - top) * factor)
    scale = 1.0 / (
        jnp.sum(weights, -1, keepdims=True) + jnp.sum(fix_weights, -1, keepdims=True)
    )
    low = (weights * scale).astype(BF16)
    fix_low = (fix_weights * scale).astype(BF16)
    prob_out[:, 0:seen] = low
    fixp_out[...] = fix_low
    attended = mm(low, v_ref[0:seen]) + mm(fix_low, fixed_values)
    held = jnp.sum(low.astype(F32), -1, keepdims=True) + jnp.sum(
        fix_low.astype(F32), -1, keepdims=True
    )
    att_out[...] = attended
    ratio_out[...] = attended / held


def attend(qkv, fixed, aux, head, heads, after):
    total = qkv.shape[0]
    count = total // MBLK
    fixed_count = fixed.shape[1]
    lanes = lambda c: pl.BlockSpec((total, DH), lambda i: (0, c * heads + head))
    at = lambda i: (i, 0)
    return call(
        attend_kernel,
        (count,),
        [
            pl.BlockSpec((MBLK, DH), lambda i: (i, head)),
            lanes(1),
            lanes(2),
            pl.BlockSpec((2, fixed_count, DH), lambda i: (0, 0, head)),
            pl.BlockSpec((MBLK, DH), at),
        ],
        [pl.BlockSpec((MBLK, DH), at)] * 2
        + [pl.BlockSpec((MBLK, total), at), pl.BlockSpec((MBLK, fixed_count), at)],
        [sds((total, DH), F32)] * 2
        + [sds((total, total), BF16), sds((total, fixed_count), BF16)],
        flops=1.5e9,
        moved=8e6,
        after=after,
        outs="ohhh",
    )(qkv, qkv, qkv, fixed, aux)


def within_kernel(qkv_ref, kmat_ref, out_ref, *, heads):
    local = heads * DH
    for h in range(heads):
        lo = h * DH
        near = mm(qkv_ref[:, lo : lo + DH], qkv_ref[:, local + lo : local + lo + DH], NT)
        weights = (kmat_ref[h, 0].astype(F32) * near).astype(BF16)
        out_ref[:, lo : lo + DH] = mm(weights, qkv_ref[:, 2 * local + lo : 2 * local + lo + DH])


def within(qkv, kmat, after):
    total = qkv.shape[0]
    heads, count = kmat.shape[:2]
    at = lambda b: (b, 0)
    return call(
        functools.partial(within_kernel, heads=heads),
        (count,),
        [
            pl.BlockSpec((MBLK, qkv.shape[1]), at),
            pl.BlockSpec((heads, 1, MBLK, MBLK), lambda b: (0, b, 0, 0)),
        ],
        [pl.BlockSpec((MBLK, heads * DH), at)],
        [sds((total, heads * DH), F32)],
        flops=3e8,
        moved=4e6,
        after=after,
    )(qkv, kmat)[0]


def within_back_kernel(qkv_ref, kmat_ref, gm_ref, out_ref, *, heads):
    local = heads * DH
    for h in range(heads):
        lo = h * DH
        query, keys, values = [
            qkv_ref[:, c * local + lo : c * local + lo + DH] for c in range(3)
        ]
        grad = gm_ref[:, lo : lo + DH]
        kernel = kmat_ref[h, 0].astype(F32)
        near = (kernel * mm(query, keys, NT)).astype(BF16)
        cross = (kernel * mm(grad, values, NT)).astype(BF16)
        out_ref[:, lo : lo + DH] = mm(cross, keys)
        out_ref[:, local + lo : local + lo + DH] = mm(cross, query, TN)
        out_ref[:, 2 * local + lo : 2 * local + lo + DH] = mm(near, grad, TN)


def within_back(qkv, kmat, gm, after):
    total, columns = qkv.shape
    heads, count = kmat.shape[:2]
    at = lambda b: (b, 0)
    return call(
        functools.partial(within_back_kernel, heads=heads),
        (count,),
        [
            pl.BlockSpec((MBLK, columns), at),
            pl.BlockSpec((heads, 1, MBLK, MBLK), lambda b: (0, b, 0, 0)),
            pl.BlockSpec((MBLK, heads * DH), at),
        ],
        [pl.BlockSpec((MBLK, columns), at)],
        [sds((total, columns), F32)],
        flops=6e8,
        moved=6e6,
        after=after,
    )(qkv, kmat, gm)[0]


def attend_back_kernel(*refs):
    count = pl.num_programs(0)
    total = refs[1].shape[0]
    for i in range(total // MBLK):

        @pl.when(count - 1 - pl.program_id(0) == i)
        def _():
            attend_back_block(i, *refs)


def attend_back_block(
    i,
    q_ref,
    k_ref,
    v_ref,
    fix_ref,
    prob_ref,
    fixp_ref,
    ratio_ref,
    grad_ref,
    dq_out,
    dk_out,
    dv_out,
    dfix_out,
):
    fixed_keys, fixed_values = fix_ref[0], fix_ref[1]
    factor = DH ** (-0.5)
    span = slice(i * MBLK, (i + 1) * MBLK)
    seen = (i + 1) * MBLK
    query, grad = q_ref[...], grad_ref[...]
    delta = jnp.sum(grad.astype(F32) * ratio_ref[...], -1, keepdims=True)
    low, fix_low = prob_ref[:, 0:seen], fixp_ref[...]
    back = mm(grad, v_ref[0:seen], NT)
    fix_back = mm(grad, fixed_values, NT)
    grad_raw = (low.astype(F32) * (back - delta) * factor).astype(BF16)
    fix_raw = (fix_low.astype(F32) * (fix_back - delta) * factor).astype(BF16)
    dk, dv = mm(grad_raw, query, TN), mm(low, grad, TN)
    dfix_k, dfix_v = mm(fix_raw, query, TN), mm(fix_low, grad, TN)
    if seen == k_ref.shape[0]:
        dk_out[...] = dk
        dv_out[...] = dv
        dfix_out[0] = dfix_k
        dfix_out[1] = dfix_v
    else:
        dk_out[0:seen] += dk
        dv_out[0:seen] += dv
        dfix_out[0] += dfix_k
        dfix_out[1] += dfix_v
    dq_out[...] = mm(grad_raw, k_ref[0:seen]) + mm(fix_raw, fixed_keys)


def attend_back(qkv, fixed, prob, fixp, ratio, grads, head, heads, after):
    total = qkv.shape[0]
    count = total // MBLK
    fixed_count = fixed.shape[1]
    lanes = lambda c: pl.BlockSpec((total, DH), lambda s: (0, c * heads + head))
    at = lambda s: (count - 1 - s, 0)
    of_head = pl.BlockSpec((MBLK, DH), lambda s: (count - 1 - s, head))
    return call(
        attend_back_kernel,
        (count,),
        [
            of_head,
            lanes(1),
            lanes(2),
            pl.BlockSpec((2, fixed_count, DH), lambda s: (0, 0, head)),
            pl.BlockSpec((MBLK, total), at),
            pl.BlockSpec((MBLK, fixed_count), at),
            pl.BlockSpec((MBLK, DH), at),
            of_head,
        ],
        [pl.BlockSpec((MBLK, DH), at)] + [whole((total, DH))] * 2 + [whole((2, fixed_count, DH))],
        [sds((total, DH), F32)] * 3 + [sds((2, fixed_count, DH), F32)],
        flops=3e9,
        moved=10e6,
        after=after,
        ins="oooohhho",
        outs="hhho",
    )(qkv, qkv, qkv, fixed, prob, fixp, ratio, grads)


def merge_kernel(q_ref, *refs, heads):
    atts = refs[:heads]
    (
        intra_ref,
        aux_ref,
        part_ref,
        state_ref,
        merged_out,
        normed_out,
        scale_out,
        state_low,
        state_sc,
    ) = refs[heads:]
    rows = q_ref.shape[0]
    lane = iota((rows, DH), 1)
    scales = jnp.zeros((rows, DH), F32)

    @pl.when(pl.program_id(0) == 0)
    def _():
        state_sc[...] = state_ref[0 : state_sc.shape[0]]

    for h in range(heads):
        lo, mid = h * DH, (heads + h) * DH
        memory, momentum = state_sc[lo : lo + DH], state_sc[mid : mid + DH]
        memory_low, momentum_low = memory.astype(BF16), momentum.astype(BF16)
        state_low[0, lo : lo + DH] = memory_low
        state_low[0, mid : mid + DH] = momentum_low
        query = q_ref[:, lo : lo + DH]
        keep = aux_ref[:, h : h + 1]
        cross = aux_ref[:, heads + h : heads + h + 1]
        carry = aux_ref[:, 2 * heads + h : 2 * heads + h + 1]
        out = (
            intra_ref[:, lo : lo + DH]
            + keep * mm(query, memory_low, NT)
            + cross * mm(query, momentum_low, NT)
        )
        scale = lax.rsqrt(jnp.mean(out * out, -1, keepdims=True) + MEMORY_FLOOR)
        normed = out * scale
        normed_out[:, lo : lo + DH] = normed.astype(BF16)
        scales = jnp.where(lane == h, scale, scales)
        merged_out[:, lo : lo + DH] = (atts[h][...] + normed).astype(BF16)
        end = slice(rows - 1, rows)
        state_sc[lo : lo + DH] = (
            keep[end] * memory + cross[end] * momentum + part_ref[0, lo : lo + DH].astype(F32)
        )
        state_sc[mid : mid + DH] = (
            carry[end] * momentum + part_ref[0, mid : mid + DH].astype(F32)
        )
    scale_out[...] = scales


def merge(qkv, atts, intra, aux, parts, state, heads, after):
    total = qkv.shape[0]
    count = total // MBLK
    local = heads * DH
    scal = 2 * local
    at = lambda b, *_: (b, 0)
    by_block = pl.BlockSpec((1, scal, DH), lambda b, *_: (b, 0, 0))
    return call(
        functools.partial(merge_kernel, heads=heads),
        (count,),
        [pl.BlockSpec((MBLK, local), at)]
        + [pl.BlockSpec((MBLK, DH), at)] * heads
        + [pl.BlockSpec((MBLK, local), at), pl.BlockSpec((MBLK, DH), at)]
        + [by_block, whole(state.shape)],
        [
            pl.BlockSpec((MBLK, local), at),
            pl.BlockSpec((MBLK, local), at),
            pl.BlockSpec((MBLK, DH), at),
            by_block,
        ],
        [
            sds((total, local), BF16),
            sds((total, local), BF16),
            sds((total, DH), F32),
            sds((count, scal, DH), BF16),
        ],
        [pltpu.VMEM((scal, DH), F32)],
        flops=3e8,
        moved=6e6,
        after=after,
        outs="ohhh",
    )(qkv, *atts, intra, aux, parts, state)


def quarter(p, rank_ref):
    return rank_ref[0] ^ ((1 - (p >> 1)) | ((p & 1) << 1))


def middle_kernel(rank_ref, *refs):
    merged, weights = refs[:REL], refs[REL : 2 * REL]
    (
        x_ref,
        gain_ref,
        hid_out,
        normed_out,
        scale_out,
        share_out,
        mid_sc,
        merged_sc,
        weight_sc,
    ) = refs[2 * REL :]
    width = share_out.shape[1]
    local = merged[0].shape[1]

    @pl.when(pl.program_id(0) == 0)
    def _():
        for k in range(REL):
            for q in range(REL):
                weight_sc[k * local : (k + 1) * local, q * width : (q + 1) * width] = weights[k][
                    q * local : (q + 1) * local
                ]

    for k in range(REL):
        merged_sc[:, k * local : (k + 1) * local] = merged[k][...]
    middle = x_ref[...].astype(F32) + mm(merged_sc[...], weight_sc[...])
    mid_sc[...] = middle
    scale = lax.rsqrt(jnp.mean(middle * middle, -1, keepdims=True) + EPSILON)
    normed = middle * scale
    hid_out[...] = (normed * gain_ref[9:10]).astype(BF16)

    @pl.when(pl.program_id(0) == REL // 2)
    def _():
        normed_out[...] = normed
        scale_out[...] = scale

    share_out[...] = mid_sc[:, pl.ds(pl.multiple_of(rank_ref[0] * width, width), width)]


def middle(rank, merged, weights, x, gains, after):
    total, model = x.shape
    local = merged[0].shape[1]
    width = model // REL
    rows = total // REL
    at = lambda p, r: (quarter(p, r), 0)
    return call(
        middle_kernel,
        (total // rows,),
        [pl.BlockSpec((rows, local), at)] * REL
        + [pl.BlockSpec((REL * local, width), lambda *_: (total // (REL * local), 0))] * REL
        + [pl.BlockSpec((rows, model), at), whole(gains.shape)],
        [
            pl.BlockSpec((rows, model), lambda p, r: (p, 0)),
            whole((rows, model)),
            whole((rows, 1)),
            pl.BlockSpec((rows, width), at),
        ],
        [
            sds((total, model), BF16),
            sds((rows, model), F32),
            sds((rows, 1), F32),
            sds((total, width), F32),
        ],
        [
            pltpu.VMEM((rows, model), F32),
            pltpu.VMEM((rows, REL * local), BF16),
            pltpu.VMEM((REL * local, model), BF16),
        ],
        flops=2.2e9,
        moved=10e6,
        prefetch=1,
        after=after,
        ins="o" * (2 * REL) + "ho",
        outs="ohhh",
    )(rank, *merged, *weights, x, gains)


def recall_kernel(rank_ref, *refs):
    cots = refs[:REL]
    down_ref, act_out, cot_out, _ = refs[REL:]
    rank = rank_ref[0]
    width = cots[0].shape[1]
    for k in range(REL):
        span = pl.ds(pl.multiple_of((rank ^ k) * width, width), width)
        cot_out[:, span] = cots[k][...]
    act_out[...] = mm(cot_out[...], down_ref[...], NT).astype(BF16)


def recall(rank, cots, total, down, after):
    width = cots[0].shape[1]
    units, model = down.shape
    rows = total // REL
    at = lambda p, r: (p, 0)
    return call(
        recall_kernel,
        (REL,),
        [pl.BlockSpec((rows, width), lambda p, r: (quarter(p, r), 0))] * REL + [whole(down.shape)],
        [
            pl.BlockSpec((rows, units), at),
            pl.BlockSpec((rows, model), at),
            pl.BlockSpec(memory_space=pl.ANY),
        ],
        [
            sds((total, units), BF16),
            sds((total, model), BF16),
            sds((3, total, units), BF16),
        ],
        flops=1.5e9,
        moved=7e6,
        prefetch=1,
        after=after,
        outs="ohh",
    )(rank, *cots, down)


def ffn_kernel(hid_ref, grad_ref, gate_ref, _, trio_out, back_out):
    rows = back_out.shape[1]
    hidden = hid_ref[...]
    gate = mm(hidden, gate_ref[0], NT)
    up = mm(hidden, gate_ref[1], NT)
    grad_act = grad_ref[...].astype(F32)
    sig = jax.nn.sigmoid(gate)
    silu = gate * sig
    trio_out[0] = (silu * up).astype(BF16)
    grad_gate = (grad_act * up * (sig * (1.0 + gate * (1.0 - sig)))).astype(BF16)
    grad_up = (grad_act * silu).astype(BF16)
    trio_out[1] = grad_gate
    trio_out[2] = grad_up
    back = mm(grad_gate, gate_ref[0]) + mm(grad_up, gate_ref[1])
    for i in range(2):
        back_out[i] = back[i * rows : (i + 1) * rows].astype(BF16)


def ffn(hidden, grad_act, gate_up, trio, part):
    total, model = hidden.shape
    units = grad_act.shape[1]
    rows = total // REL
    at = lambda s: (part, 0)
    return call(
        ffn_kernel,
        (1,),
        [
            pl.BlockSpec((2 * rows, model), at),
            pl.BlockSpec((2 * rows, units), at),
            whole(gate_up.shape),
            pl.BlockSpec(memory_space=pl.ANY),
        ],
        [pl.BlockSpec((3, 2 * rows, units), lambda s: (0, part, 0)), whole((2, rows, model))],
        [sds((3, total, units), BF16), sds((2, rows, model), BF16)],
        flops=3e9,
        moved=8e6,
        alias={3: 0},
        ins="oooh",
        outs="hh",
        spare=10,
    )(hidden, grad_act, gate_up, trio)


def answer_kernel(rank_ref, act_ref, down_ref, send_out, far_out, keep_out):
    rank = rank_ref[0]
    width = keep_out.shape[1]
    spans = [pl.ds(pl.multiple_of((rank ^ k) * width, width), width) for k in range(REL)]
    act = act_ref[0]
    keep_out[...] = mm(act, down_ref[:, spans[0]]).astype(BF16)
    send_out[0] = mm(act, down_ref[:, spans[1]]).astype(BF16)
    far_out[...] = mm(act, down_ref[:, spans[2]]).astype(BF16)
    send_out[1] = mm(act, down_ref[:, spans[3]]).astype(BF16)


def answer(rank, trio, down, after):
    _, total, units = trio.shape
    width = down.shape[1] // REL
    rows = total // REL
    at = lambda p, r: (quarter(p, r), 0)
    return call(
        answer_kernel,
        (REL,),
        [pl.BlockSpec((1, rows, units), lambda p, r: (0, p, 0)), whole(down.shape)],
        [
            pl.BlockSpec((2, rows, width), lambda p, r: (0, quarter(p, r), 0)),
            pl.BlockSpec((rows, width), at),
            pl.BlockSpec((rows, width), at),
        ],
        [sds((2, total, width), BF16), sds((total, width), BF16), sds((total, width), BF16)],
        flops=1.5e9,
        moved=5e6,
        prefetch=1,
        after=after,
        ins="ho",
        outs="hhh",
    )(rank, trio, down)


def seats(bits):
    levels = [[0]]
    for bit in reversed(bits):
        levels.insert(0, [bit | r for level in levels for r in level])
    return levels


def deal(product, outs, bits, seat, by_rows):
    for out, level in zip(outs, seats(bits)):
        chunk = out.shape[2 if by_rows else 3]
        for slot, r in enumerate(level):
            span = pl.ds(pl.multiple_of((seat ^ r) * chunk, chunk), chunk)
            out[slot, 0] = (product[span] if by_rows else product[:, span]).astype(BF16)


def harvest_kernel(rank_ref, cot_ref, hid_ref, trio_ref, *outs, orders, by_rows):
    acc = outs[-1]
    levels = len(orders[0]) + 1
    for i, bits in enumerate(orders):

        @pl.when(pl.program_id(0) == i)
        def _():
            wide = hid_ref[...] if i else cot_ref[...]
            acc[...] = mm(wide, trio_ref[0], TN) if by_rows else mm(trio_ref[0], wide, TN)
            deal(acc, outs[i * levels : (i + 1) * levels], bits, rank_ref[1], by_rows)


def harvest(rank, cot, hidden, trio, orders, after):
    _, total, units = trio.shape
    model = cot.shape[1]
    chunk = model // 2 ** len(orders[0])
    by_rows = chunk % DH != 0
    cut = (chunk, units) if by_rows else (units, chunk)
    shapes = [(len(level), 1) + cut for bits in orders for level in seats(bits)]
    outs = call(
        functools.partial(harvest_kernel, orders=orders, by_rows=by_rows),
        (len(orders),),
        [
            whole(cot.shape),
            whole(hidden.shape),
            pl.BlockSpec((1, total, units), lambda p, r: (p, 0, 0)),
        ],
        [whole(shape) for shape in shapes],
        [sds(shape, BF16) for shape in shapes],
        [pltpu.VMEM((model, units) if by_rows else (units, model), F32)],
        flops=6 * total * model * units,
        moved=1.2e7,
        prefetch=1,
        after=after,
        ins="hoh",
        outs="h" * len(shapes),
    )(rank, cot, hidden, trio)
    levels = len(orders[0]) + 1
    return [outs[i * levels : (i + 1) * levels] for i in range(len(orders))], by_rows


def reap_kernel(rank_ref, hid_ref, gp_ref, tail_ref, back_ref, *outs, cuts):
    gp_sc, acc = outs[-2:]
    outs = outs[:-2]
    seat = rank_ref[1]
    rows = gp_ref.shape[0]
    gp_sc[...] = gp_ref[...]
    gp_sc[rows - 16 : rows] = repaired(tail_ref, back_ref)
    acc[...] = mm(hid_ref[...], gp_sc[...], TN)
    cut_rows(acc, outs, seat, cuts)


def cut_rows(acc, outs, seat, cuts):
    for bits, lo, hi in cuts:
        levels = seats(bits)
        for out, level in zip(outs, levels):
            chunk = out.shape[1]
            for slot, r in enumerate(level):
                span = pl.ds(pl.multiple_of((seat ^ r) * chunk, chunk), chunk)
                out[slot] = acc[span, lo:hi].astype(BF16)
        outs = outs[len(levels) :]


def repaired(tail_ref, back_ref):
    tail = tail_ref[...]
    return jnp.concatenate([tail[:8], tail[8:] + back_ref[...]], 0).astype(BF16)


def reap(rank, hidden, gp, tail, returned, cuts):
    total, model = hidden.shape
    columns = gp.shape[1]
    shapes = [
        (len(level), model // 2 ** len(bits), hi - lo)
        for bits, lo, hi in cuts
        for level in seats(bits)
    ]
    outs = call(
        functools.partial(reap_kernel, cuts=cuts),
        (1,),
        [whole(a.shape) for a in (hidden, gp, tail, returned)],
        [whole(shape) for shape in shapes],
        [sds(shape, BF16) for shape in shapes],
        [pltpu.VMEM((total, columns), BF16), pltpu.VMEM((model, columns), F32)],
        flops=2 * total * model * columns,
        moved=6e6,
        prefetch=1,
        ins="oooo",
    )(rank, hidden, gp, tail, returned)
    split = len(seats(cuts[0][0]))
    return outs[:split], outs[split:]


def absorb(parts, lap, got):
    parts = list(parts)
    at = 0
    for m in range(lap + 1, len(parts)):
        size = parts[m].shape[0]
        kind = F32 if m == len(parts) - 1 else BF16
        parts[m] = parts[m].astype(kind) + got[at : at + size].astype(kind)
        at += size
    return parts


def bend_kernel(rank_ref, keep_ref, near_ref, far_ref, cot_ref, normed_ref, scale_ref, gain_ref, *outs):
    low_out, dgain_out = outs
    grad = (
        keep_ref[0].astype(F32) + near_ref[0].astype(F32) + far_ref[0].astype(F32)
    )
    normed = normed_ref[...]
    total = jnp.sum(grad * normed, 0, keepdims=True)
    dgain_out[...] = jnp.where(iota(dgain_out.shape, 0) == 1, total, 0.0)
    g = grad * gain_ref[9:10]
    mean = jnp.mean(g * normed, -1, keepdims=True)
    low_out[...] = (cot_ref[...].astype(F32) + scale_ref[...] * (g - normed * mean)).astype(BF16)


def bend(rank, keep, near, far, cot, normed, scale, gains, after):
    total, model = cot.shape
    rows = total // REL
    own = lambda s, r: (REL // 2, 0)
    one = pl.BlockSpec((1, rows, model), lambda *_: (0, 0, 0))
    return call(
        bend_kernel,
        (1,),
        [
            one,
            one,
            one,
            pl.BlockSpec((rows, model), own),
            whole((rows, model)),
            whole((rows, 1)),
            whole(gains.shape),
        ],
        [whole((rows, model)), whole((8, model))],
        [sds((rows, model), BF16), sds((8, model), F32)],
        flops=5e6,
        moved=4e6,
        prefetch=1,
        after=after,
        ins="hoohhhh",
    )(rank, keep, near, far, cot, normed, scale, gains)


def turn_kernel(rank_ref, *refs, heads, bits, by_rows):
    lows = refs[:REL]
    (
        w_ref,
        q_ref,
        normed_ref,
        scale_ref,
        aux_ref,
        merged_ref,
        dev_ref,
        ga_out,
        gm_out,
        part_out,
        share_out,
        state_out,
        load_out,
        *levels_out,
        low_sc,
        acc_sc,
        state_sc,
    ) = refs[REL:]
    step = pl.program_id(0)
    last = pl.num_programs(0) - 1
    block = last - step
    rank = rank_ref[0]
    rows = q_ref.shape[0]
    scal = 2 * heads * DH
    for k in range(REL):

        @pl.when((rank ^ k) == block)
        def _():
            low_sc[...] = lows[k][...]

    @pl.when(step == 0)
    def _():
        state_sc[...] = jnp.zeros_like(state_sc)
        acc_sc[...] = jnp.zeros_like(acc_sc)

    low = low_sc[...]
    if by_rows:
        acc_sc[...] += mm(low, merged_ref[...], TN)
    else:
        acc_sc[...] += mm(merged_ref[...], low, TN)
    width = share_out.shape[1]
    share_out[...] = low_sc[:, pl.ds(pl.multiple_of(rank * width, width), width)]
    grad_merged = mm(low, w_ref[...], NT)
    ga_out[...] = grad_merged.astype(BF16)
    end = slice(rows - 1, rows)
    for h in range(heads):
        lo, mid = h * DH, (heads + h) * DH
        g = grad_merged[:, lo : lo + DH]
        normed = normed_ref[:, lo : lo + DH].astype(F32)
        scale = scale_ref[:, h : h + 1]
        grad = scale * (g - normed * jnp.mean(g * normed, -1, keepdims=True))
        gm_out[:, lo : lo + DH] = grad.astype(BF16)
        query = q_ref[:, lo : lo + DH]
        keep = aux_ref[:, h : h + 1]
        cross = aux_ref[:, heads + h : heads + h + 1]
        carry = aux_ref[:, 2 * heads + h : 2 * heads + h + 1]
        mem_part = mm((keep * grad).astype(BF16), query, TN)
        mom_part = mm((cross * grad).astype(BF16), query, TN)
        part_out[0, lo : lo + DH] = mem_part.astype(BF16)
        part_out[0, mid : mid + DH] = mom_part.astype(BF16)
        memory, momentum = state_sc[lo : lo + DH], state_sc[mid : mid + DH]
        state_sc[lo : lo + DH] = keep[end] * memory + mem_part
        state_sc[mid : mid + DH] = cross[end] * memory + carry[end] * momentum + mom_part

    @pl.when(step == last)
    def _():
        state_sc[scal : scal + 8] = dev_ref[scal : scal + 8]
        state_out[...] = state_sc[...]
        pack_load(load_out, state_sc[...], scal)
        seat = rank_ref[1]
        for out, level in zip(levels_out, seats(bits)):
            chunk = out.shape[1 if by_rows else 2]
            for slot, r in enumerate(level):
                span = pl.ds(pl.multiple_of((seat ^ r) * chunk, chunk), chunk)
                out[slot] = (acc_sc[span] if by_rows else acc_sc[:, span]).astype(BF16)


def turn(rank, lows, weight, qkv, normed, scales, aux, merged, dev, bits, heads):
    total = qkv.shape[0]
    count = total // MBLK
    local, model = weight.shape
    width = model // REL
    scal = 2 * local
    at = lambda b, *_: (count - 1 - b, 0)
    chunk = model // 2 ** len(bits)
    by_rows = chunk % DH != 0
    cut = (chunk, local) if by_rows else (local, chunk)
    levels = [(len(level),) + cut for level in seats(bits)]
    out = call(
        functools.partial(turn_kernel, heads=heads, bits=bits, by_rows=by_rows),
        (count,),
        [whole(lows[0].shape)] * REL
        + [
            whole(weight.shape),
            pl.BlockSpec((MBLK, local), at),
            pl.BlockSpec((MBLK, local), at),
            pl.BlockSpec((MBLK, DH), at),
            pl.BlockSpec((MBLK, DH), at),
            pl.BlockSpec((MBLK, local), at),
            whole(dev.shape),
        ],
        [
            pl.BlockSpec((MBLK, local), at),
            pl.BlockSpec((MBLK, local), at),
            pl.BlockSpec((1, scal, DH), lambda b, *_: (count - 1 - b, 0, 0)),
            pl.BlockSpec((MBLK, width), at),
            whole((scal + 8, DH)),
            whole((scal + 16, DH)),
        ]
        + [whole(shape) for shape in levels],
        [
            sds((total, local), BF16),
            sds((total, local), BF16),
            sds((count, scal, DH), BF16),
            sds((total, width), BF16),
            sds((scal + 8, DH), F32),
            sds((scal + 16, DH), BF16),
        ]
        + [sds(shape, BF16) for shape in levels],
        [
            pltpu.VMEM((MBLK, model), BF16),
            pltpu.VMEM((model, local) if by_rows else (local, model), F32),
            pltpu.VMEM((scal + 8, DH), F32),
        ],
        flops=8e8,
        moved=8e6,
        prefetch=1,
        ins="o" * (REL + 2) + "hhooo",
        outs="ooohoo" + "o" * len(levels),
    )(rank, *lows, weight, qkv, normed, scales, aux, merged, dev)
    return out[:6], out[6:], by_rows


def settle_kernel(qkv_ref, *refs, heads):
    rests = refs[: 3 * heads]
    (
        within_ref,
        gm_ref,
        aux_ref,
        low_ref,
        part_ref,
        state_ref,
        proj_ref,
        halo_ref,
        conv_ref,
        gp_out,
        tail_out,
        head_out,
        gconv_out,
        _,
        _,
        _,
        state_sc,
        mix_sc,
        tap_sc,
        proj_sc,
    ) = refs[3 * heads :]
    step = pl.program_id(0)
    last = pl.num_programs(0) - 1
    block = last - step
    rows = qkv_ref.shape[0]
    local = heads * DH
    base = block * rows

    @pl.when(step == 0)
    def _():
        state_sc[...] = state_ref[0 : state_sc.shape[0]]
        tap_sc[...] = jnp.zeros_like(tap_sc)
        gconv_out[...] = jnp.zeros_like(gconv_out)

    end = slice(rows - 1, rows)
    for h in range(heads):
        lo, mid = h * DH, (heads + h) * DH
        memory, momentum = state_sc[lo : lo + DH], state_sc[mid : mid + DH]
        memory_low, momentum_low = memory.astype(BF16), momentum.astype(BF16)
        keep = aux_ref[:, h : h + 1]
        cross = aux_ref[:, heads + h : heads + h + 1]
        carry = aux_ref[:, 2 * heads + h : 2 * heads + h + 1]
        end_kernel = aux_ref[:, 3 * heads + h : 3 * heads + h + 1]
        end_carry = aux_ref[:, 4 * heads + h : 4 * heads + h + 1]
        keys = qkv_ref[:, local + lo : local + lo + DH]
        values = qkv_ref[:, 2 * local + lo : 2 * local + lo + DH]
        gmem = gm_ref[:, lo : lo + DH]
        both = lambda a, one, two: jnp.concatenate(
            [a.astype(F32) * one, a.astype(F32) * two], 1
        ).astype(BF16)
        states = jnp.concatenate([low_ref[0, lo : lo + DH], low_ref[0, mid : mid + DH]], 0)
        ends = jnp.concatenate([memory_low, momentum_low], 0)
        wide = jnp.concatenate([memory_low, momentum_low], 1)
        dq = mm(both(gmem, keep, cross), states)
        dk = mm(both(values, end_kernel, end_carry), ends)
        dv = mm(both(keys, end_kernel, end_carry), wide, NT)
        for c, extra in enumerate((dq, dk, dv)):
            mix_sc[:, c * local + lo : c * local + lo + DH] = (
                rests[c * heads + h][...]
                + within_ref[:, c * local + lo : c * local + lo + DH]
                + extra
            )
        state_sc[lo : lo + DH] = keep[end] * memory + part_ref[0, lo : lo + DH].astype(F32)
        state_sc[mid : mid + DH] = (
            cross[end] * memory
            + carry[end] * momentum
            + part_ref[0, mid : mid + DH].astype(F32)
        )
    before = proj_ref[pl.ds(pl.multiple_of(jnp.maximum(base - 16, 0), 16), 16)].astype(F32)[8:16]
    proj_sc[0:8] = jnp.where(block == 0, halo_ref[...], before)
    proj_sc[8 : 8 + rows] = proj_ref[pl.ds(pl.multiple_of(base, rows), rows)].astype(F32)
    place = base + iota((rows, 1), 0)
    starts = aux_ref[:, START_AT : START_AT + 1].astype(jnp.int32)
    mix = mix_sc[...]
    total = conv_ref[0:1] * mix
    gconv_out[0:1] += jnp.sum(mix * proj_sc[8 : 8 + rows], 0, keepdims=True)
    for j in range(1, KW):
        tap_sc[j - 1, 8 + rows : 16 + rows] = tap_sc[j - 1, 8:16]
        tap = mix * (place - j >= starts).astype(F32)
        tap_sc[j - 1, 8 : 8 + rows] = conv_ref[j : j + 1] * tap
        gconv_out[j : j + 1] += jnp.sum(tap * proj_sc[8 - j : 8 - j + rows], 0, keepdims=True)
        total = total + tap_sc[j - 1, 8 + j : 8 + j + rows]
    gp_out[...] = total.astype(BF16)

    @pl.when(step == 0)
    def _():
        tail_out[...] = total[rows - 16 : rows]

    @pl.when(step == last)
    def _():
        head_out[...] = tap_sc[0, 1:9] + tap_sc[1, 2:10] + tap_sc[2, 3:11]


def settle(qkv, grads, inner, gm, aux, lows, parts, state, proj, halo, conv, width, heads):
    total = qkv.shape[0]
    count = total // MBLK
    local = heads * DH
    scal = 2 * local
    at = lambda b, *_: (count - 1 - b, 0)
    by_block = pl.BlockSpec((1, scal, DH), lambda b, *_: (count - 1 - b, 0, 0))
    return call(
        functools.partial(settle_kernel, heads=heads),
        (count,),
        [pl.BlockSpec((MBLK, 3 * local), at)]
        + [pl.BlockSpec((MBLK, DH), at)] * (3 * heads)
        + [
            pl.BlockSpec((MBLK, 3 * local), at),
            pl.BlockSpec((MBLK, local), at),
            pl.BlockSpec((MBLK, DH), at),
            by_block,
            by_block,
            whole(state.shape),
            whole(proj.shape),
            whole(halo.shape),
            whole(conv.shape),
        ],
        [
            pl.BlockSpec((MBLK, 3 * local), at),
            whole((16, 3 * local)),
            whole((8, 3 * local)),
            whole((8, 3 * local)),
        ]
        + [pl.BlockSpec(memory_space=pl.ANY)] * 3,
        [
            sds((total, 3 * local), BF16),
            sds((16, 3 * local), F32),
            sds((8, 3 * local), F32),
            sds((8, 3 * local), F32),
            sds((2, total, width), BF16),
            sds((total, width), BF16),
            sds((total, width), BF16),
        ],
        [
            pltpu.VMEM((scal, DH), F32),
            pltpu.VMEM((MBLK, 3 * local), F32),
            pltpu.VMEM((KW - 1, MBLK + 16, 3 * local), F32),
            pltpu.VMEM((MBLK + 8, 3 * local), F32),
        ],
        flops=6e8,
        moved=14e6,
        ins="o" + "h" * (3 * heads) + "ooohoohoo",
        outs="oooohhh",
    )(qkv, *grads, inner, gm, aux, lows, parts, state, proj, halo, conv)


def back_kernel(
    rank_ref,
    gp_ref,
    tail_ref,
    back_ref,
    w_ref,
    x_ref,
    gain_ref,
    other_ref,
    send_in,
    far_in,
    keep_in,
    send_out,
    far_out,
    keep_out,
    dgain_out,
    grad_sc,
    gp_sc,
    w_sc,
    *,
    last,
):
    rank = rank_ref[0]
    width = keep_out.shape[1]
    local = w_ref.shape[2]

    @pl.when(pl.program_id(0) == 0)
    def _():
        dgain_out[...] = other_ref[...]
        for c in range(3):
            w_sc[:, c * local : (c + 1) * local] = w_ref[c]

    rows = gp_ref.shape[0]
    gp_sc[...] = gp_ref[...]
    if last:
        gp_sc[rows - 16 : rows] = repaired(tail_ref, back_ref)
    grad = mm(gp_sc[...], w_sc[...], NT)
    x = x_ref[...].astype(F32)
    scale = lax.rsqrt(jnp.mean(x * x, -1, keepdims=True) + EPSILON)
    normed = x * scale
    dgain_out[0:1] += jnp.sum(grad * normed, 0, keepdims=True)
    g = grad * gain_ref[8:9]
    grad_sc[...] = (scale * (g - normed * jnp.mean(g * normed, -1, keepdims=True))).astype(BF16)
    spans = [pl.ds(pl.multiple_of((rank ^ k) * width, width), width) for k in range(REL)]
    keep_out[...] = grad_sc[:, spans[0]]
    send_out[0] = grad_sc[:, spans[1]]
    far_out[...] = grad_sc[:, spans[2]]
    send_out[1] = grad_sc[:, spans[3]]


def back(rank, gp, tail, returned, weight, x, gains, dgain, rooms, last, after):
    total, model = x.shape
    width = model // REL
    count = total // MBLK
    first = count - 1 if last else 0
    at = lambda b, *_: (b + first, 0)
    columns = gp.shape[1]
    return call(
        functools.partial(back_kernel, last=last),
        (1 if last else count - 1,),
        [
            pl.BlockSpec((MBLK, columns), at),
            whole(tail.shape),
            whole(returned.shape),
            whole(weight.shape),
            pl.BlockSpec((MBLK, model), at),
            whole(gains.shape),
            whole(dgain.shape),
        ]
        + [pl.BlockSpec(memory_space=pl.ANY)] * 3,
        [
            pl.BlockSpec((2, MBLK, width), lambda b, *_: (0, b + first, 0)),
            pl.BlockSpec((MBLK, width), at),
            pl.BlockSpec((MBLK, width), at),
            whole((8, model)),
        ],
        [
            sds((2, total, width), BF16),
            sds((total, width), BF16),
            sds((total, width), BF16),
            sds((8, model), F32),
        ],
        [
            pltpu.VMEM((MBLK, model), BF16),
            pltpu.VMEM((MBLK, columns), BF16),
            pltpu.VMEM((model, columns), BF16),
        ],
        flops=4e8 if last else 1.3e9,
        moved=2e6 if last else 6e6,
        prefetch=1,
        after=after,
        alias={7: 0, 8: 1, 9: 2},
        ins="oooohoohhh",
        outs="hhho",
    )(rank, gp, tail, returned, weight, x, gains, dgain, *rooms)


def finish_kernel(
    little_ref, more_ref, own_ref, got_ref, last_ref, one_out, two_out, conv_out, fixed_out, qkv_out
):
    total = little_ref[...] + more_ref[...]
    one_out[...] = total[0:1]
    two_out[...] = total[1:2]
    taps, parts, local = conv_out.shape
    for j in range(taps):
        conv_out[j] = total[2 + parts * j : 2 + parts * (j + 1)]
    rest = 2 + taps * parts
    rows = fixed_out.shape[1]
    for c in range(fixed_out.shape[0]):
        fixed_out[c] = total[rest + c * rows : rest + (c + 1) * rows]
    both = own_ref[0] + got_ref[0].astype(F32)
    for c in range(2):
        qkv_out[c] = both[:, c * local : (c + 1) * local]
    qkv_out[2] = last_ref[0]


def finish(little, more, own, got, last, fixed_count):
    local = little.shape[1]
    _, rows, columns = last.shape
    shapes = [
        (1, local),
        (1, local),
        (KW, 3, local),
        (2, fixed_count, local),
        (3, rows, columns),
    ]
    return call(
        finish_kernel,
        (1,),
        [whole(a.shape) for a in (little, more, own, got, last)],
        [whole(shape) for shape in shapes],
        [sds(shape, F32) for shape in shapes],
        moved=1e6,
    )(little, more, own, got, last)


def per_device(
    inputs,
    cotangent,
    norm_gain,
    qkv_weight,
    conv_kernel,
    persistent,
    out_weight,
    ffn_gain,
    gate_up,
    down_weight,
    memory_decay,
    momentum_decay,
    doc_start,
):
    total, width = inputs.shape
    local = qkv_weight.shape[2]
    heads = local // DH
    model = width * REL
    rank = jnp.stack([lax.axis_index("head"), lax.axis_index("seq")]).astype(jnp.int32)
    conv = conv_kernel.reshape(KW, 3 * local)

    kmat, aux = prepare(rank, doc_start.reshape(1, total), memory_decay.T, momentum_decay.T)
    columns = out_weight.reshape(local, REL, width).transpose(1, 0, 2).reshape(-1, width)
    pair = jnp.concatenate([cotangent, columns], 0)
    small = pack(shifted(inputs[total - 8 :], "seq", 1), norm_gain, ffn_gain, ())
    smalls = gather_rel(small)
    blocks = gather_rel(inputs, beside=(kmat, smalls[2]))
    pair_far = swap(hold(pair, blocks[2], smalls[2]), "head", 2)

    (
        x,
        hidden_one,
        proj,
        qkv,
        parts,
        halo,
        gains,
        dev_state,
        load,
    ) = front(
        rank,
        blocks,
        smalls,
        qkv_weight,
        conv,
        aux,
        heads,
    )

    ahead = []

    def attend_head(sent):
        ahead.append(attend(qkv, persistent, aux, len(ahead), heads, (sent,)))
        return ahead[-1][:1]

    def inside_blocks(sent):
        ahead.append(within(qkv, kmat, (sent,)))
        return ahead[-1:]


    prefix = entering(
        rank, load, dev_state, heads, False, [attend_head] * heads + [inside_blocks]
    )
    intra = ahead.pop()
    atts, ratios, probs, fixps = zip(*ahead)
    pair_far = hold(pair_far, prefix)
    pairs = [pair, swap(pair, "head", 1), pair_far, swap(pair_far, "head", 1)]
    merged, normed_mem, mem_scales, state_lows = merge(
        qkv, atts, intra, aux, parts, prefix, heads, ()
    )
    grad_act, cot, trio = recall(rank, pairs, total, down_weight, (merged,))
    merged_rel = gather_rel(merged, beside=(grad_act,))
    hidden_two, normed_two, scale_two, middle_share = middle(
        rank, merged_rel, pairs, x, gains, (grad_act,)
    )
    gate_weights = gate_up.transpose(0, 2, 1)
    trio, send = ffn(hidden_two, grad_act, gate_weights, trio, 0)
    trio, rest = ffn(hidden_two, grad_act, gate_weights, trio, 1)
    places = lax.axis_size("seq")
    bits = tuple(2**i for i in range((places - 1).bit_length()))
    laps = len(bits)
    turned = bits[1:] + bits[:1]

    near = hold(swap(send, "head", 1), rest)
    half = rest[1:2] + near[1:2]
    turned = bits[1:] + bits[:1]
    ffn_levels, ffn_rows = harvest(
        rank, cot, hidden_two, trio, (turned, bits, bits), (half,)
    )
    far_sum = hold(swap(half, "head", 2), ffn_levels[-1][-1])
    (down, gate, up), _ = lax.optimization_barrier((ffn_levels, far_sum))
    low_own, dgain_two = bend(
        rank, rest, near, far_sum, cot, normed_two, scale_two, gains, ()
    )
    ans_send, ans_far, ans_keep = answer(rank, trio, down_weight, (low_own,))
    down = absorb(down, 0, hold(swap(down[0], "seq", turned[0]), ans_keep))
    lows = gather_rel(low_own, beside=(ans_keep, *down[1:]))

    (grad_att, grad_mem, mem_parts, low_share, back_state, back_load), three, by_rows = turn(
        rank,
        lows,
        out_weight,
        qkv,
        normed_mem,
        mem_scales,
        aux,
        merged,
        dev_state,
        bits,
        heads,
    )
    pieces, extra = [], {"three": three, "down": down, "gate": gate, "up": up}

    def later(name, lap, mark):
        extra[name] = list(extra[name])
        extra[name][lap] = hold(extra[name][lap], mark)


    def exchanged(name, lap, mark):
        order = turned if name == "down" else bits
        got = hold(swap(extra[name][lap], "seq", order[lap]), mark)
        extra[name] = absorb(extra[name], lap, got)
        return extra[name][lap + 1 :]

    def attend_back_head(sent):
        h = len(pieces)
        pieces.append(
            attend_back(
                qkv, persistent, probs[h], fixps[h], ratios[h], grad_att, h, heads, (sent,)
            )
        )
        if h == 0:
            return [pieces[-1][3], *exchanged("gate", 0, sent)]
        later("gate", 1, sent)
        later("up", 0, sent)
        extra["ans_near"] = hold(swap(ans_send, "head", 1), sent)
        extra["ans_half"] = ans_far + extra["ans_near"][1]
        return [
            pieces[-1][3],
            extra["ans_half"],
            *exchanged("down", 1, sent),
            *exchanged("three", 0, sent),
        ]

    def back_inside(sent):
        extra["inner"] = within_back(qkv, kmat, grad_mem, (sent,))
        extra["ans_sum"] = swap(extra["ans_half"], "head", 2)
        return [
            extra["inner"],
            extra["ans_sum"],
            *exchanged("three", 1, sent),
        ]

    suffix = entering(
        rank, back_load, back_state, heads, True, [attend_back_head] * heads + [back_inside]
    )
    inner = extra["inner"]
    suffix = hold(suffix, *exchanged("gate", 1, suffix), *exchanged("up", 0, suffix))
    gp, tail, head_rows, gconv, *rooms = settle(
        qkv,
        [pieces[h][c] for c in range(3) for h in range(heads)],
        inner,
        grad_mem,
        aux,
        state_lows,
        mem_parts,
        suffix,
        proj,
        halo,
        conv,
        width,
        heads,
    )
    returned = shifted(head_rows, "seq", -1)
    for lap in range(2, laps):
        exchanged("three", lap, gp)
        exchanged("down", lap, gp)
        exchanged("gate", lap, gp)
    exchanged("up", 1, gp)
    three, down = extra["three"], extra["down"]
    ans_near, ans_sum = extra["ans_near"], extra["ans_sum"]
    *rooms, dgain = back(
        rank, gp, tail, head_rows, qkv_weight, x, gains, dgain_two, rooms, False, (head_rows,)
    )
    returned = hold(returned, three[-1], down[-1], extra["gate"][-1], extra["up"][2], dgain)
    one, two = reap(
        rank,
        hidden_one,
        gp,
        tail,
        returned,
        ((bits, 0, 2 * local), (turned, 2 * local, 3 * local)),
    )
    bsend, bfar, bkeep, dgain = back(
        rank, gp, tail, returned, qkv_weight, x, gains, dgain, rooms, True, (two[-1],)
    )

    def take(x, mark, axis, bit):
        return hold(swap(x, axis, bit), *mark)

    gain_half = dgain + swap(dgain, "head", 1)
    bnear = take(bsend, (gain_half,), "head", 1)
    bhalf = bfar + bnear[1]
    output = (
        middle_share
        + ans_keep.astype(F32)
        + ans_near[0].astype(F32)
        + hold(ans_sum, bhalf).astype(F32)
    ).astype(BF16)
    gain_sums = gain_half + take(gain_half, (output,), "head", 2)
    gain_own = lax.dynamic_slice_in_dim(
        gain_sums, lax.axis_index("head") * width, width, 1
    )
    fixed_count = persistent.shape[1]
    little = jnp.concatenate(
        [
            gain_own[:2],
            gconv[:KW].reshape(3 * KW, local),
            jnp.concatenate([p[3] for p in pieces], -1).reshape(2 * fixed_count, local),
        ],
        0,
    )
    two = absorb(two, 0, take(two[0], (little,), "seq", turned[0]))
    one = absorb(one, 0, take(one[0], (two[1],), "seq", bits[0]))
    mark = (one[1],)
    for lap in range(1, laps):
        little = little + take(little, mark, "seq", bits[lap - 1])
        two = absorb(two, lap, take(two[lap], (little,), "seq", turned[lap]))
        mark = (two[lap + 1],)
        if lap + 1 < laps:
            one = absorb(one, lap, take(one[lap], mark, "seq", bits[lap]))
            mark = (one[lap + 1],)
    for lap in range(2, laps):
        exchanged("up", lap, mark[0])
    flip = (lambda a: a.transpose(0, 2, 1)) if ffn_rows else (lambda a: a)
    grad_down = flip(down[-1][0])[0]
    grad_gate_up = flip(jnp.concatenate([extra["gate"][-1][0], extra["up"][-1][0]], 0))
    grad_gate_up = grad_gate_up.transpose(0, 2, 1)
    mark = (grad_gate_up,)
    input_grad = (
        bkeep.astype(F32)
        + bnear[0].astype(F32)
        + take(bhalf, mark, "head", 2).astype(F32)
        + low_share.astype(F32)
    )
    more = take(little, (input_grad,), "seq", bits[-1])
    got = take(one[-2], (more,), "seq", bits[-1])
    gain_one, gain_two, grad_conv, grad_fixed, grad_qkv = finish(
        little, more, one[-1], got, two[-1], fixed_count
    )
    grad_out = three[-1][0].T if by_rows else three[-1][0]
    return (
        output,
        input_grad,
        gain_one[0],
        grad_qkv,
        grad_conv,
        grad_fixed,
        grad_out,
        gain_two[0],
        grad_gate_up,
        grad_down,
    )


def solution(mesh):
    placed = (
        P("seq", "head"),
        P("seq", "head"),
        P("head"),
        P(None, None, "head"),
        P(None, None, "head"),
        P(None, None, "head"),
        P("head", None),
        P("head"),
        P(None, None, "head"),
        P("head", None),
        P("seq", "head"),
        P("seq", "head"),
        P("seq"),
    )
    return jax.shard_map(
        per_device,
        mesh=mesh,
        in_specs=placed,
        out_specs=(
            P("seq", "head"),
            P("seq", "head"),
            P("head"),
            P(None, "seq", "head"),
            P(None, None, "head"),
            P(None, None, "head"),
            P("head", "seq"),
            P("head"),
            P(None, "seq", "head"),
            P("head", "seq"),
        ),
        check_vma=False,
    )
```
